32 devices in a mesh: dp: 4 (over z), fsdp: 8 (over y, x, core).
Axes of the slice: x: 2, y: 2, z: 4, core: 2. Of those that a mesh axis runs over, the one named last changes fastest.
Arguments:
- tokens: bfloat16 [64, 1024, 512], P(('dp', 'fsdp')), may hold values from -6 to 6
- flat_params: float32 [2699264], P(('dp', 'fsdp')), may hold values from -4 to 4, as said below
- segments: int32 [64, 1024], P(('dp', 'fsdp')), may hold values from 0 to 31, never falling along the last dimension, each value on 1 to 64 neighbouring positions
- experts: int32 [64, 1024, 2], P(('dp', 'fsdp')), may hold values from 0 to 7, all different within a row
- counts: int32 [64], P(('dp', 'fsdp')), may hold values from 512 to 1024, as said below
- cotangent: bfloat16 [64, 1024, 512], P(('dp', 'fsdp')), may hold values from -6 to 6
Outputs:
- output: bfloat16 [64, 1024, 512], P(('dp', 'fsdp'))
- grad_tokens: bfloat16 [64, 1024, 512], P(('dp', 'fsdp'))
- grad_flat: float32 [2699264], P(('dp', 'fsdp'))
The draws below stay inside these ranges and needn't reach their ends.
Inputs may be any that keep to these rules, and one draw needn't show every extreme that they name: `flat_params`: packed parameters in the order of the first step. `counts`: positions from this count on are padding; some row has exactly 1024 real tokens and another exactly 512. For each token slot, its 2 entries along the last dimension name different experts; across the token slots of a packed row the same experts recur freely.
All inputs are finite; a program needn't handle non-finite values.
Results may differ from the reference program's by a relative error of at most 0.0074.
Values may be sent and summed in bfloat16 or wider, within the bound.
No kernel may reach another device: no remote copies, remote signals or barrier semaphores. Data moves between devices by JAX's collectives and lax.ppermute only.
A program may use at most 192 MiB of HBM per device.

```python
import math
import jax
import jax.numpy as jnp
import numpy as np
from jax import lax

D = 512
FF = 2048
EXPERTS = 8
HEAD = 64
TOPK = 2
LEN = 1024
ROWS = 64
PARAMS = 2695680
FLAT = 2699264


def draw_flat_params(key, part):
    key = jax.random.fold_in(key, 11)
    first_key, second_key = jax.random.split(key)
    base_draw = jnp.clip(jax.random.normal(first_key, (FLAT,), jnp.float32), -4.0, 4.0)
    even_draw = jax.random.uniform(second_key, (FLAT,), jnp.float32, -1.0, 1.0)
    layout = [(D * EXPERTS * HEAD, D ** (-0.5), 0.0), (D * HEAD, D ** (-0.5), 0.0), (D * HEAD, D ** (-0.5), 0.0), (EXPERTS * HEAD * D, 1.6 * HEAD ** (-0.5), 0.0), (D * FF, D ** (-0.5), 0.0), (FF * D, 1.5 * FF ** (-0.5), 0.0), (D * EXPERTS, 0.7 * D ** (-0.5), 0.0), (FF, 0.3, 0.0), (D, 0.0, 1.0), (D, 0.2, 0.0), (D, 0.0, 1.0), (D, 0.2, 0.0), (D, 0.3, 0.0), (FLAT - PARAMS, 1.0, 0.0)]
    scales = jnp.concatenate([jnp.full((entry[0],), entry[1], jnp.float32) for entry in layout])
    gains = jnp.concatenate([jnp.full((entry[0],), entry[2], jnp.float32) for entry in layout])
    return scales * base_draw + gains * (1.0 + 0.3 * even_draw)


def draw_counts(key, part):
    key = jax.random.fold_in(key, 12)
    first_key, second_key, third_key = jax.random.split(key, 3)
    drawn = jax.random.randint(first_key, (ROWS,), LEN // 2, LEN + 1)
    full_row = jax.random.randint(second_key, (), 0, ROWS)
    half_row = (full_row + 1 + jax.random.randint(third_key, (), 0, ROWS - 1)) % ROWS
    places = jnp.arange(ROWS, dtype=jnp.int32)
    drawn = jnp.where(places == full_row, LEN, drawn)
    return jnp.where(places == half_row, LEN // 2, drawn).astype(jnp.int32)


def shard_levels(stream_key, shape, cuts, smallest, largest):
    loudness = 1.0
    for axis_at, blocks in cuts:
        heights = jax.random.uniform(jax.random.fold_in(jax.random.fold_in(stream_key, 6), axis_at), (blocks,), jnp.float32, smallest / len(cuts), largest / len(cuts))
        loudness = loudness * jnp.repeat(jnp.exp(heights), shape[axis_at] // blocks).reshape((-1,) + (1,) * (len(shape) - 1 - axis_at))
    return loudness


def different_ones(rng, rows, number_of, top, lift):
    ranking = jax.random.permutation(jax.random.fold_in(rng, 1), number_of)
    favour = ranking
    for power in range(3):
        favour = favour * favour // number_of
    favour = favour * lift // number_of
    chance = jax.random.randint(jax.random.fold_in(rng, 2), (rows, number_of), 0, 4096) + favour
    sure = jax.random.permutation(jax.random.fold_in(rng, 3), rows)[jnp.arange(number_of) % rows]
    chance = jnp.where(jnp.arange(rows)[:, None] == sure[None, :], 1 << 14, chance)
    merit = chance * number_of + jnp.arange(number_of)
    return lax.top_k(merit.astype(jnp.int32), top)[1].astype(jnp.int32)


def profile(count, total, reach, skew):
    portions = [(1 << 20) // math.isqrt(grade ** skew) + 1 for grade in range(2, count + 1)]
    surplus, given = total - reach - (count - 1), [1] * (count - 1)
    while surplus > 0:
        movable = [i for i in range(count - 1) if given[i] < reach]
        pool, remaining = sum([portions[i] for i in movable]), surplus
        for i in movable:
            extra = min(reach - given[i], max(1, remaining * portions[i] // pool), surplus)
            given[i] = given[i] + extra
            surplus = surplus - extra
    return np.array([reach] + given)


def uneven(key, count, total, most, skew):
    if count == 2:
        one = jax.random.randint(key, (), max(1, total - most), min(most, total - 1) + 1)
        return jnp.stack([one, total - one])
    lengths = jnp.asarray(profile(count, total, most, skew), jnp.int32)
    twos = (count - 1) // 2
    source_of, sink = lengths[1:1 + 2 * twos:2], lengths[2:2 + 2 * twos:2]
    slack = jnp.minimum(source_of - 1, most - sink)
    passed = jax.random.randint(jax.random.fold_in(key, 1), (twos,), 0, 1 << 20) % (slack + 1)
    lengths = lengths.at[1:1 + 2 * twos:2].set(source_of - passed).at[2:2 + 2 * twos:2].set(sink + passed)
    return lengths[jax.random.permutation(jax.random.fold_in(key, 2), count)]


def gaussian(rng, shape, scale, reach, cuts=(), kind=jnp.bfloat16):
    values = scale * jax.random.normal(rng, shape, jnp.float32)
    if cuts:
        values = values * shard_levels(rng, shape, cuts, -0.22, 0.18)
    return jnp.clip(values, -reach, reach).astype(kind)


def setup_inputs(seed: int = 0) -> dict:
    key_list = jax.random.split(jax.random.key(seed), 7)
    tokens = gaussian(key_list[0], (ROWS, LEN, D), 1.0, 6.0, ((0, 32),))
    flat_params = draw_flat_params(jax.random.fold_in(key_list[6], 71), 0)
    segments = jax.vmap(lambda own: jnp.searchsorted(jnp.cumsum(uneven(own, LEN // 32, LEN, 64, 1)), jnp.arange(LEN), side="right"))(jax.random.split(key_list[2], ROWS)).reshape((ROWS, LEN)).astype(jnp.int32)
    experts = different_ones(key_list[3], ROWS * LEN, EXPERTS, TOPK, 0).reshape((ROWS, LEN, TOPK))
    counts = draw_counts(jax.random.fold_in(key_list[6], 71), 0)
    cotangent = gaussian(key_list[5], (ROWS, LEN, D), 1.0, 6.0, ((0, 32),))
    return {"tokens": tokens, "flat_params": flat_params, "segments": segments, "experts": experts, "counts": counts, "cotangent": cotangent}


EPS = 1e-05
NEG = -1e+30
HIGHEST = lax.Precision.HIGHEST

@jax.custom_vjp
def low(v):
    return lax.optimization_barrier(v.astype(jnp.bfloat16)).astype(jnp.float32)

@jax.custom_vjp
def low_back(v):
    return v

def low_keep(v):
    return (low(v), None)

def low_pass(kept, grad):
    return (grad,)

def back_keep(v):
    return (v, None)

def back_low(kept, grad):
    return (low(grad),)
low.defvjp(low_keep, low_pass)
low_back.defvjp(back_keep, back_low)

def split_params(flat):
    shapes = [(D, EXPERTS * HEAD), (D, HEAD), (D, HEAD), (EXPERTS * HEAD, D), (D, FF), (FF, D), (D, EXPERTS), (FF,), (D,), (D,), (D,), (D,), (D,)]
    pieces = []
    offset = 0
    for target in shapes:
        amount = math.prod(target)
        pieces.append(flat[offset:offset + amount].reshape(target))
        offset = offset + amount
    return pieces

def matmul(left, right):
    return jnp.dot(left, right, precision=HIGHEST)

def layer_norm(source, gain, shift):
    center = source - lax.optimization_barrier(jnp.mean(source, axis=-1, keepdims=True))
    spread = lax.optimization_barrier(jnp.mean(center * center, axis=-1, keepdims=True))
    return center * lax.rsqrt(spread + EPS) * gain + shift

def layer_row(source, segment_row, expert_row, real_count, weights):
    w_query, w_key, w_value, w_out, w_up, w_down, w_router, bias_up, gain_one, shift_one, gain_two, shift_two, bias_down = weights
    length = source.shape[0]
    places = jnp.arange(length, dtype=jnp.int32)
    validity = places < real_count
    normed = low(layer_norm(source, gain_one, shift_one))
    logits = low_back(matmul(normed, w_router))
    shifted = jnp.exp(logits - lax.optimization_barrier(jnp.max(logits, axis=-1, keepdims=True)))
    router_prob = shifted / lax.optimization_barrier(jnp.sum(shifted, axis=-1, keepdims=True))
    expert_ids = jnp.arange(EXPERTS, dtype=jnp.int32)[None, :]
    chosen = (expert_row[:, 0:1] == expert_ids) | (expert_row[:, 1:2] == expert_ids)
    gating = router_prob * chosen.astype(jnp.float32)
    queries = low_back(low(matmul(normed, w_query))).reshape(length, EXPERTS, HEAD)
    key_rows = low_back(low(matmul(normed, w_key)))
    value_rows = low_back(low(matmul(normed, w_value)))
    block_rows = min(512, length)
    factor = HEAD ** (-0.5)
    outputs = []
    for first_row in range(0, length, block_rows):
        last_row = first_row + block_rows
        scores = jnp.einsum('qeh,kh->eqk', queries[first_row:last_row], key_rows, precision=HIGHEST) * factor
        scores = low_back(scores)
        allowed = (segment_row[first_row:last_row, None] == segment_row[None, :]) & validity[first_row:last_row, None] & validity[None, :]
        allowed = allowed | (places[first_row:last_row, None] == places[None, :])
        scores = jnp.where(allowed[None], scores, NEG)
        expd = jnp.exp(scores - lax.optimization_barrier(jnp.max(scores, axis=-1, keepdims=True)))
        weights_soft = expd / lax.optimization_barrier(jnp.sum(expd, axis=-1, keepdims=True))
        outputs.append(jnp.einsum('eqk,kh->qeh', low(weights_soft), value_rows, precision=HIGHEST))
    attended = low_back(jnp.concatenate(outputs, axis=0))
    mixed_heads = low((gating[:, :, None] * attended).reshape(length, EXPERTS * HEAD))
    branch = low_back(matmul(mixed_heads, w_out))
    middle = source + branch
    normed_two = low(layer_norm(middle, gain_two, shift_two))
    hidden_pre = low_back(matmul(normed_two, w_up) + bias_up)
    hidden = low(jax.nn.gelu(hidden_pre, approximate=True))
    result = low_back(matmul(hidden, w_down) + bias_down)
    return validity[:, None].astype(jnp.float32) * (middle + result)

def reference(tokens, flat_params, segments, experts, counts, cotangent):
    tokens_wide = tokens.astype(jnp.float32)
    cot_wide = cotangent.astype(jnp.float32)

    def forward(source, flat):
        weights = split_params(low(flat))

        def one_row(unused, inputs_row):
            return (unused, layer_row(inputs_row[0], inputs_row[1], inputs_row[2], inputs_row[3], weights))
        unused, result = lax.scan(jax.checkpoint(one_row), jnp.zeros((), jnp.float32), (source, segments, experts, counts))
        return result
    result, pullback = jax.vjp(forward, tokens_wide, flat_params)
    grad_input, grad_params = pullback(cot_wide)
    return (result.astype(jnp.bfloat16), grad_input.astype(jnp.bfloat16), grad_params)
```

```python
from functools import partial

import jax
import jax.numpy as jnp
from jax import lax
from jax.experimental import pallas as pl
from jax.experimental.pallas import tpu as pltpu
from jax.sharding import PartitionSpec as P

D = 512
FF = 2048
EXPERTS = 8
HEAD = 64
EPS = 1e-05
NEG = -1e30
F32 = jnp.float32
BF16 = jnp.bfloat16
AXES = ("dp", "fsdp")

ROW_K = 512
ROW_V = 576
ROW_O = 640
ROW_U = 1152
ROW_D = 3200
ROW_S = 5248
SMALL = 32
ROWS_ALL = ROW_S + SMALL
T_R = 512
T_K = 528
T_V = 592
T_ALL = 656

QB = 128
KB = 256

NN = ((1,), (0,))
NT = ((1,), (1,))
TN = ((0,), (0,))

VMEM_MIB = 56


def dot(left, right, dims):
    return lax.dot_general(left, right, (dims, ((), ())), preferred_element_type=F32)


def cost(micros):
    return pl.CostEstimate(flops=int(micros * 1.1e9), bytes_accessed=int(micros * 1e5), transcendentals=0)


def after(value, *others):
    return lax.optimization_barrier((value, *others))[0]


def params(mib=VMEM_MIB):
    return pltpu.CompilerParams(vmem_limit_bytes=mib << 20)


def iota(shape, dim):
    return lax.broadcasted_iota(jnp.int32, shape, dim)


class Plan:
    def __init__(self, devices, shard):
        self.devices = devices
        self.lanes = shard // 128
        reach = max((self.lanes * d) % 64 for d in range(devices)) + self.lanes
        self.rows = -(-reach // 64) * 16

    def first(self, d):
        return (self.lanes * d) // 64

    def last(self, d):
        return (self.lanes * (d + 1) - 1) // 64


def window_kernel(plan, at_ref, shard_ref, out_ref, pad_ref):
    pad_ref[...] = jnp.zeros_like(pad_ref)
    pad_ref[64 : 64 + plan.lanes, :] = shard_ref[...]
    start = 64 - at_ref[0]
    for j in range(4):
        out_ref[:, 128 * j : 128 * (j + 1)] = pad_ref[
            pl.ds(start + j, plan.rows, stride=4), :
        ].astype(BF16)


def make_window(plan, at, shard):
    return pl.pallas_call(
        partial(window_kernel, plan),
        grid_spec=pltpu.PrefetchScalarGridSpec(
            num_scalar_prefetch=1,
            grid=(1,),
            in_specs=[pl.BlockSpec((plan.lanes, 128), lambda i, at: (0, 0))],
            out_specs=pl.BlockSpec((plan.rows, D), lambda i, at: (0, 0)),
            scratch_shapes=[pltpu.VMEM((plan.rows * 4 + 128, 128), F32)],
        ),
        out_shape=jax.ShapeDtypeStruct((plan.rows, D), BF16),
        compiler_params=params(),
    )(at, shard.reshape(plan.lanes, 128))


def row_pieces(plan, low, high):
    direct, shared = [], []
    for d in range(plan.devices):
        first, last = plan.first(d), plan.last(d)
        start = first
        if d > 0 and plan.last(d - 1) == first:
            start = first + 1
            if low <= first * 16 < high:
                shared.append((d, 0, first * 16 - low))
        begin, end = max(start * 16, low), min((last + 1) * 16, high)
        if begin < end:
            direct.append((d, begin - first * 16, begin - low, end - begin))
    return direct, shared


def start_rows(plan, source, low, high, dst_ref, tmp_ref, sem):
    direct, shared = row_pieces(plan, low, high)
    for d, at, to, amount in direct:
        pltpu.make_async_copy(
            source(d).at[pl.ds(at, amount), :], dst_ref.at[pl.ds(to, amount), :], sem.at[0]
        ).start()
    for slot, (d, at, _) in enumerate(shared):
        pltpu.make_async_copy(
            source(d).at[pl.ds(at, 16), :], tmp_ref.at[pl.ds(16 * slot, 16), :], sem.at[1]
        ).start()


def end_rows(plan, low, high, dst_ref, tmp_ref, sem):
    _, shared = row_pieces(plan, low, high)
    pltpu.make_async_copy(dst_ref, dst_ref, sem.at[0]).wait()
    if shared:
        part = tmp_ref.at[pl.ds(0, 16 * len(shared)), :]
        pltpu.make_async_copy(part, part, sem.at[1]).wait()
        for slot, (_, _, to) in enumerate(shared):
            dst_ref[to : to + 16, :] = (
                dst_ref[to : to + 16, :].astype(F32)
                + tmp_ref[16 * slot : 16 * slot + 16, :].astype(F32)
            ).astype(BF16)


def shared_rows(plan, low, high):
    return max(16, 16 * len(row_pieces(plan, low, high)[1]))


class Gathered:
    def __init__(self, plan, lanes, head, rest, whole):
        self.plan, self.lanes = plan, lanes
        self.head, self.rest, self.whole = head, rest, whole
        self.small_at = ROW_S - 16 * plan.first(plan.devices - 1)

    def arrays(self, need_head, need_rest):
        if self.whole is not None:
            return [self.whole]
        return (self.head if need_head else []) + (self.rest if need_rest else [])

    def fetch(self, place_ref, refs, need_head, start):
        if self.whole is not None:
            last = self.plan.devices - 1
            start(lambda d: refs[0].at[d], refs[0].at[last, pl.ds(self.small_at, SMALL), :])
            return
        head = refs[: self.lanes] if need_head else None
        rest = refs[self.lanes :] if need_head else refs
        for place in range(self.lanes):

            def source(d, place=place):
                plane, lane = divmod(d, self.lanes)
                if plane == 0:
                    return head[lane ^ place]
                return rest[lane ^ place].at[plane - 1]

            small = None
            if need_head:
                small = head[(self.lanes - 1) ^ place].at[pl.ds(self.plan.rows, SMALL), :]
            pl.when(place_ref[0] == place)(partial(start, source, small))


def spread(j):
    return (iota((64, D), 1) == 8 * iota((64, D), 0) + j).astype(BF16)


def narrow_transposed(flat):
    out = jnp.zeros((64, D), F32)
    for j in range(8):
        out = out + dot(flat[:, 64 * j : 64 * (j + 1)], spread(j), TN)
    return out


def narrow_flat(turned):
    return jnp.concatenate([dot(spread(j), turned, NT) for j in range(8)], axis=1)


def router_transposed(flat):
    lane = iota((8, D), 1) % 8
    at = iota((8, D), 0)
    pick = (iota((D, 64), 0) // 8 == iota((D, 64), 1)).astype(BF16)
    pieces = []
    for r in range(8):
        row = jnp.broadcast_to(flat[r : r + 1, :], (8, D))
        pieces.append(dot(jnp.where(lane == at, row, 0.0).astype(BF16), pick, NN))
    return jnp.concatenate(pieces, axis=1)


def router_flat(turned):
    lane = iota((8, D), 1) % 8
    at = iota((8, D), 0)
    pick = (iota((64, D), 1) // 8 == iota((64, D), 0)).astype(BF16)
    rows = []
    for r in range(8):
        full = dot(turned[:, 64 * r : 64 * (r + 1)].astype(BF16), pick, NN)
        rows.append(jnp.sum(jnp.where(lane == at, full, 0.0), axis=0, keepdims=True))
    return jnp.concatenate(rows, axis=0)


def norm(source):
    center = source - jnp.mean(source, axis=-1, keepdims=True)
    scaler = lax.rsqrt(jnp.mean(center * center, axis=-1, keepdims=True) + EPS)
    return center * scaler, scaler


def norm_back(grad_normal, normal, scaler):
    return scaler * (
        grad_normal
        - jnp.mean(grad_normal, axis=-1, keepdims=True)
        - normal * jnp.mean(grad_normal * normal, axis=-1, keepdims=True)
    )


def two_heads(ref, pair, q0):
    return jnp.concatenate(
        [
            ref[0, 128 * pair : 128 * pair + 64, pl.ds(q0, QB)],
            ref[0, 128 * pair + 64 : 128 * pair + 128, pl.ds(q0, QB)],
        ],
        axis=1,
    )


def block_bias(code_ref, column_ref, q0, w0):
    row = code_ref[0, :, pl.ds(q0, QB)]
    bias = jnp.where(column_ref[pl.ds(w0, KB), :] == row, 0.0, NEG)
    return jnp.concatenate([bias, bias], axis=1)


def set_columns(code_ref, column_ref):
    length = code_ref.shape[2]
    column_ref[...] = jnp.broadcast_to(code_ref[0], (QB, length)).T


def block_places(block, length):
    q0 = pl.multiple_of(block * QB, QB)
    w0 = pl.multiple_of(jnp.clip(q0 - 64, 0, length - KB), 64)
    return q0, w0


def forward_prepare(plan, gathered, place_ref, refs, turned_ref, small_ref, scratch):
    rows_ref, low_ref, tmp_ref, sem = scratch

    def start(source, small):
        start_rows(plan, source, 0, ROW_O, rows_ref, tmp_ref, sem)
        pltpu.make_async_copy(small, low_ref, sem.at[2]).start()

    gathered.fetch(place_ref, refs, True, start)
    pltpu.make_async_copy(low_ref, low_ref, sem.at[2]).wait()
    end_rows(plan, 0, ROW_O, rows_ref, tmp_ref, sem)
    small_ref[...] = low_ref[...].astype(F32)
    turned_ref[0:D, :] = rows_ref[0:D, :].astype(F32).T.astype(BF16)
    turned_ref[T_R:T_K, :] = jnp.concatenate(
        [router_transposed(small_ref[0:8, :]), jnp.zeros((8, D), F32)], axis=0
    ).astype(BF16)
    turned_ref[T_K:T_V, :] = narrow_transposed(rows_ref[ROW_K:ROW_V, :]).astype(BF16)
    turned_ref[T_V:T_ALL, :] = narrow_transposed(rows_ref[ROW_V:ROW_O, :]).astype(BF16)


def forward_row(x_ref, code_ref, turned_ref, small_ref, outs, column_ref):
    q_ref, k_ref, v_ref, h_ref, prob_ref, lse_ref, att_ref = outs
    length = x_ref.shape[1]
    set_columns(code_ref, column_ref)
    normal, _ = norm(x_ref[0].astype(F32))
    h = (normal * small_ref[12:13, :] + small_ref[13:14, :]).astype(BF16)
    h_ref[0] = h
    turned = dot(turned_ref[0:T_K, :], h, NT)
    q_ref[0] = turned[0:D].astype(BF16)
    logits = turned[T_R : T_R + 8]
    shifted = jnp.exp(logits - jnp.max(logits, axis=0, keepdims=True))
    prob_ref[0] = shifted / jnp.sum(shifted, axis=0, keepdims=True)
    kv = dot(h, turned_ref[T_K:T_ALL, :], NT).astype(BF16)
    k_ref[0] = kv[:, 0:HEAD]
    v_ref[0] = kv[:, HEAD:]

    def block_step(block, carry):
        q0, w0 = block_places(block, length)
        bias = block_bias(code_ref, column_ref, q0, w0)
        keys = k_ref[0, pl.ds(w0, KB), :]
        values = v_ref[0, pl.ds(w0, KB), :]
        for pair in range(EXPERTS // 2):
            scores = dot(keys, two_heads(q_ref, pair, q0), NN) * (HEAD**-0.5) + bias
            peak = jnp.max(scores, axis=0, keepdims=True)
            expd = jnp.exp(scores - peak)
            summed = jnp.sum(expd, axis=0, keepdims=True)
            att = dot(values, expd.astype(BF16), TN) * (1.0 / summed)
            total = peak + jnp.log(summed)
            for half in range(2):
                head = 2 * pair + half
                att_ref[0, 64 * head : 64 * (head + 1), pl.ds(q0, QB)] = att[
                    :, QB * half : QB * (half + 1)
                ]
                lse_ref[0, head : head + 1, pl.ds(q0, QB)] = total[:, QB * half : QB * (half + 1)]
        return carry

    lax.fori_loop(0, length // QB, block_step, 0)


def forward_first(plan, gathered, count, place_ref, x_ref, code_ref, *refs):
    wins, refs = refs[:count], refs[count:]
    outs, (turned_ref, small_ref), scratch = refs[:7], refs[7:9], refs[9:]
    forward_prepare(plan, gathered, place_ref, wins, turned_ref, small_ref, scratch[1:])
    forward_row(x_ref, code_ref, turned_ref, small_ref, outs, scratch[0])


def forward_next(place_ref, x_ref, code_ref, turned_ref, small_ref, *refs):
    forward_row(x_ref, code_ref, turned_ref, small_ref, refs[7:14], refs[14])


def attention_forward(plan, gathered, place, x, code, row, before):
    rows, length = x.shape[0], x.shape[1]
    row3 = lambda a, b: pl.BlockSpec((1, a, b), lambda *_: (row, 0, 0))
    sizes = [
        (D, length, BF16),
        (length, HEAD, BF16),
        (length, HEAD, BF16),
        (length, D, BF16),
        (8, length, F32),
        (8, length, F32),
        (D, length, F32),
    ]
    out_specs = [row3(a, b) for a, b, _ in sizes]
    out_shape = [kind(c, rows, a, b) for a, b, c in sizes]
    scratch = [pltpu.VMEM((length, QB), F32)]
    in_specs = [row3(length, D), row3(1, length)]
    if before is None:
        wins = gathered.arrays(True, False)
        kernel = partial(forward_first, plan, gathered, len(wins))
        operands = [place, x, code, *wins]
        in_specs = in_specs + [ANYWHERE] * len(wins)
        out_specs = out_specs + [whole(T_ALL, D), whole(SMALL, D)]
        out_shape = out_shape + [kind(BF16, T_ALL, D), kind(F32, SMALL, D)]
        scratch = scratch + [
            pltpu.VMEM((ROW_O, D), BF16),
            pltpu.VMEM((SMALL, D), BF16),
            pltpu.VMEM((shared_rows(plan, 0, ROW_O), D), BF16),
            pltpu.SemaphoreType.DMA((3,)),
        ]
        aliases = {}
    else:
        kernel = forward_next
        operands = [place, x, code, *before[7:9], *before[:7]]
        in_specs = in_specs + [whole(T_ALL, D), whole(SMALL, D)] + [ANYWHERE] * 7
        aliases = {5 + i: i for i in range(7)}
    return pl.pallas_call(
        kernel,
        grid_spec=pltpu.PrefetchScalarGridSpec(
            num_scalar_prefetch=1,
            grid=(1,),
            in_specs=in_specs,
            out_specs=out_specs,
            scratch_shapes=scratch,
        ),
        out_shape=out_shape,
        input_output_aliases=aliases,
        cost_estimate=cost(14),
        compiler_params=params(),
    )(*operands)


TB = 512


def chosen_experts(experts_ref, length):
    ids = iota((EXPERTS, length), 0)
    chosen = (experts_ref[0, 0:1, :] == ids) | (experts_ref[0, 1:2, :] == ids)
    return chosen.astype(F32)


def valid_tokens(counts_ref, amount):
    place = pl.program_id(1) * amount + iota((amount, 1), 0)
    return (place < counts_ref[pl.program_id(0)]).astype(F32)


def by_head(values, gate):
    return jnp.concatenate(
        [values[64 * e : 64 * (e + 1)] * gate[e : e + 1] for e in range(EXPERTS)], axis=0
    )


def gelu_parts(source):
    scale = (2.0 / jnp.pi) ** 0.5
    square = source * source
    bent = jnp.tanh(source * (scale + (scale * 0.044715) * square))
    half = 0.5 * source
    value = half + half * bent
    slope = (0.5 + 0.5 * bent) + (half - half * bent * bent) * (
        scale + (3.0 * scale * 0.044715) * square
    )
    return value, slope


def first_step():
    return (pl.program_id(0) == 0) & (pl.program_id(1) == 0)


def last_step():
    return (pl.program_id(0) == pl.num_programs(0) - 1) & (
        pl.program_id(1) == pl.num_programs(1) - 1
    )


def up_kernel(plan, gathered, count, place_ref, counts_ref, *refs):
    x_ref, cot_ref, att_ref, prob_ref, experts_ref, small_ref = refs[:6]
    wins = refs[6 : 6 + count]
    hid_ref, slope_ref, mid_ref, up_ref, out_ref, gdown_ref = refs[6 + count : 12 + count]
    rows_ref, tmp_ref, wide_ref, total_ref, sem = refs[12 + count :]

    @pl.when(first_step())
    def _():
        def start(source, small):
            start_rows(plan, source, ROW_O, ROW_D, rows_ref, tmp_ref, sem)

        gathered.fetch(place_ref, wins, True, start)
        end_rows(plan, ROW_O, ROW_D, rows_ref, tmp_ref, sem)
        for c in range(4):
            lanes = slice(128 * c, 128 * (c + 1))
            wide_ref[c] = rows_ref[D:, lanes].astype(F32)
            for j in range(4):
                up_ref[:, D * j + 128 * c : D * j + 128 * (c + 1)] = wide_ref[
                    c, pl.ds(j, D, stride=4), :
                ].astype(BF16)
        out_ref[...] = rows_ref[0:D, :]
        total_ref[...] = jnp.zeros_like(total_ref)

    amount = x_ref.shape[1]
    gate = prob_ref[0] * chosen_experts(experts_ref, amount)
    mixed = by_head(att_ref[0], gate).astype(BF16)
    middle = x_ref[0].astype(F32) + dot(mixed, rows_ref[0:D, :], TN)
    mid_ref[0] = middle
    normal, _ = norm(middle)
    h = (normal * small_ref[14:15, :] + small_ref[15:16, :]).astype(BF16)
    grad_low = (valid_tokens(counts_ref, amount) * cot_ref[0].astype(F32)).astype(BF16)
    for j in range(4):
        part = slice(D * j, D * (j + 1))
        value, slope = gelu_parts(dot(h, up_ref[:, part], NN) + small_ref[8 + j : 9 + j, :])
        value = value.astype(BF16)
        hid_ref[0, :, part] = value
        slope_ref[0, :, part] = slope.astype(BF16)
        total_ref[part, :] += dot(value, grad_low, TN)

    @pl.when(last_step())
    def _():
        gdown_ref[...] = total_ref[...].astype(BF16)


def row_block(*tail):
    return pl.BlockSpec((1, TB, *tail), lambda i, j, *_: (i, j, 0))


def column_block(height):
    return pl.BlockSpec((1, height, TB), lambda i, j, *_: (i, 0, j))


def whole(*shape):
    return pl.BlockSpec(shape, lambda *_: (0,) * len(shape))


ANYWHERE = pl.BlockSpec(memory_space=pl.ANY)


def kind(dtype, *shape):
    return jax.ShapeDtypeStruct(shape, dtype)


def feed_up(plan, gathered, place, counts, x, cot, att, prob, experts, small):
    rows, length = x.shape[0], x.shape[1]
    wins = gathered.arrays(True, True)
    return pl.pallas_call(
        partial(up_kernel, plan, gathered, len(wins)),
        grid_spec=pltpu.PrefetchScalarGridSpec(
            num_scalar_prefetch=2,
            grid=(rows, length // TB),
            in_specs=[
                row_block(D),
                row_block(D),
                column_block(D),
                column_block(8),
                column_block(2),
                whole(SMALL, D),
            ]
            + [ANYWHERE] * len(wins),
            out_specs=[
                row_block(FF),
                row_block(FF),
                row_block(D),
                whole(D, FF),
                whole(D, D),
                whole(FF, D),
            ],
            scratch_shapes=[
                pltpu.VMEM((ROW_D - ROW_O, D), BF16),
                pltpu.VMEM((shared_rows(plan, ROW_O, ROW_D), D), BF16),
                pltpu.VMEM((4, FF, 128), F32),
                pltpu.VMEM((FF, D), F32),
                pltpu.SemaphoreType.DMA((2,)),
            ],
        ),
        out_shape=[
            kind(BF16, rows, length, FF),
            kind(BF16, rows, length, FF),
            kind(F32, rows, length, D),
            kind(BF16, D, FF),
            kind(BF16, D, D),
            kind(BF16, FF, D),
        ],
        cost_estimate=cost(30),
        compiler_params=params(),
    )(place, counts, x, cot, att, prob, experts, small, *wins)


def hidden_kernel(plan, gathered, count, pieces, place_ref, counts_ref, *refs):
    cot_ref, slope_ref, mid_ref, small_ref, gdown_ref = refs[:5]
    wins = refs[5 : 5 + count]
    pre_ref, down_ref, gbias_ref, gup_ref = refs[5 + count : 9 + count]
    packed = refs[9 + count : -6]
    flat_ref, tmp_ref, wide_ref, total_ref, sem, pack_sem = refs[-6:]

    @pl.when(first_step())
    def _():
        def start(source, small):
            start_rows(plan, source, ROW_D, ROW_S, down_ref, tmp_ref, sem)

        gathered.fetch(place_ref, wins, False, start)
        if pieces:
            pack_start(pieces, [1], place_ref, [flat_ref, gdown_ref], packed, pack_sem)
        end_rows(plan, ROW_D, ROW_S, down_ref, tmp_ref, sem)
        total_ref[...] = jnp.zeros_like(total_ref)
        gbias_ref[...] = jnp.zeros_like(gbias_ref)

    amount = cot_ref.shape[1]
    grad = valid_tokens(counts_ref, amount) * cot_ref[0].astype(F32)
    grad_low = grad.astype(BF16)
    normal, _ = norm(mid_ref[0])
    h = (normal * small_ref[14:15, :] + small_ref[15:16, :]).astype(BF16)
    for j in range(4):
        part = slice(D * j, D * (j + 1))
        pre = slope_ref[0, :, part].astype(F32) * dot(grad_low, down_ref[part, :], NT)
        gbias_ref[j : j + 1, :] += jnp.sum(pre, axis=0, keepdims=True)
        pre = pre.astype(BF16)
        pre_ref[0, :, part] = pre
        total_ref[:, part] += dot(h, pre, TN)
    gbias_ref[4:5, :] += jnp.sum(grad, axis=0, keepdims=True)

    @pl.when(last_step())
    def _():
        for c in range(4):
            for j in range(4):
                wide_ref[c, pl.ds(j, D, stride=4), :] = total_ref[
                    :, D * j + 128 * c : D * j + 128 * (c + 1)
                ]
            flat_ref[:, 128 * c : 128 * (c + 1)] = wide_ref[c].astype(BF16)
        gup_ref[...] = flat_ref[0 : gup_ref.shape[0], :]
        if pieces:
            pack_start(pieces, [0], place_ref, [flat_ref, gdown_ref], packed, pack_sem)
            pack_end(packed, pack_sem)


def feed_hidden(plan, gathered, place, counts, cot, slope, mid, small, gdown, pieces):
    rows, length = cot.shape[0], cot.shape[1]
    wins = gathered.arrays(False, True)
    head = LATE_ROWS if pieces else FF
    packed = [kind(BF16, LANES // 2, PLANES - 1, plan.rows, D)] * 2 if pieces else []
    return pl.pallas_call(
        partial(hidden_kernel, plan, gathered, len(wins), pieces),
        grid_spec=pltpu.PrefetchScalarGridSpec(
            num_scalar_prefetch=2,
            grid=(rows, length // TB),
            in_specs=[row_block(D), row_block(FF), row_block(D), whole(SMALL, D), whole(FF, D)]
            + [ANYWHERE] * len(wins),
            out_specs=[row_block(FF), whole(FF, D), whole(8, D), whole(head, D)]
            + [ANYWHERE] * len(packed),
            scratch_shapes=[
                pltpu.VMEM((FF, D), BF16),
                pltpu.VMEM((shared_rows(plan, ROW_D, ROW_S), D), BF16),
                pltpu.VMEM((4, FF, 128), F32),
                pltpu.VMEM((D, FF), F32),
                pltpu.SemaphoreType.DMA((2,)),
                pltpu.SemaphoreType.DMA((2,)),
            ],
        ),
        out_shape=[
            kind(BF16, rows, length, FF),
            kind(BF16, FF, D),
            kind(F32, 8, D),
            kind(BF16, head, D),
        ]
        + packed,
        cost_estimate=cost(20),
        compiler_params=params(),
    )(place, counts, cot, slope, mid, small, gdown, *wins)


def branch_kernel(
    counts_ref,
    cot_ref,
    pre_ref,
    mid_ref,
    att_ref,
    prob_ref,
    experts_ref,
    small_ref,
    up_ref,
    out_ref,
    dmid_ref,
    datt_ref,
    dlog_ref,
    gout_ref,
    gnorm_ref,
    total_ref,
):
    @pl.when(first_step())
    def _():
        total_ref[...] = jnp.zeros_like(total_ref)
        gnorm_ref[...] = jnp.zeros_like(gnorm_ref)

    amount = cot_ref.shape[1]
    grad = valid_tokens(counts_ref, amount) * cot_ref[0].astype(F32)
    normal, scaler = norm(mid_ref[0])
    back = dot(pre_ref[0], up_ref[...], NT)
    gnorm_ref[0:1, :] += jnp.sum(back * normal, axis=0, keepdims=True)
    gnorm_ref[1:2, :] += jnp.sum(back, axis=0, keepdims=True)
    dmid = grad + norm_back(back * small_ref[14:15, :], normal, scaler)
    dmid_ref[0] = dmid
    branch = dmid.astype(BF16)
    prob = prob_ref[0]
    chosen = chosen_experts(experts_ref, amount)
    gate = prob * chosen
    att = att_ref[0]
    total_ref[...] += dot(by_head(att, gate).astype(BF16), branch, NN)
    dmixed = dot(out_ref[...], branch, NT)
    dgate = jnp.concatenate(
        [
            jnp.sum(
                dmixed[64 * e : 64 * (e + 1)] * att[64 * e : 64 * (e + 1)], axis=0, keepdims=True
            )
            for e in range(EXPERTS)
        ],
        axis=0,
    )
    datt_ref[0] = by_head(dmixed, gate).astype(BF16)
    dprob = dgate * chosen
    dlog = prob * (dprob - jnp.sum(prob * dprob, axis=0, keepdims=True))
    dlog_ref[0] = jnp.concatenate([dlog, jnp.zeros_like(dlog)], axis=0).astype(BF16)

    @pl.when(last_step())
    def _():
        gout_ref[...] = total_ref[...].astype(BF16)


def feed_branch(counts, cot, pre, mid, att, prob, experts, small, up, out):
    rows, length = cot.shape[0], cot.shape[1]
    return pl.pallas_call(
        branch_kernel,
        grid_spec=pltpu.PrefetchScalarGridSpec(
            num_scalar_prefetch=1,
            grid=(rows, length // TB),
            in_specs=[
                row_block(D),
                row_block(FF),
                row_block(D),
                column_block(D),
                column_block(8),
                column_block(2),
                whole(SMALL, D),
                whole(D, FF),
                whole(D, D),
            ],
            out_specs=[
                row_block(D),
                column_block(D),
                column_block(16),
                whole(D, D),
                whole(8, D),
            ],
            scratch_shapes=[pltpu.VMEM((D, D), F32)],
        ),
        out_shape=[
            kind(F32, rows, length, D),
            kind(BF16, rows, D, length),
            kind(BF16, rows, 16, length),
            kind(BF16, D, D),
            kind(F32, 8, D),
        ],
        cost_estimate=cost(16),
        compiler_params=params(),
    )(counts, cot, pre, mid, att, prob, experts, small, up, out)


def backward_kernel(pieces, place_ref, *refs):
    x_ref, h_ref, q_ref, k_ref, v_ref, lse_ref, datt_ref, dlog_ref, code_ref = refs[:9]
    turned_ref, gbias_ref, gnorm_ref, gout_ref, gup_ref = refs[9:14]
    back_ref, ghead_ref, glow_ref = refs[14:17]
    packed = refs[17:-7]
    dk_ref, dv_ref, column_ref, total_ref, gain_ref, shift_ref, pack_sem = refs[-7:]
    length = x_ref.shape[1]

    @pl.when(pl.program_id(0) == 0)
    def _():
        total_ref[...] = jnp.zeros_like(total_ref)
        gain_ref[...] = jnp.zeros_like(gain_ref)
        shift_ref[...] = jnp.zeros_like(shift_ref)

    set_columns(code_ref, column_ref)
    dk_ref[...] = jnp.zeros_like(dk_ref)
    dv_ref[...] = jnp.zeros_like(dv_ref)

    def block_step(block, carry):
        q0, w0 = block_places(block, length)
        bias = block_bias(code_ref, column_ref, q0, w0)
        keys = k_ref[0, pl.ds(w0, KB), :]
        values = v_ref[0, pl.ds(w0, KB), :]
        dk = jnp.zeros((KB, HEAD), F32)
        dv = jnp.zeros((KB, HEAD), F32)
        for pair in range(EXPERTS // 2):
            queries = two_heads(q_ref, pair, q0)
            datt = two_heads(datt_ref, pair, q0)
            total = jnp.concatenate(
                [lse_ref[0, 2 * pair + half : 2 * pair + half + 1, pl.ds(q0, QB)] for half in (0, 1)],
                axis=1,
            )
            scores = dot(keys, queries, NN) * (HEAD**-0.5) + bias
            soft = jnp.exp(scores - total)
            dsoft = dot(values, datt, NN)
            dv = dv + dot(soft.astype(BF16), datt, NT)
            inner = jnp.sum(soft * dsoft, axis=0, keepdims=True)
            dscores = (soft * (dsoft - inner)).astype(BF16)
            dk = dk + dot(dscores, queries, NT)
            dq = (dot(keys, dscores, TN) * (HEAD**-0.5)).astype(BF16)
            for half in range(2):
                head = 2 * pair + half
                back_ref[0, 64 * head : 64 * (head + 1), pl.ds(q0, QB)] = dq[
                    :, QB * half : QB * (half + 1)
                ]
        dk_ref[pl.ds(w0, KB), :] += dk * (HEAD**-0.5)
        dv_ref[pl.ds(w0, KB), :] += dv
        return carry

    lax.fori_loop(0, length // QB, block_step, 0)
    back_ref[0, T_R:T_K, :] = dlog_ref[0]
    back_ref[0, T_K:T_V, :] = dk_ref[...].T.astype(BF16)
    back_ref[0, T_V:T_ALL, :] = dv_ref[...].T.astype(BF16)
    normal, _ = norm(x_ref[0].astype(F32))
    back = back_ref[0]
    total_ref[...] += dot(back, h_ref[0], NN)
    gain_ref[...] += dot(back, normal.astype(BF16), NN)
    shift_ref[...] += jnp.sum(back.astype(F32), axis=1, keepdims=True)

    @pl.when(pl.program_id(0) == pl.num_programs(0) - 1)
    def _():
        ghead_ref[0:D, :] = total_ref[0:D, :].T.astype(BF16)
        low = total_ref[T_K:T_ALL, :].astype(BF16)
        ghead_ref[D : D + 64, :] = narrow_flat(low[0:64]).astype(BF16)
        ghead_ref[D + 64 : D + 128, :] = narrow_flat(low[64:128]).astype(BF16)
        turned = turned_ref[...].astype(F32)
        glow_ref[...] = jnp.concatenate(
            [
                router_flat(total_ref[T_R : T_R + 8, :]),
                gbias_ref[0:4, :],
                jnp.sum(turned * gain_ref[...], axis=0, keepdims=True),
                jnp.sum(turned * shift_ref[...], axis=0, keepdims=True),
                gnorm_ref[0:2, :],
                gbias_ref[4:5, :],
                jnp.zeros((SMALL - 17, D), F32),
            ],
            axis=0,
        ).astype(BF16)
        if pieces:
            ins = [ghead_ref, gout_ref, gup_ref, glow_ref]
            pack_start(pieces, range(4), place_ref, ins, packed, pack_sem)
            pack_end(packed, pack_sem)


def attention_backward(
    plan, place, x, h, q, k, v, lse, datt, dlog, code, turned, gbias, gnorm, gout, gup, pieces
):
    rows, length = x.shape[0], x.shape[1]
    row3 = lambda a, b: pl.BlockSpec((1, a, b), lambda i, *_: (i, 0, 0))
    packed = [kind(BF16, LANES // 2, 1, plan.rows + SMALL, D)] * 2 if pieces else []
    head = min(LATE_ROWS, gup.shape[0])
    return pl.pallas_call(
        partial(backward_kernel, pieces),
        grid_spec=pltpu.PrefetchScalarGridSpec(
            num_scalar_prefetch=1,
            grid=(rows,),
            in_specs=[
                row3(length, D),
                row3(length, D),
                row3(D, length),
                row3(length, HEAD),
                row3(length, HEAD),
                row3(8, length),
                row3(D, length),
                row3(16, length),
                row3(1, length),
                whole(T_ALL, D),
                whole(8, D),
                whole(8, D),
                whole(D, D),
                whole(head, D),
            ],
            out_specs=[row3(T_ALL, length), whole(ROW_O, D), whole(SMALL, D)]
            + [ANYWHERE] * len(packed),
            scratch_shapes=[
                pltpu.VMEM((length, HEAD), F32),
                pltpu.VMEM((length, HEAD), F32),
                pltpu.VMEM((length, QB), F32),
                pltpu.VMEM((T_ALL, D), F32),
                pltpu.VMEM((T_ALL, D), F32),
                pltpu.VMEM((T_ALL, 1), F32),
                pltpu.SemaphoreType.DMA((2,)),
            ],
        ),
        out_shape=[
            kind(BF16, rows, T_ALL, length),
            kind(BF16, ROW_O, D),
            kind(BF16, SMALL, D),
        ]
        + packed,
        cost_estimate=cost(33),
        compiler_params=params(),
    )(place, x, h, q, k, v, lse, datt, dlog, code, turned, gbias, gnorm, gout, gup)


def input_kernel(x_ref, dmid_ref, back_ref, turned_ref, small_ref, gx_ref):
    normal, scaler = norm(x_ref[0].astype(F32))
    back = dot(back_ref[0], turned_ref[...], TN) * small_ref[12:13, :]
    gx_ref[0] = (dmid_ref[0] + norm_back(back, normal, scaler)).astype(BF16)


def input_grad(x, dmid, back, turned, small):
    rows, length = x.shape[0], x.shape[1]
    return pl.pallas_call(
        input_kernel,
        grid=(rows, length // TB),
        in_specs=[
            row_block(D),
            row_block(D),
            column_block(T_ALL),
            whole(T_ALL, D),
            whole(SMALL, D),
        ],
        out_specs=row_block(D),
        out_shape=kind(BF16, rows, length, D),
        cost_estimate=cost(8),
        compiler_params=params(),
    )(x, dmid, back, turned, small)


def output_kernel(counts_ref, mid_ref, hid_ref, small_ref, down_ref, out_ref):
    result = dot(hid_ref[0], down_ref[...], NN) + small_ref[16:17, :]
    valid = valid_tokens(counts_ref, mid_ref.shape[1])
    out_ref[0] = (valid * (mid_ref[0] + result)).astype(BF16)


def layer_output(counts, mid, hid, small, down):
    rows, length = mid.shape[0], mid.shape[1]
    return pl.pallas_call(
        output_kernel,
        grid_spec=pltpu.PrefetchScalarGridSpec(
            num_scalar_prefetch=1,
            grid=(rows, length // TB),
            in_specs=[row_block(D), row_block(FF), whole(SMALL, D), whole(FF, D)],
            out_specs=row_block(D),
        ),
        out_shape=kind(BF16, rows, length, D),
        cost_estimate=cost(9),
        compiler_params=params(),
    )(counts, mid, hid, small, down)


PLANES = 4
LANES = 8
ALL = PLANES * LANES
LATE_ROWS = 192


def move(value, pairs):
    return lax.ppermute(value, AXES, pairs)


def across(value, bits):
    return move(value, [(d, d ^ bits) for d in range(ALL)])


def by_plane(values, plane):
    out = values[-1]
    for z in range(len(values) - 1):
        out = jnp.where(plane == z, values[z], out)
    return out


def plane_spread(own):
    return [own] + [across(own, bits) for bits in (2, 4, 6)]


def core_spread(got):
    swapped = [across(part, 1) for part in got]
    return [part for both in zip(got, swapped) for part in both]


def plane_gather(plan, window, my_plane):
    got = [window]
    for s in range(1, PLANES):
        got.append(
            move(window, [(z * LANES + f, (z ^ s) * LANES + f) for z in range(PLANES) for f in range(LANES)])
        )
    of = lambda z: by_plane([got[z ^ mine] for mine in range(PLANES)], my_plane)
    low = ROW_S - 16 * plan.first(ALL - 1)
    planes = [of(z) for z in range(PLANES)]
    head = jnp.concatenate([planes[0], planes[-1][low : low + SMALL]], axis=0)
    return head, jnp.stack(planes[1:])


def pack_start(pieces, sources, place_ref, ins, packed, sem):
    keep_ref, send_ref = packed
    for place in range(LANES):

        def start(place=place):
            for source, at, amount, plane, lane, to in pieces:
                if source not in sources:
                    continue
                out = send_ref if (lane ^ place) & 1 else keep_ref
                pltpu.make_async_copy(
                    ins[source].at[pl.ds(at, amount), :],
                    out.at[(lane ^ place) >> 1, plane, pl.ds(to, amount), :],
                    sem.at[(lane ^ place) & 1],
                ).start()

        pl.when(place_ref[0] == place)(start)


def pack_end(packed, sem):
    for i in range(2):
        pltpu.make_async_copy(packed[i], packed[i], sem.at[i]).wait()


def window_pieces(plan, windows, spans, extra):
    pieces = []
    for d in windows:
        plane, lane = divmod(d, LANES)
        plane = plane - windows[0] // LANES
        begin = 16 * plan.first(d)
        for source, (low, high) in enumerate(spans):
            a, b = max(begin, low), min(begin + plan.rows, high)
            if a < b:
                pieces.append((source, a - low, b - a, plane, lane, a - begin))
        end = spans[-1][1]
        if begin + plan.rows > end:
            left = begin + plan.rows - end
            pieces.append((len(spans) - 1, 0, left, plane, lane, plan.rows - left))
        if extra:
            pieces.append((len(spans), 0, SMALL, plane, lane, plan.rows))
    return pieces


def core_sum(keep, send):
    got = across(send, 1)
    return [(keep[p].astype(F32) + got[p].astype(F32)).astype(BF16) for p in range(LANES // 2)]


def plane_sum(parts):
    total = parts[0].astype(F32)
    for p in range(1, LANES // 2):
        total = total + across(parts[p], 2 * p).astype(F32)
    return total.astype(BF16)


def main_parts(total, my_plane):
    owned = [total[0]] + [total[z] for z in range(PLANES - 1)]
    pick = lambda s: by_plane([owned[mine ^ s] for mine in range(PLANES)], my_plane)
    out = [pick(0)]
    for s in range(1, PLANES):
        pairs = [
            (z * LANES + f, (z ^ s) * LANES + f)
            for z in range(PLANES)
            if z ^ s
            for f in range(LANES)
        ]
        out.append(move(pick(s), pairs))
    return out


def head_parts(total):
    out = [total]
    last = PLANES - 1
    for s in range(1, PLANES):
        pairs = [(s * LANES + f, f) for f in range(LANES)]
        pairs.append(((s - 1) * LANES + LANES - 1, last * LANES + LANES - 1))
        out.append(move(total, pairs))
    return out


def owned_kernel(plan, at_ref, me_ref, *refs):
    main, head = refs[:PLANES], refs[PLANES : 2 * PLANES]
    out_ref, sum_ref, pad_ref = refs[2 * PLANES :]

    def add(parts, low, high):
        total = parts[0][low:high].astype(F32)
        for part in parts[1:]:
            total = total + part[low:high].astype(F32)
        return total

    @pl.when(me_ref[0] < LANES)
    def _():
        sum_ref[...] = add(head, 0, plan.rows)

    @pl.when(me_ref[0] >= LANES)
    def _():
        sum_ref[...] = add(main, 0, plan.rows)

    @pl.when(me_ref[0] == ALL - 1)
    def _():
        low = ROW_S - 16 * plan.first(ALL - 1)
        sum_ref[low : low + SMALL, :] = add(head, plan.rows, plan.rows + SMALL)

    for j in range(4):
        pad_ref[pl.ds(j, plan.rows, stride=4), :] = sum_ref[:, 128 * j : 128 * (j + 1)]
    out_ref[...] = pad_ref[pl.ds(at_ref[0], plan.lanes), :]


def take_owned(plan, at, me, main, head):
    out = pl.pallas_call(
        partial(owned_kernel, plan),
        grid_spec=pltpu.PrefetchScalarGridSpec(
            num_scalar_prefetch=2,
            grid=(1,),
            in_specs=[whole(plan.rows, D)] * PLANES + [whole(plan.rows + SMALL, D)] * PLANES,
            out_specs=whole(plan.lanes, 128),
            scratch_shapes=[
                pltpu.VMEM((plan.rows, D), F32),
                pltpu.VMEM((plan.rows * 4, 128), F32),
            ],
        ),
        out_shape=kind(F32, plan.lanes, 128),
        compiler_params=params(),
    )(at, me, *main, *head)
    return out.reshape(-1)


def plain_sum(plan, planes, lanes, me, at, ghead, gout, gup, gdown, glow):
    grads = jnp.concatenate([ghead, gout, gup, gdown, glow], axis=0)
    grads = jnp.pad(grads, ((0, plan.rows), (0, 0)))
    parts = jnp.stack([grads[16 * plan.first(d) :][: plan.rows] for d in range(plan.devices)])
    parts = parts.reshape(planes, lanes, plan.rows, D)
    parts = lax.psum_scatter(parts, "fsdp", scatter_dimension=1, tiled=True)
    parts = lax.psum_scatter(parts, "dp", scatter_dimension=0, tiled=True)
    flat = parts.reshape(-1).astype(F32)
    return lax.dynamic_slice(flat, (at[0] * 128,), (plan.lanes * 128,))


def local(planes, lanes, x, shard, segments, experts, counts, cot):
    plan = Plan(planes * lanes, shard.shape[0])
    my_plane, my_lane = lax.axis_index("dp"), lax.axis_index("fsdp")
    me = my_plane * lanes + my_lane
    place = my_lane.astype(jnp.int32).reshape(1)
    at = ((plan.lanes * me) % 64).astype(jnp.int32).reshape(1)
    window = make_window(plan, at, shard)
    staged = (planes, lanes, plan.lanes) == (PLANES, LANES, 659)
    main_pieces, head_pieces = [], []
    ready = [place, place]
    if staged:
        head, rest = plane_gather(plan, window, my_plane)
        ready[0] = after(place, rest)
        head = core_spread(plane_spread(head))
        rest = plane_spread(rest)
        ready[1] = after(place, *rest)
        gathered = Gathered(plan, lanes, head, core_spread(rest), None)
        main_pieces = window_pieces(
            plan, range(LANES, ALL), [(ROW_U, ROW_D), (ROW_D, ROW_S)], False
        )
        head_pieces = window_pieces(
            plan, range(LANES), [(0, ROW_O), (ROW_O, ROW_U), (ROW_U, ROW_U + LATE_ROWS)], True
        )
    else:
        gathered = Gathered(plan, lanes, None, None, lax.all_gather(window, AXES, axis=0))
    rows, length = x.shape[0], x.shape[1]
    places = jnp.arange(length, dtype=jnp.int32)[None, :]
    code = jnp.where(places < counts[:, None], segments, -1 - places)
    code = code.astype(F32).reshape(-1, 1, length)
    pairs = jnp.swapaxes(experts, 1, 2)
    state = attention_forward(plan, gathered, ready[0], x, code, 0, None)
    turned, small = state[7:9]
    for row in range(1, rows):
        before = [*state[:7], turned, small]
        state = attention_forward(plan, gathered, ready[1], x, code, row, before)
    q, k, v, h, prob, lse, att = state[:7]
    hid, slope, mid, up, out, gdown = feed_up(
        plan, gathered, place, counts, x, cot, att, prob, pairs, small
    )
    pre, down, gbias, gup, *packed = feed_hidden(
        plan, gathered, place, counts, cot, slope, mid, small, gdown, main_pieces
    )
    dmid, datt, dlog, gout, gnorm = feed_branch(
        counts, cot, pre, mid, att, prob, pairs, small, up, out
    )
    third = place
    if staged:
        parts = core_sum(*packed)
        third = after(place, *parts)
        main = plane_sum(parts)
    back, ghead, glow, *packed = attention_backward(
        plan, third, x, h, q, k, v, lse, datt, dlog, code, turned, gbias, gnorm, gout, gup, head_pieces
    )
    if not staged:
        grads = plain_sum(plan, planes, lanes, me, at, ghead, gout, gup, gdown, glow)
        output = layer_output(counts, mid, hid, small, down)
        return output, input_grad(x, dmid, back, turned, small), grads
    main = main_parts(main, my_plane)
    parts = core_sum(packed[0][:, 0], packed[1][:, 0])
    grad_tokens = input_grad(x, dmid, after(back, *parts), turned, small)
    total = plane_sum(parts)
    output = layer_output(counts, after(mid, total), hid, small, down)
    me = me.astype(jnp.int32).reshape(1)
    return output, grad_tokens, take_owned(plan, at, me, main, head_parts(total))


def solution(mesh):
    spec = P(AXES)
    return jax.shard_map(
        partial(local, mesh.shape["dp"], mesh.shape["fsdp"]),
        mesh=mesh,
        in_specs=(spec,) * 6,
        out_specs=(spec,) * 3,
        check_vma=False,
    )
```

```python
from functools import partial

import jax
import jax.numpy as jnp
from jax import lax
from jax.experimental import pallas as pl
from jax.experimental.pallas import tpu as pltpu
from jax.sharding import PartitionSpec as P

D = 512
FF = 2048
EXPERTS = 8
HEAD = 64
EPS = 1e-05
NEG = -1e30
F32 = jnp.float32
BF16 = jnp.bfloat16
AXES = ("dp", "fsdp")

ROW_K = 512
ROW_V = 576
ROW_O = 640
ROW_U = 1152
ROW_D = 3200
ROW_S = 5248
SMALL = 32
ROWS_ALL = ROW_S + SMALL
T_R = 512
T_K = 528
T_V = 592
T_ALL = 656

QB = 128
KB = 256

NN = ((1,), (0,))
NT = ((1,), (1,))
TN = ((0,), (0,))

VMEM_MIB = 56


def dot(left, right, dims):
    return lax.dot_general(left, right, (dims, ((), ())), preferred_element_type=F32)


def cost(micros):
    return pl.CostEstimate(flops=int(micros * 1.1e9), bytes_accessed=int(micros * 1e5), transcendentals=0)


def after(value, *others):
    return lax.optimization_barrier((value, *others))[0]


def all_after(values, *others):
    return lax.optimization_barrier((*values, *others))[: len(values)]


def params(mib=VMEM_MIB):
    return pltpu.CompilerParams(vmem_limit_bytes=mib << 20)


def iota(shape, dim):
    return lax.broadcasted_iota(jnp.int32, shape, dim)


class Plan:
    def __init__(self, devices, shard):
        self.devices = devices
        self.lanes = shard // 128
        reach = max((self.lanes * d) % 64 for d in range(devices)) + self.lanes
        self.rows = -(-reach // 64) * 16

    def first(self, d):
        return (self.lanes * d) // 64

    def last(self, d):
        return (self.lanes * (d + 1) - 1) // 64


def window_kernel(plan, at_ref, shard_ref, out_ref, pad_ref):
    pad_ref[...] = jnp.zeros_like(pad_ref)
    pad_ref[64 : 64 + plan.lanes, :] = shard_ref[...]
    start = 64 - at_ref[0]
    for j in range(4):
        out_ref[:, 128 * j : 128 * (j + 1)] = pad_ref[
            pl.ds(start + j, plan.rows, stride=4), :
        ].astype(BF16)


def make_window(plan, at, shard):
    return pl.pallas_call(
        partial(window_kernel, plan),
        grid_spec=pltpu.PrefetchScalarGridSpec(
            num_scalar_prefetch=1,
            grid=(1,),
            in_specs=[pl.BlockSpec((plan.lanes, 128), lambda i, at: (0, 0))],
            out_specs=pl.BlockSpec((plan.rows, D), lambda i, at: (0, 0)),
            scratch_shapes=[pltpu.VMEM((plan.rows * 4 + 128, 128), F32)],
        ),
        out_shape=jax.ShapeDtypeStruct((plan.rows, D), BF16),
        compiler_params=params(),
    )(at, shard.reshape(plan.lanes, 128))


def row_pieces(plan, low, high):
    direct, shared = [], []
    for d in range(plan.devices):
        first, last = plan.first(d), plan.last(d)
        start = first
        if d > 0 and plan.last(d - 1) == first:
            start = first + 1
            if low <= first * 16 < high:
                shared.append((d, 0, first * 16 - low))
        begin, end = max(start * 16, low), min((last + 1) * 16, high)
        if begin < end:
            direct.append((d, begin - first * 16, begin - low, end - begin))
    return direct, shared


def start_rows(plan, source, low, high, dst_ref, tmp_ref, sem):
    direct, shared = row_pieces(plan, low, high)
    for d, at, to, amount in direct:
        pltpu.make_async_copy(
            source(d).at[pl.ds(at, amount), :], dst_ref.at[pl.ds(to, amount), :], sem.at[0]
        ).start()
    for slot, (d, at, _) in enumerate(shared):
        pltpu.make_async_copy(
            source(d).at[pl.ds(at, 16), :], tmp_ref.at[pl.ds(16 * slot, 16), :], sem.at[1]
        ).start()


def end_rows(plan, low, high, dst_ref, tmp_ref, sem):
    _, shared = row_pieces(plan, low, high)
    pltpu.make_async_copy(dst_ref, dst_ref, sem.at[0]).wait()
    if shared:
        part = tmp_ref.at[pl.ds(0, 16 * len(shared)), :]
        pltpu.make_async_copy(part, part, sem.at[1]).wait()
        for slot, (_, _, to) in enumerate(shared):
            dst_ref[to : to + 16, :] = (
                dst_ref[to : to + 16, :].astype(F32)
                + tmp_ref[16 * slot : 16 * slot + 16, :].astype(F32)
            ).astype(BF16)


def shared_rows(plan, low, high):
    return max(16, 16 * len(row_pieces(plan, low, high)[1]))


class Gathered:
    def __init__(self, plan, whole=None, own=(), head=(), rest=(), diag=()):
        self.plan, self.whole = plan, whole
        self.parts = [list(own), list(head), list(rest), list(diag)]
        self.small_at = ROW_S - 16 * plan.first(plan.devices - 1)

    def arrays(self, kinds):
        if self.whole is not None:
            return [self.whole]
        return [array for i in range(kinds) for array in self.parts[i]]

    def fetch(self, place_ref, refs, kinds, start):
        if self.whole is not None:
            last = self.plan.devices - 1
            start(lambda d: refs[0].at[d], refs[0].at[last, pl.ds(self.small_at, SMALL), :])
            return
        sets, at = [], 0
        for part in self.parts[:kinds]:
            sets.append(refs[at : at + len(part)])
            at += len(part)
        for mine in range(PLANES):
            for place in range(LANES):

                def source(d, mine=mine, place=place):
                    plane, lane = divmod(d, LANES)
                    lane = lane ^ place
                    if plane == mine:
                        return sets[0][lane]
                    if plane == early_plane(mine):
                        return sets[1][lane].at[pl.ds(0, self.plan.rows), :]
                    if lane < 6:
                        return sets[2][lane].at[late_planes(mine).index(plane)]
                    return sets[3][2 * ((plane ^ mine) - 1) + (lane & 1)]

                small = sets[1][(LANES - 1) ^ place].at[pl.ds(self.plan.rows, SMALL), :]
                here = (place_ref[0] == place) & (place_ref[1] == mine)
                pl.when(here)(partial(start, source, small))


def narrow_places():
    row, column = iota((D, D), 0), iota((D, D), 1)
    return (column == 8 * (row % 64) + row // 64).astype(BF16)


def narrow_transposed(flat):
    stacked = [
        jnp.concatenate([flat[64 * i : 64 * (i + 1), 64 * j : 64 * (j + 1)] for i in (0, 1)], axis=1)
        for j in range(8)
    ]
    return dot(jnp.concatenate(stacked, axis=0), narrow_places(), TN)


def narrow_flat(turned):
    stacked = dot(narrow_places(), turned, NT)
    return jnp.concatenate(
        [
            jnp.concatenate(
                [stacked[64 * j : 64 * (j + 1), 64 * i : 64 * (i + 1)] for j in range(8)], axis=1
            )
            for i in (0, 1)
        ],
        axis=0,
    )


def router_mask():
    return iota((64, D), 1) % 8 == iota((64, D), 0) % 8


def router_places():
    return (iota((D, 64), 0) // 8 == iota((D, 64), 1)).astype(BF16)


def router_transposed(flat):
    rows = jnp.concatenate([jnp.broadcast_to(flat[r : r + 1, :], (8, D)) for r in range(8)], axis=0)
    picked = dot(jnp.where(router_mask(), rows, 0.0).astype(BF16), router_places(), NN)
    return jnp.concatenate([picked[8 * r : 8 * (r + 1), :] for r in range(8)], axis=1)


def router_flat(turned):
    stacked = jnp.concatenate([turned[:, 64 * r : 64 * (r + 1)] for r in range(8)], axis=0)
    full = jnp.where(router_mask(), dot(stacked.astype(BF16), router_places(), NT), 0.0)
    return jnp.concatenate(
        [jnp.sum(full[8 * r : 8 * (r + 1)], axis=0, keepdims=True) for r in range(8)], axis=0
    )


def norm(source):
    center = source - jnp.mean(source, axis=-1, keepdims=True)
    scaler = lax.rsqrt(jnp.mean(center * center, axis=-1, keepdims=True) + EPS)
    return center * scaler, scaler


def norm_back(grad_normal, normal, scaler):
    return scaler * (
        grad_normal
        - jnp.mean(grad_normal, axis=-1, keepdims=True)
        - normal * jnp.mean(grad_normal * normal, axis=-1, keepdims=True)
    )


def two_heads(ref, pair, q0):
    return jnp.concatenate(
        [
            ref[0, 128 * pair : 128 * pair + 64, pl.ds(q0, QB)],
            ref[0, 128 * pair + 64 : 128 * pair + 128, pl.ds(q0, QB)],
        ],
        axis=1,
    )


def two_rows(ref, pair, q0):
    return jnp.concatenate(
        [ref[0, 2 * pair + half : 2 * pair + half + 1, pl.ds(q0, QB)] for half in (0, 1)], axis=1
    )


def block_bias(code_ref, column_ref, q0, w0):
    row = code_ref[0, :, pl.ds(q0, QB)]
    bias = jnp.where(column_ref[pl.ds(w0, KB), :] == row, 0.0, NEG)
    return jnp.concatenate([bias, bias], axis=1)


def set_columns(code_ref, column_ref):
    length = code_ref.shape[2]
    column_ref[...] = jnp.broadcast_to(code_ref[0], (QB, length)).T


def block_places(block, length):
    q0 = pl.multiple_of(block * QB, QB)
    w0 = pl.multiple_of(jnp.clip(q0 - 64, 0, length - KB), 64)
    return q0, w0


def forward_prepare(plan, gathered, place_ref, refs, turned_ref, small_ref, scratch):
    rows_ref, low_ref, tmp_ref, sem = scratch

    def start(source, small):
        start_rows(plan, source, 0, ROW_O, rows_ref, tmp_ref, sem)
        pltpu.make_async_copy(small, low_ref, sem.at[2]).start()

    gathered.fetch(place_ref, refs, 2, start)
    pltpu.make_async_copy(low_ref, low_ref, sem.at[2]).wait()
    end_rows(plan, 0, ROW_O, rows_ref, tmp_ref, sem)
    small_ref[...] = low_ref[...].astype(F32)
    turned_ref[0:D, :] = rows_ref[0:D, :].astype(F32).T.astype(BF16)
    turned_ref[T_R:T_K, :] = jnp.concatenate(
        [router_transposed(small_ref[0:8, :]), jnp.zeros((8, D), F32)], axis=0
    ).astype(BF16)
    turned_ref[T_K:T_ALL, :] = narrow_transposed(rows_ref[ROW_K:ROW_O, :]).astype(BF16)


def forward_row(x_ref, code_ref, turned_ref, small_ref, outs, column_ref):
    q_ref, k_ref, v_ref, h_ref, prob_ref, lse_ref, att_ref = outs
    length = x_ref.shape[1]
    set_columns(code_ref, column_ref)
    normal, _ = norm(x_ref[0].astype(F32))
    h = (normal * small_ref[12:13, :] + small_ref[13:14, :]).astype(BF16)
    h_ref[0] = h
    turned = dot(turned_ref[0:T_K, :], h, NT)
    q_ref[0] = turned[0:D].astype(BF16)
    logits = turned[T_R : T_R + 8]
    shifted = jnp.exp(logits - jnp.max(logits, axis=0, keepdims=True))
    prob_ref[0] = shifted / jnp.sum(shifted, axis=0, keepdims=True)
    kv = dot(h, turned_ref[T_K:T_ALL, :], NT).astype(BF16)
    k_ref[0] = kv[:, 0:HEAD]
    v_ref[0] = kv[:, HEAD:]

    def block_step(block, carry):
        q0, w0 = block_places(block, length)
        bias = block_bias(code_ref, column_ref, q0, w0)
        keys = k_ref[0, pl.ds(w0, KB), :]
        values = v_ref[0, pl.ds(w0, KB), :]
        pairs = range(EXPERTS // 2)
        scores = [dot(keys, two_heads(q_ref, pair, q0), NN) * (HEAD**-0.5) + bias for pair in pairs]
        peak = [jnp.max(part, axis=0, keepdims=True) for part in scores]
        expd = [jnp.exp(part - top) for part, top in zip(scores, peak)]
        summed = [jnp.sum(part, axis=0, keepdims=True) for part in expd]
        atts = [dot(values, part.astype(BF16), TN) for part in expd]
        for pair in pairs:
            att = atts[pair] * (1.0 / summed[pair])
            total = peak[pair] + jnp.log(summed[pair])
            for half in range(2):
                head, part = 2 * pair + half, slice(QB * half, QB * (half + 1))
                att_ref[0, 64 * head : 64 * (head + 1), pl.ds(q0, QB)] = att[:, part]
                lse_ref[0, head : head + 1, pl.ds(q0, QB)] = total[:, part]
        return carry

    lax.fori_loop(0, length // QB, block_step, 0, unroll=2)


def forward_first(plan, gathered, count, place_ref, x_ref, code_ref, *refs):
    wins, refs = refs[:count], refs[count:]
    outs, (turned_ref, small_ref), scratch = refs[:7], refs[7:9], refs[9:]
    forward_prepare(plan, gathered, place_ref, wins, turned_ref, small_ref, scratch[1:])
    forward_row(x_ref, code_ref, turned_ref, small_ref, outs, scratch[0])


def forward_next(place_ref, x_ref, code_ref, turned_ref, small_ref, *refs):
    forward_row(x_ref, code_ref, turned_ref, small_ref, refs[7:14], refs[14])


def attention_forward(plan, gathered, place, x, code, row, before):
    rows, length = x.shape[0], x.shape[1]
    row3 = lambda a, b: pl.BlockSpec((1, a, b), lambda *_: (row, 0, 0))
    sizes = [
        (D, length, BF16),
        (length, HEAD, BF16),
        (length, HEAD, BF16),
        (length, D, BF16),
        (8, length, F32),
        (8, length, F32),
        (D, length, F32),
    ]
    out_specs = [row3(a, b) for a, b, _ in sizes]
    out_shape = [kind(c, rows, a, b) for a, b, c in sizes]
    scratch = [pltpu.VMEM((length, QB), F32)]
    in_specs = [row3(length, D), row3(1, length)]
    if before is None:
        wins = gathered.arrays(2)
        kernel = partial(forward_first, plan, gathered, len(wins))
        operands = [place, x, code, *wins]
        in_specs = in_specs + [ANYWHERE] * len(wins)
        out_specs = out_specs + [whole(T_ALL, D), whole(SMALL, D)]
        out_shape = out_shape + [kind(BF16, T_ALL, D), kind(F32, SMALL, D)]
        scratch = scratch + [
            pltpu.VMEM((ROW_O, D), BF16),
            pltpu.VMEM((SMALL, D), BF16),
            pltpu.VMEM((shared_rows(plan, 0, ROW_O), D), BF16),
            pltpu.SemaphoreType.DMA((3,)),
        ]
        aliases = {}
    else:
        kernel = forward_next
        operands = [place, x, code, *before[7:9], *before[:7]]
        in_specs = in_specs + [whole(T_ALL, D), whole(SMALL, D)] + [ANYWHERE] * 7
        aliases = {5 + i: i for i in range(7)}
    return pl.pallas_call(
        kernel,
        grid_spec=pltpu.PrefetchScalarGridSpec(
            num_scalar_prefetch=1,
            grid=(1,),
            in_specs=in_specs,
            out_specs=out_specs,
            scratch_shapes=scratch,
        ),
        out_shape=out_shape,
        input_output_aliases=aliases,
        cost_estimate=cost(14),
        compiler_params=params(),
    )(*operands)


TB = 512


def chosen_experts(experts_ref, length):
    ids = iota((EXPERTS, length), 0)
    chosen = (experts_ref[0, 0:1, :] == ids) | (experts_ref[0, 1:2, :] == ids)
    return chosen.astype(F32)


def valid_tokens(counts_ref, amount):
    place = pl.program_id(1) * amount + iota((amount, 1), 0)
    return (place < counts_ref[pl.program_id(0)]).astype(F32)


def by_head(values, gate):
    return jnp.concatenate(
        [values[64 * e : 64 * (e + 1)] * gate[e : e + 1] for e in range(EXPERTS)], axis=0
    )


def gelu_parts(source):
    scale = (2.0 / jnp.pi) ** 0.5
    square = source * source
    share = 0.5 + 0.5 * jnp.tanh(source * (scale + (scale * 0.044715) * square))
    value = source * share
    slope = share + (value - value * share) * (2.0 * scale + (6.0 * scale * 0.044715) * square)
    return value, slope


def first_step():
    return (pl.program_id(0) == 0) & (pl.program_id(1) == 0)


def last_step():
    return (pl.program_id(0) == pl.num_programs(0) - 1) & (
        pl.program_id(1) == pl.num_programs(1) - 1
    )


def feed_kernel(plan, gathered, count, pieces, place_ref, counts_ref, *refs):
    x_ref, cot_ref, att_ref, prob_ref, experts_ref, small_ref = refs[:6]
    wins = refs[6 : 6 + count]
    hid_ref, mid_ref, dmid_ref, datt_ref, dlog_ref, inner_ref = refs[6 + count : 12 + count]
    down_ref, gout_ref, gsmall_ref, gup_ref, gdown_ref = refs[12 + count : 17 + count]
    packed = refs[17 + count : -12]
    rows_ref, up_ref, flat_ref, tmp_ref, tmp2_ref, wide_ref = refs[-12:-6]
    tdown_ref, tup_ref, tout_ref, sem, sem2, pack_sem = refs[-6:]

    @pl.when(first_step())
    def _():
        def start(source, small):
            start_rows(plan, source, ROW_O, ROW_D, rows_ref, tmp_ref, sem)
            start_rows(plan, source, ROW_D, ROW_S, down_ref, tmp2_ref, sem2)

        gathered.fetch(place_ref, wins, 4, start)
        for ref in (tdown_ref, tup_ref, tout_ref, gsmall_ref):
            ref[...] = jnp.zeros_like(ref)
        end_rows(plan, ROW_O, ROW_D, rows_ref, tmp_ref, sem)
        for c in range(4):
            wide_ref[c] = rows_ref[D:, 128 * c : 128 * (c + 1)].astype(F32)
            for j in range(4):
                up_ref[:, D * j + 128 * c : D * j + 128 * (c + 1)] = wide_ref[
                    c, pl.ds(j, D, stride=4), :
                ].astype(BF16)
        end_rows(plan, ROW_D, ROW_S, down_ref, tmp2_ref, sem2)

    amount = x_ref.shape[1]
    prob = prob_ref[0]
    chosen = chosen_experts(experts_ref, amount)
    gate = prob * chosen
    att = att_ref[0]
    mixed = by_head(att, gate).astype(BF16)
    middle = x_ref[0].astype(F32) + dot(mixed, rows_ref[0:D, :], TN)
    mid_ref[0] = middle
    normal, scaler = norm(middle)
    gain = small_ref[14:15, :]
    h = (normal * gain + small_ref[15:16, :]).astype(BF16)
    grad = valid_tokens(counts_ref, amount) * cot_ref[0].astype(F32)
    grad_low = grad.astype(BF16)
    parts = [slice(2 * D * j, 2 * D * (j + 1)) for j in range(2)]
    dhid = [dot(grad_low, down_ref[part, :], NT) for part in parts]
    back = jnp.zeros((amount, D), F32)
    for j, part in enumerate(parts):
        bias = jnp.concatenate([small_ref[8 + i : 9 + i, :] for i in (2 * j, 2 * j + 1)], axis=1)
        value, slope = gelu_parts(dot(h, up_ref[:, part], NN) + bias)
        value = value.astype(BF16)
        hid_ref[0, :, part] = value
        pre = slope * dhid[j]
        sums = jnp.sum(pre, axis=0, keepdims=True)
        for i in range(2):
            gsmall_ref[2 * j + i : 2 * j + i + 1, :] += sums[:, D * i : D * (i + 1)]
        pre = pre.astype(BF16)
        tdown_ref[part, :] += dot(value, grad_low, TN)
        tup_ref[:, part] += dot(h, pre, TN)
        back = back + dot(pre, up_ref[:, part], NT)
    gsmall_ref[4:5, :] += jnp.sum(back * normal, axis=0, keepdims=True)
    gsmall_ref[5:6, :] += jnp.sum(back, axis=0, keepdims=True)
    gsmall_ref[6:7, :] += jnp.sum(grad, axis=0, keepdims=True)
    dmid = grad + norm_back(back * gain, normal, scaler)
    dmid_ref[0] = dmid
    branch = dmid.astype(BF16)
    tout_ref[...] += dot(mixed, branch, NN)
    dmixed = dot(rows_ref[0:D, :], branch, NT)
    dgate = jnp.concatenate(
        [
            jnp.sum(
                dmixed[64 * e : 64 * (e + 1)] * att[64 * e : 64 * (e + 1)], axis=0, keepdims=True
            )
            for e in range(EXPERTS)
        ],
        axis=0,
    )
    datt_ref[0] = by_head(dmixed, gate).astype(BF16)
    inner_ref[0] = gate * dgate
    dprob = dgate * chosen
    dlog = prob * (dprob - jnp.sum(prob * dprob, axis=0, keepdims=True))
    dlog_ref[0] = jnp.concatenate([dlog, jnp.zeros_like(dlog)], axis=0).astype(BF16)

    @pl.when(last_step())
    def _():
        gdown_ref[...] = tdown_ref[...].astype(BF16)
        if pieces:
            pack_start(pieces, [1], place_ref, [flat_ref, gdown_ref], packed, pack_sem)
        gout_ref[...] = tout_ref[...].astype(BF16)
        for c in range(4):
            for j in range(4):
                wide_ref[c, pl.ds(j, D, stride=4), :] = tup_ref[
                    :, D * j + 128 * c : D * j + 128 * (c + 1)
                ]
            flat_ref[:, 128 * c : 128 * (c + 1)] = wide_ref[c].astype(BF16)
        gup_ref[...] = flat_ref[0 : gup_ref.shape[0], :]
        if pieces:
            pack_start(pieces, [0], place_ref, [flat_ref, gdown_ref], packed, pack_sem)
            pack_end(packed, pack_sem)


def row_block(*tail):
    return pl.BlockSpec((1, TB, *tail), lambda i, j, *_: (i, j, 0))


def column_block(height):
    return pl.BlockSpec((1, height, TB), lambda i, j, *_: (i, 0, j))


def whole(*shape):
    return pl.BlockSpec(shape, lambda *_: (0,) * len(shape))


ANYWHERE = pl.BlockSpec(memory_space=pl.ANY)


def kind(dtype, *shape):
    return jax.ShapeDtypeStruct(shape, dtype)


def feed_forward(plan, gathered, place, counts, x, cot, att, prob, experts, small, pieces):
    rows, length = x.shape[0], x.shape[1]
    wins = gathered.arrays(4)
    head = LATE_ROWS if pieces else FF
    packed = [kind(BF16, LANES // 2, PLANES - 1, plan.rows, D)] * 2 if pieces else []
    return pl.pallas_call(
        partial(feed_kernel, plan, gathered, len(wins), pieces),
        grid_spec=pltpu.PrefetchScalarGridSpec(
            num_scalar_prefetch=2,
            grid=(rows, length // TB),
            in_specs=[
                row_block(D),
                row_block(D),
                column_block(D),
                column_block(8),
                column_block(2),
                whole(SMALL, D),
            ]
            + [ANYWHERE] * len(wins),
            out_specs=[
                row_block(FF),
                row_block(D),
                row_block(D),
                column_block(D),
                column_block(16),
                column_block(8),
                whole(FF, D),
                whole(D, D),
                whole(8, D),
                whole(head, D),
                whole(FF, D),
            ]
            + [ANYWHERE] * len(packed),
            scratch_shapes=[
                pltpu.VMEM((ROW_D - ROW_O, D), BF16),
                pltpu.VMEM((D, FF), BF16),
                pltpu.VMEM((FF, D), BF16),
                pltpu.VMEM((shared_rows(plan, ROW_O, ROW_D), D), BF16),
                pltpu.VMEM((shared_rows(plan, ROW_D, ROW_S), D), BF16),
                pltpu.VMEM((4, FF, 128), F32),
                pltpu.VMEM((FF, D), F32),
                pltpu.VMEM((D, FF), F32),
                pltpu.VMEM((D, D), F32),
                pltpu.SemaphoreType.DMA((2,)),
                pltpu.SemaphoreType.DMA((2,)),
                pltpu.SemaphoreType.DMA((2,)),
            ],
        ),
        out_shape=[
            kind(BF16, rows, length, FF),
            kind(F32, rows, length, D),
            kind(F32, rows, length, D),
            kind(BF16, rows, D, length),
            kind(BF16, rows, 16, length),
            kind(F32, rows, 8, length),
            kind(BF16, FF, D),
            kind(BF16, D, D),
            kind(F32, 8, D),
            kind(BF16, head, D),
            kind(BF16, FF, D),
        ]
        + packed,
        cost_estimate=cost(50),
        compiler_params=params(60),
    )(place, counts, x, cot, att, prob, experts, small, *wins)


def backward_kernel(pieces, place_ref, *refs):
    x_ref, h_ref, q_ref, k_ref, v_ref, lse_ref, inner_ref, datt_ref, dlog_ref, code_ref = refs[:10]
    turned_ref, gsmall_ref, gout_ref, gup_ref = refs[10:14]
    back_ref, ghead_ref, glow_ref = refs[14:17]
    packed = refs[17:-7]
    dk_ref, dv_ref, column_ref, total_ref, gain_ref, shift_ref, pack_sem = refs[-7:]
    length = x_ref.shape[1]

    @pl.when(pl.program_id(0) == 0)
    def _():
        total_ref[...] = jnp.zeros_like(total_ref)
        gain_ref[...] = jnp.zeros_like(gain_ref)
        shift_ref[...] = jnp.zeros_like(shift_ref)

    set_columns(code_ref, column_ref)
    dk_ref[...] = jnp.zeros_like(dk_ref)
    dv_ref[...] = jnp.zeros_like(dv_ref)

    def block_step(block, carry):
        q0, w0 = block_places(block, length)
        bias = block_bias(code_ref, column_ref, q0, w0)
        keys = k_ref[0, pl.ds(w0, KB), :]
        values = v_ref[0, pl.ds(w0, KB), :]
        pairs = range(EXPERTS // 2)
        queries = [two_heads(q_ref, pair, q0) for pair in pairs]
        datt = [two_heads(datt_ref, pair, q0) for pair in pairs]
        soft = [
            jnp.exp(dot(keys, part, NN) * (HEAD**-0.5) + bias - two_rows(lse_ref, pair, q0))
            for pair, part in enumerate(queries)
        ]
        dscores = [
            (soft[pair] * (dot(values, part, NN) - two_rows(inner_ref, pair, q0))).astype(BF16)
            for pair, part in enumerate(datt)
        ]
        soft = jnp.concatenate([part.astype(BF16) for part in soft], axis=1)
        dv = dot(soft, jnp.concatenate(datt, axis=1), NT)
        dk = dot(jnp.concatenate(dscores, axis=1), jnp.concatenate(queries, axis=1), NT)
        for pair in pairs:
            dq = (dot(keys, dscores[pair], TN) * (HEAD**-0.5)).astype(BF16)
            for half in range(2):
                head, part = 2 * pair + half, slice(QB * half, QB * (half + 1))
                back_ref[0, 64 * head : 64 * (head + 1), pl.ds(q0, QB)] = dq[:, part]
        dk_ref[pl.ds(w0, KB), :] += dk * (HEAD**-0.5)
        dv_ref[pl.ds(w0, KB), :] += dv
        return carry

    lax.fori_loop(0, length // QB, block_step, 0, unroll=2)
    back_ref[0, T_R:T_K, :] = dlog_ref[0]
    back_ref[0, T_K:T_V, :] = dk_ref[...].T.astype(BF16)
    back_ref[0, T_V:T_ALL, :] = dv_ref[...].T.astype(BF16)
    normal, _ = norm(x_ref[0].astype(F32))
    back = back_ref[0]
    total_ref[...] += dot(back, h_ref[0], NN)
    gain_ref[...] += dot(back, normal.astype(BF16), NN)
    shift_ref[...] += jnp.sum(back.astype(F32), axis=1, keepdims=True)

    @pl.when(pl.program_id(0) == pl.num_programs(0) - 1)
    def _():
        ghead_ref[0:D, :] = total_ref[0:D, :].T.astype(BF16)
        ghead_ref[D:ROW_O, :] = narrow_flat(total_ref[T_K:T_ALL, :].astype(BF16)).astype(BF16)
        turned = turned_ref[...].astype(F32)
        glow_ref[...] = jnp.concatenate(
            [
                router_flat(total_ref[T_R : T_R + 8, :]),
                gsmall_ref[0:4, :],
                jnp.sum(turned * gain_ref[...], axis=0, keepdims=True),
                jnp.sum(turned * shift_ref[...], axis=0, keepdims=True),
                gsmall_ref[4:7, :],
                jnp.zeros((SMALL - 17, D), F32),
            ],
            axis=0,
        ).astype(BF16)
        if pieces:
            ins = [ghead_ref, gout_ref, gup_ref, glow_ref]
            pack_start(pieces, range(4), place_ref, ins, packed, pack_sem)
            pack_end(packed, pack_sem)


def attention_backward(
    plan, place, x, h, q, k, v, lse, inner, datt, dlog, code, turned, gsmall, gout, gup, pieces
):
    rows, length = x.shape[0], x.shape[1]
    row3 = lambda a, b: pl.BlockSpec((1, a, b), lambda i, *_: (i, 0, 0))
    packed = [kind(BF16, LANES // 2, 1, plan.rows + SMALL, D)] * 2 if pieces else []
    head = min(LATE_ROWS, gup.shape[0])
    return pl.pallas_call(
        partial(backward_kernel, pieces),
        grid_spec=pltpu.PrefetchScalarGridSpec(
            num_scalar_prefetch=1,
            grid=(rows,),
            in_specs=[
                row3(length, D),
                row3(length, D),
                row3(D, length),
                row3(length, HEAD),
                row3(length, HEAD),
                row3(8, length),
                row3(8, length),
                row3(D, length),
                row3(16, length),
                row3(1, length),
                whole(T_ALL, D),
                whole(8, D),
                whole(D, D),
                whole(head, D),
            ],
            out_specs=[row3(T_ALL, length), whole(ROW_O, D), whole(SMALL, D)]
            + [ANYWHERE] * len(packed),
            scratch_shapes=[
                pltpu.VMEM((length, HEAD), F32),
                pltpu.VMEM((length, HEAD), F32),
                pltpu.VMEM((length, QB), F32),
                pltpu.VMEM((T_ALL, D), F32),
                pltpu.VMEM((T_ALL, D), F32),
                pltpu.VMEM((T_ALL, 1), F32),
                pltpu.SemaphoreType.DMA((2,)),
            ],
        ),
        out_shape=[
            kind(BF16, rows, T_ALL, length),
            kind(BF16, ROW_O, D),
            kind(BF16, SMALL, D),
        ]
        + packed,
        cost_estimate=cost(33),
        compiler_params=params(),
    )(place, x, h, q, k, v, lse, inner, datt, dlog, code, turned, gsmall, gout, gup)


def input_kernel(x_ref, dmid_ref, back_ref, turned_ref, small_ref, gx_ref):
    normal, scaler = norm(x_ref[0].astype(F32))
    back = dot(back_ref[0], turned_ref[...], TN) * small_ref[12:13, :]
    gx_ref[0] = (dmid_ref[0] + norm_back(back, normal, scaler)).astype(BF16)


def input_grad(x, dmid, back, turned, small):
    rows, length = x.shape[0], x.shape[1]
    return pl.pallas_call(
        input_kernel,
        grid=(rows, length // TB),
        in_specs=[
            row_block(D),
            row_block(D),
            column_block(T_ALL),
            whole(T_ALL, D),
            whole(SMALL, D),
        ],
        out_specs=row_block(D),
        out_shape=kind(BF16, rows, length, D),
        cost_estimate=cost(8),
        compiler_params=params(),
    )(x, dmid, back, turned, small)


def output_kernel(counts_ref, mid_ref, hid_ref, small_ref, down_ref, out_ref):
    result = dot(hid_ref[0], down_ref[...], NN) + small_ref[16:17, :]
    valid = valid_tokens(counts_ref, mid_ref.shape[1])
    out_ref[0] = (valid * (mid_ref[0] + result)).astype(BF16)


def layer_output(counts, mid, hid, small, down):
    rows, length = mid.shape[0], mid.shape[1]
    return pl.pallas_call(
        output_kernel,
        grid_spec=pltpu.PrefetchScalarGridSpec(
            num_scalar_prefetch=1,
            grid=(rows, length // TB),
            in_specs=[row_block(D), row_block(FF), whole(SMALL, D), whole(FF, D)],
            out_specs=row_block(D),
        ),
        out_shape=kind(BF16, rows, length, D),
        cost_estimate=cost(9),
        compiler_params=params(),
    )(counts, mid, hid, small, down)


PLANES = 4
LANES = 8
ALL = PLANES * LANES
LATE_ROWS = 192


def move(value, pairs):
    return lax.ppermute(value, AXES, pairs)


def across(value, bits):
    return move(value, [(d, d ^ bits) for d in range(ALL)])


def by_plane(values, plane):
    out = values[-1]
    for z in range(len(values) - 1):
        out = jnp.where(plane == z, values[z], out)
    return out


def early_plane(mine):
    return 0 if mine else PLANES - 1


def late_planes(mine):
    return [z for z in range(PLANES) if z not in (mine, early_plane(mine))]


def core_spread(got):
    swapped = [across(part, 1) for part in got]
    return [part for both in zip(got, swapped) for part in both]


def gather_staged(plan, window, my_plane):
    got = [window]
    for s in range(1, PLANES):
        pairs = [(z * LANES + f, (z ^ s) * LANES + f) for z in range(PLANES) for f in range(LANES)]
        got.append(move(window, pairs))
    own = [window] + [across(window, bits) for bits in (2, 4, 6)]
    of = lambda f: by_plane([got[f(mine) ^ mine] for mine in range(PLANES)], my_plane)
    low = ROW_S - 16 * plan.first(ALL - 1)
    last = of(lambda mine: PLANES - 1)
    head = jnp.concatenate([of(early_plane), last[low : low + SMALL]], axis=0)
    rest = jnp.stack([of(lambda mine: late_planes(mine)[0]), of(lambda mine: late_planes(mine)[1])])
    head = [head] + [across(head, bits) for bits in (2, 4, 6)]
    ready = [rest, *own]
    rest = [rest] + [across(rest, bits) for bits in (2, 4)]
    diag = []
    for s in range(1, PLANES):
        pairs = [
            ((z ^ s) * LANES + f, z * LANES + f)
            for z in range(PLANES)
            if z ^ s in late_planes(z)
            for f in range(LANES)
        ]
        diag.append(move(own[3], pairs))
    spread = [core_spread(part) for part in (own, head, rest, diag)]
    return Gathered(plan, None, *spread), ready


def pack_start(pieces, sources, place_ref, ins, packed, sem):
    keep_ref, send_ref = packed
    for place in range(LANES):

        def start(place=place):
            for source, at, amount, plane, lane, to in pieces:
                if source not in sources:
                    continue
                out = send_ref if (lane ^ place) & 1 else keep_ref
                pltpu.make_async_copy(
                    ins[source].at[pl.ds(at, amount), :],
                    out.at[(lane ^ place) >> 1, plane, pl.ds(to, amount), :],
                    sem.at[(lane ^ place) & 1],
                ).start()

        pl.when(place_ref[0] == place)(start)


def pack_end(packed, sem):
    for i in range(2):
        pltpu.make_async_copy(packed[i], packed[i], sem.at[i]).wait()


def window_pieces(plan, windows, spans, extra):
    pieces = []
    for d in windows:
        plane, lane = divmod(d, LANES)
        plane = plane - windows[0] // LANES
        begin = 16 * plan.first(d)
        for source, (low, high) in enumerate(spans):
            a, b = max(begin, low), min(begin + plan.rows, high)
            if a < b:
                pieces.append((source, a - low, b - a, plane, lane, a - begin))
        end = spans[-1][1]
        if begin + plan.rows > end:
            left = begin + plan.rows - end
            pieces.append((len(spans) - 1, 0, left, plane, lane, plan.rows - left))
        if extra:
            pieces.append((len(spans), 0, SMALL, plane, lane, plan.rows))
    return pieces


def core_sum(keep, send):
    got = across(send, 1)
    return [(keep[p].astype(F32) + got[p].astype(F32)).astype(BF16) for p in range(LANES // 2)]


def plane_swap(parts):
    return [parts[0]] + [across(parts[p], 2 * p) for p in range(1, LANES // 2)]


def summed(parts):
    total = parts[0].astype(F32)
    for part in parts[1:]:
        total = total + part.astype(F32)
    return total.astype(BF16)


def main_picks(total, my_plane):
    owned = [total[0]] + [total[z] for z in range(PLANES - 1)]
    return [
        by_plane([owned[mine ^ s] for mine in range(PLANES)], my_plane) for s in range(PLANES)
    ]


def main_parts(picks):
    out = [picks[0]]
    for s in range(1, PLANES):
        pairs = [
            (z * LANES + f, (z ^ s) * LANES + f)
            for z in range(PLANES)
            if z ^ s
            for f in range(LANES)
        ]
        out.append(move(picks[s], pairs))
    return out


def head_parts(total):
    out = [total]
    last = PLANES - 1
    for s in range(1, PLANES):
        pairs = [(s * LANES + f, f) for f in range(LANES)]
        pairs.append(((s - 1) * LANES + LANES - 1, last * LANES + LANES - 1))
        out.append(move(total, pairs))
    return out


def owned_kernel(plan, at_ref, me_ref, *refs):
    main, head = refs[:PLANES], refs[PLANES : 2 * PLANES]
    out_ref, sum_ref, pad_ref = refs[2 * PLANES :]

    def add(parts, low, high):
        total = parts[0][low:high].astype(F32)
        for part in parts[1:]:
            total = total + part[low:high].astype(F32)
        return total

    @pl.when(me_ref[0] < LANES)
    def _():
        sum_ref[...] = add(head, 0, plan.rows)

    @pl.when(me_ref[0] >= LANES)
    def _():
        sum_ref[...] = add(main, 0, plan.rows)

    @pl.when(me_ref[0] == ALL - 1)
    def _():
        low = ROW_S - 16 * plan.first(ALL - 1)
        sum_ref[low : low + SMALL, :] = add(head, plan.rows, plan.rows + SMALL)

    for j in range(4):
        pad_ref[pl.ds(j, plan.rows, stride=4), :] = sum_ref[:, 128 * j : 128 * (j + 1)]
    out_ref[...] = pad_ref[pl.ds(at_ref[0], plan.lanes), :]


def take_owned(plan, at, me, main, head):
    out = pl.pallas_call(
        partial(owned_kernel, plan),
        grid_spec=pltpu.PrefetchScalarGridSpec(
            num_scalar_prefetch=2,
            grid=(1,),
            in_specs=[whole(plan.rows, D)] * PLANES + [whole(plan.rows + SMALL, D)] * PLANES,
            out_specs=whole(plan.lanes, 128),
            scratch_shapes=[
                pltpu.VMEM((plan.rows, D), F32),
                pltpu.VMEM((plan.rows * 4, 128), F32),
            ],
        ),
        out_shape=kind(F32, plan.lanes, 128),
        compiler_params=params(),
    )(at, me, *main, *head)
    return out.reshape(-1)


def plain_sum(plan, planes, lanes, me, at, ghead, gout, gup, gdown, glow):
    grads = jnp.concatenate([ghead, gout, gup, gdown, glow], axis=0)
    grads = jnp.pad(grads, ((0, plan.rows), (0, 0)))
    parts = jnp.stack([grads[16 * plan.first(d) :][: plan.rows] for d in range(plan.devices)])
    parts = parts.reshape(planes, lanes, plan.rows, D)
    parts = lax.psum_scatter(parts, "fsdp", scatter_dimension=1, tiled=True)
    parts = lax.psum_scatter(parts, "dp", scatter_dimension=0, tiled=True)
    flat = parts.reshape(-1).astype(F32)
    return lax.dynamic_slice(flat, (at[0] * 128,), (plan.lanes * 128,))


def local(planes, lanes, x, shard, segments, experts, counts, cot):
    plan = Plan(planes * lanes, shard.shape[0])
    my_plane, my_lane = lax.axis_index("dp"), lax.axis_index("fsdp")
    me = my_plane * lanes + my_lane
    place = jnp.stack([my_lane, my_plane]).astype(jnp.int32)
    at = ((plan.lanes * me) % 64).astype(jnp.int32).reshape(1)
    window = make_window(plan, at, shard)
    staged = (planes, lanes, plan.lanes) == (PLANES, LANES, 659)
    main_pieces, head_pieces = [], []
    first = place
    if staged:
        gathered, ready = gather_staged(plan, window, my_plane)
        first = after(place, *ready)
        main_pieces = window_pieces(
            plan, range(LANES, ALL), [(ROW_U, ROW_D), (ROW_D, ROW_S)], False
        )
        head_pieces = window_pieces(
            plan, range(LANES), [(0, ROW_O), (ROW_O, ROW_U), (ROW_U, ROW_U + LATE_ROWS)], True
        )
    else:
        gathered = Gathered(plan, lax.all_gather(window, AXES, axis=0))
    rows, length = x.shape[0], x.shape[1]
    places = jnp.arange(length, dtype=jnp.int32)[None, :]
    code = jnp.where(places < counts[:, None], segments, -1 - places)
    code = code.astype(F32).reshape(-1, 1, length)
    pairs = jnp.swapaxes(experts, 1, 2)
    state = attention_forward(plan, gathered, first, x, code, 0, None)
    turned, small = state[7:9]
    for row in range(1, rows):
        before = [*state[:7], turned, small]
        state = attention_forward(plan, gathered, place, x, code, row, before)
    q, k, v, h, prob, lse, att = state[:7]
    hid, mid, dmid, datt, dlog, inner, down, gout, gsmall, gup, gdown, *packed = feed_forward(
        plan, gathered, place, counts, x, cot, att, prob, pairs, small, main_pieces
    )
    third = place
    if staged:
        parts = core_sum(*packed)
        third = after(place, *parts)
        main = plane_swap(parts)
    back, ghead, glow, *packed = attention_backward(
        plan, third, x, h, q, k, v, lse, inner, datt, dlog, code, turned, gsmall, gout, gup, head_pieces
    )
    if not staged:
        grads = plain_sum(plan, planes, lanes, me, at, ghead, gout, gup, gdown, glow)
        output = layer_output(counts, mid, hid, small, down)
        return output, input_grad(x, dmid, back, turned, small), grads
    keep, send = (part[:, 0] for part in packed)
    main = summed(all_after(main, keep))
    picks = main_picks(main, my_plane)
    parts = core_sum(keep, send)
    grad_tokens = input_grad(x, dmid, after(back, *parts, *picks), turned, small)
    total = summed(all_after(plane_swap(parts), grad_tokens))
    output = layer_output(counts, after(mid, total), hid, small, down)
    me = me.astype(jnp.int32).reshape(1)
    owned = all_after([*main_parts(picks), *head_parts(total)], output)
    return output, grad_tokens, take_owned(plan, at, me, owned[:PLANES], owned[PLANES:])


def solution(mesh):
    spec = P(AXES)
    return jax.shard_map(
        partial(local, mesh.shape["dp"], mesh.shape["fsdp"]),
        mesh=mesh,
        in_specs=(spec,) * 6,
        out_specs=(spec,) * 3,
        check_vma=False,
    )
```

```python
from functools import partial

import jax
import jax.numpy as jnp
from jax import lax
from jax.experimental import pallas as pl
from jax.experimental.pallas import tpu as pltpu
from jax.sharding import PartitionSpec as P

D = 512
FF = 2048
EXPERTS = 8
HEAD = 64
EPS = 1e-05
NEG = -1e30
F32 = jnp.float32
BF16 = jnp.bfloat16
AXES = ("dp", "fsdp")

ROW_K = 512
ROW_V = 576
ROW_O = 640
ROW_U = 1152
ROW_D = 3200
ROW_S = 5248
SMALL = 32
ROWS_ALL = ROW_S + SMALL
T_R = 512
T_K = 528
T_V = 592
T_ALL = 656

QB = 128
KB = 256

NN = ((1,), (0,))
NT = ((1,), (1,))
TN = ((0,), (0,))

VMEM_MIB = 56


def dot(left, right, dims):
    return lax.dot_general(left, right, (dims, ((), ())), preferred_element_type=F32)


def cost(micros):
    return pl.CostEstimate(flops=int(micros * 1.1e9), bytes_accessed=int(micros * 1e5), transcendentals=0)


def after(value, *others):
    return lax.optimization_barrier((value, *others))[0]


def all_after(values, *others):
    return lax.optimization_barrier((*values, *others))[: len(values)]


def params(mib=VMEM_MIB):
    return pltpu.CompilerParams(vmem_limit_bytes=mib << 20)


def iota(shape, dim):
    return lax.broadcasted_iota(jnp.int32, shape, dim)


class Plan:
    def __init__(self, devices, shard):
        self.devices = devices
        self.lanes = shard // 128
        reach = max((self.lanes * d) % 64 for d in range(devices)) + self.lanes
        self.rows = -(-reach // 64) * 16

    def first(self, d):
        return (self.lanes * d) // 64

    def last(self, d):
        return (self.lanes * (d + 1) - 1) // 64


def window_kernel(plan, at_ref, shard_ref, out_ref, pad_ref):
    pad_ref[...] = jnp.zeros_like(pad_ref)
    pad_ref[64 : 64 + plan.lanes, :] = shard_ref[...]
    start = 64 - at_ref[0]
    for j in range(4):
        out_ref[:, 128 * j : 128 * (j + 1)] = pad_ref[
            pl.ds(start + j, plan.rows, stride=4), :
        ].astype(BF16)


def make_window(plan, at, shard):
    return pl.pallas_call(
        partial(window_kernel, plan),
        grid_spec=pltpu.PrefetchScalarGridSpec(
            num_scalar_prefetch=1,
            grid=(1,),
            in_specs=[pl.BlockSpec((plan.lanes, 128), lambda i, at: (0, 0))],
            out_specs=pl.BlockSpec((plan.rows, D), lambda i, at: (0, 0)),
            scratch_shapes=[pltpu.VMEM((plan.rows * 4 + 128, 128), F32)],
        ),
        out_shape=jax.ShapeDtypeStruct((plan.rows, D), BF16),
        compiler_params=params(),
    )(at, shard.reshape(plan.lanes, 128))


def row_pieces(plan, low, high):
    direct, shared = [], []
    for d in range(plan.devices):
        first, last = plan.first(d), plan.last(d)
        start = first
        if d > 0 and plan.last(d - 1) == first:
            start = first + 1
            if low <= first * 16 < high:
                shared.append((d, 0, first * 16 - low))
        begin, end = max(start * 16, low), min((last + 1) * 16, high)
        if begin < end:
            direct.append((d, begin - first * 16, begin - low, end - begin))
    return direct, shared


def start_rows(plan, source, low, high, dst_ref, tmp_ref, sem):
    direct, shared = row_pieces(plan, low, high)
    for d, at, to, amount in direct:
        pltpu.make_async_copy(
            source(d).at[pl.ds(at, amount), :], dst_ref.at[pl.ds(to, amount), :], sem.at[0]
        ).start()
    for slot, (d, at, _) in enumerate(shared):
        pltpu.make_async_copy(
            source(d).at[pl.ds(at, 16), :], tmp_ref.at[pl.ds(16 * slot, 16), :], sem.at[1]
        ).start()


def end_rows(plan, low, high, dst_ref, tmp_ref, sem):
    _, shared = row_pieces(plan, low, high)
    pltpu.make_async_copy(dst_ref, dst_ref, sem.at[0]).wait()
    if shared:
        part = tmp_ref.at[pl.ds(0, 16 * len(shared)), :]
        pltpu.make_async_copy(part, part, sem.at[1]).wait()
        for slot, (_, _, to) in enumerate(shared):
            dst_ref[to : to + 16, :] = (
                dst_ref[to : to + 16, :].astype(F32)
                + tmp_ref[16 * slot : 16 * slot + 16, :].astype(F32)
            ).astype(BF16)


def shared_rows(plan, low, high):
    return max(16, 16 * len(row_pieces(plan, low, high)[1]))


class Gathered:
    def __init__(self, plan, whole=None, own=(), head=(), rest=(), diag=()):
        self.plan, self.whole = plan, whole
        self.parts = [list(own), list(head), list(rest), list(diag)]
        self.small_at = ROW_S - 16 * plan.first(plan.devices - 1)

    def arrays(self, kinds):
        if self.whole is not None:
            return [self.whole]
        return [array for i in range(kinds) for array in self.parts[i]]

    def fetch(self, place_ref, refs, kinds, start):
        if self.whole is not None:
            last = self.plan.devices - 1
            start(lambda d: refs[0].at[d], refs[0].at[last, pl.ds(self.small_at, SMALL), :])
            return
        sets, at = [], 0
        for part in self.parts[:kinds]:
            sets.append(refs[at : at + len(part)])
            at += len(part)
        for mine in range(PLANES):
            for place in range(LANES):

                def source(d, mine=mine, place=place):
                    plane, lane = divmod(d, LANES)
                    lane = lane ^ place
                    if plane == mine:
                        return sets[0][lane]
                    if plane == early_plane(mine):
                        return sets[1][lane].at[pl.ds(0, self.plan.rows), :]
                    if lane < 6:
                        return sets[2][lane].at[late_planes(mine).index(plane)]
                    return sets[3][2 * ((plane ^ mine) - 1) + (lane & 1)]

                small = sets[1][(LANES - 1) ^ place].at[pl.ds(self.plan.rows, SMALL), :]
                here = (place_ref[0] == place) & (place_ref[1] == mine)
                pl.when(here)(partial(start, source, small))


def narrow_places():
    row, column = iota((D, D), 0), iota((D, D), 1)
    return (column == 8 * (row % 64) + row // 64).astype(BF16)


def narrow_transposed(flat):
    stacked = [
        jnp.concatenate([flat[64 * i : 64 * (i + 1), 64 * j : 64 * (j + 1)] for i in (0, 1)], axis=1)
        for j in range(8)
    ]
    return dot(jnp.concatenate(stacked, axis=0), narrow_places(), TN)


def narrow_flat(turned):
    stacked = dot(narrow_places(), turned, NT)
    return jnp.concatenate(
        [
            jnp.concatenate(
                [stacked[64 * j : 64 * (j + 1), 64 * i : 64 * (i + 1)] for j in range(8)], axis=1
            )
            for i in (0, 1)
        ],
        axis=0,
    )


def router_mask():
    return iota((64, D), 1) % 8 == iota((64, D), 0) % 8


def router_places():
    return (iota((D, 64), 0) // 8 == iota((D, 64), 1)).astype(BF16)


def router_transposed(flat):
    rows = jnp.concatenate([jnp.broadcast_to(flat[r : r + 1, :], (8, D)) for r in range(8)], axis=0)
    picked = dot(jnp.where(router_mask(), rows, 0.0).astype(BF16), router_places(), NN)
    return jnp.concatenate([picked[8 * r : 8 * (r + 1), :] for r in range(8)], axis=1)


def router_flat(turned):
    stacked = jnp.concatenate([turned[:, 64 * r : 64 * (r + 1)] for r in range(8)], axis=0)
    full = jnp.where(router_mask(), dot(stacked.astype(BF16), router_places(), NT), 0.0)
    return jnp.concatenate(
        [jnp.sum(full[8 * r : 8 * (r + 1)], axis=0, keepdims=True) for r in range(8)], axis=0
    )


def norm(source):
    center = source - jnp.mean(source, axis=-1, keepdims=True)
    scaler = lax.rsqrt(jnp.mean(center * center, axis=-1, keepdims=True) + EPS)
    return center * scaler, scaler


def norm_back(grad_normal, normal, scaler):
    return scaler * (
        grad_normal
        - jnp.mean(grad_normal, axis=-1, keepdims=True)
        - normal * jnp.mean(grad_normal * normal, axis=-1, keepdims=True)
    )


def two_heads(ref, pair, q0):
    return jnp.concatenate(
        [
            ref[0, 128 * pair : 128 * pair + 64, pl.ds(q0, QB)],
            ref[0, 128 * pair + 64 : 128 * pair + 128, pl.ds(q0, QB)],
        ],
        axis=1,
    )


def two_rows(ref, pair, q0):
    return jnp.concatenate(
        [ref[0, 2 * pair + half : 2 * pair + half + 1, pl.ds(q0, QB)] for half in (0, 1)], axis=1
    )


def block_bias(code_ref, column_ref, q0, w0):
    row = code_ref[0, :, pl.ds(q0, QB)]
    bias = jnp.where(column_ref[pl.ds(w0, KB), :] == row, 0.0, NEG)
    return jnp.concatenate([bias, bias], axis=1)


def set_columns(code_ref, column_ref):
    length = code_ref.shape[2]
    column_ref[...] = jnp.broadcast_to(code_ref[0], (QB, length)).T


def block_places(block, length):
    q0 = pl.multiple_of(block * QB, QB)
    w0 = pl.multiple_of(jnp.clip(q0 - 64, 0, length - KB), 64)
    return q0, w0


def forward_prepare(plan, gathered, place_ref, refs, turned_ref, small_ref, scratch):
    rows_ref, low_ref, tmp_ref, sem = scratch

    def start(source, small):
        start_rows(plan, source, 0, ROW_O, rows_ref, tmp_ref, sem)
        pltpu.make_async_copy(small, low_ref, sem.at[2]).start()

    gathered.fetch(place_ref, refs, 2, start)
    pltpu.make_async_copy(low_ref, low_ref, sem.at[2]).wait()
    end_rows(plan, 0, ROW_O, rows_ref, tmp_ref, sem)
    small_ref[...] = low_ref[...].astype(F32)
    turned_ref[0:D, :] = rows_ref[0:D, :].astype(F32).T.astype(BF16)
    turned_ref[T_R:T_K, :] = jnp.concatenate(
        [router_transposed(small_ref[0:8, :]), jnp.zeros((8, D), F32)], axis=0
    ).astype(BF16)
    turned_ref[T_K:T_ALL, :] = narrow_transposed(rows_ref[ROW_K:ROW_O, :]).astype(BF16)


def forward_row(x_ref, code_ref, turned_ref, small_ref, outs, column_ref):
    q_ref, k_ref, v_ref, h_ref, prob_ref, lse_ref, att_ref = outs
    length = x_ref.shape[1]
    set_columns(code_ref, column_ref)
    normal, _ = norm(x_ref[0].astype(F32))
    h = (normal * small_ref[12:13, :] + small_ref[13:14, :]).astype(BF16)
    h_ref[0] = h
    turned = dot(turned_ref[0:T_K, :], h, NT)
    q_ref[0] = turned[0:D].astype(BF16)
    logits = turned[T_R : T_R + 8]
    shifted = jnp.exp(logits - jnp.max(logits, axis=0, keepdims=True))
    prob_ref[0] = shifted / jnp.sum(shifted, axis=0, keepdims=True)
    kv = dot(h, turned_ref[T_K:T_ALL, :], NT).astype(BF16)
    k_ref[0] = kv[:, 0:HEAD]
    v_ref[0] = kv[:, HEAD:]

    def block_step(block, carry):
        q0, w0 = block_places(block, length)
        bias = block_bias(code_ref, column_ref, q0, w0)
        keys = k_ref[0, pl.ds(w0, KB), :]
        values = v_ref[0, pl.ds(w0, KB), :]
        pairs = range(EXPERTS // 2)
        scores = [dot(keys, two_heads(q_ref, pair, q0), NN) * (HEAD**-0.5) + bias for pair in pairs]
        peak = [jnp.max(part, axis=0, keepdims=True) for part in scores]
        expd = [jnp.exp(part - top) for part, top in zip(scores, peak)]
        summed = [jnp.sum(part, axis=0, keepdims=True) for part in expd]
        atts = [dot(values, part.astype(BF16), TN) for part in expd]
        for pair in pairs:
            att = atts[pair] * (1.0 / summed[pair])
            total = peak[pair] + jnp.log(summed[pair])
            for half in range(2):
                head, part = 2 * pair + half, slice(QB * half, QB * (half + 1))
                att_ref[0, 64 * head : 64 * (head + 1), pl.ds(q0, QB)] = att[:, part]
                lse_ref[0, head : head + 1, pl.ds(q0, QB)] = total[:, part]
        return carry

    lax.fori_loop(0, length // QB, block_step, 0, unroll=2)


def forward_first(plan, gathered, count, place_ref, x_ref, code_ref, *refs):
    wins, refs = refs[:count], refs[count:]
    outs, (turned_ref, small_ref), scratch = refs[:7], refs[7:9], refs[9:]
    forward_prepare(plan, gathered, place_ref, wins, turned_ref, small_ref, scratch[1:])
    forward_row(x_ref, code_ref, turned_ref, small_ref, outs, scratch[0])


def forward_next(place_ref, x_ref, code_ref, turned_ref, small_ref, *refs):
    forward_row(x_ref, code_ref, turned_ref, small_ref, refs[7:14], refs[14])


def attention_forward(plan, gathered, place, x, code, row, before):
    rows, length = x.shape[0], x.shape[1]
    row3 = lambda a, b: pl.BlockSpec((1, a, b), lambda *_: (row, 0, 0))
    sizes = [
        (D, length, BF16),
        (length, HEAD, BF16),
        (length, HEAD, BF16),
        (length, D, BF16),
        (8, length, F32),
        (8, length, F32),
        (D, length, F32),
    ]
    out_specs = [row3(a, b) for a, b, _ in sizes]
    out_shape = [kind(c, rows, a, b) for a, b, c in sizes]
    scratch = [pltpu.VMEM((length, QB), F32)]
    in_specs = [row3(length, D), row3(1, length)]
    if before is None:
        wins = gathered.arrays(2)
        kernel = partial(forward_first, plan, gathered, len(wins))
        operands = [place, x, code, *wins]
        in_specs = in_specs + [ANYWHERE] * len(wins)
        out_specs = out_specs + [whole(T_ALL, D), whole(SMALL, D)]
        out_shape = out_shape + [kind(BF16, T_ALL, D), kind(F32, SMALL, D)]
        scratch = scratch + [
            pltpu.VMEM((ROW_O, D), BF16),
            pltpu.VMEM((SMALL, D), BF16),
            pltpu.VMEM((shared_rows(plan, 0, ROW_O), D), BF16),
            pltpu.SemaphoreType.DMA((3,)),
        ]
        aliases = {}
    else:
        kernel = forward_next
        operands = [place, x, code, *before[7:9], *before[:7]]
        in_specs = in_specs + [whole(T_ALL, D), whole(SMALL, D)] + [ANYWHERE] * 7
        aliases = {5 + i: i for i in range(7)}
    return pl.pallas_call(
        kernel,
        grid_spec=pltpu.PrefetchScalarGridSpec(
            num_scalar_prefetch=1,
            grid=(1,),
            in_specs=in_specs,
            out_specs=out_specs,
            scratch_shapes=scratch,
        ),
        out_shape=out_shape,
        input_output_aliases=aliases,
        cost_estimate=cost(14),
        compiler_params=params(),
    )(*operands)


TB = 512


def chosen_experts(experts_ref, length):
    ids = iota((EXPERTS, length), 0)
    chosen = (experts_ref[0, 0:1, :] == ids) | (experts_ref[0, 1:2, :] == ids)
    return chosen.astype(F32)


def valid_tokens(counts_ref, amount):
    place = pl.program_id(1) * amount + iota((amount, 1), 0)
    return (place < counts_ref[pl.program_id(0)]).astype(F32)


def by_head(values, gate):
    return jnp.concatenate(
        [values[64 * e : 64 * (e + 1)] * gate[e : e + 1] for e in range(EXPERTS)], axis=0
    )


def gelu_parts(source):
    scale = (2.0 / jnp.pi) ** 0.5
    square = source * source
    share = 0.5 + 0.5 * jnp.tanh(source * (scale + (scale * 0.044715) * square))
    value = source * share
    slope = share + (value - value * share) * (2.0 * scale + (6.0 * scale * 0.044715) * square)
    return value, slope


def first_step():
    return (pl.program_id(0) == 0) & (pl.program_id(1) == 0)


def last_step():
    return (pl.program_id(0) == pl.num_programs(0) - 1) & (
        pl.program_id(1) == pl.num_programs(1) - 1
    )


def feed_kernel(plan, gathered, count, pieces, place_ref, counts_ref, *refs):
    x_ref, cot_ref, att_ref, prob_ref, experts_ref, small_ref = refs[:6]
    wins = refs[6 : 6 + count]
    hid_ref, mid_ref, dmid_ref, datt_ref, dlog_ref, inner_ref = refs[6 + count : 12 + count]
    down_ref, gout_ref, gsmall_ref, gup_ref, gdown_ref = refs[12 + count : 17 + count]
    packed, bias_ref = refs[17 + count : -13], refs[-13]
    rows_ref, up_ref, flat_ref, tmp_ref, tmp2_ref, wide_ref = refs[-12:-6]
    tdown_ref, tup_ref, tout_ref, sem, sem2, pack_sem = refs[-6:]

    @pl.when(first_step())
    def _():
        def start(source, small):
            start_rows(plan, source, ROW_O, ROW_D, rows_ref, tmp_ref, sem)
            start_rows(plan, source, ROW_D, ROW_S, down_ref, tmp2_ref, sem2)

        gathered.fetch(place_ref, wins, 4, start)
        for ref in (tdown_ref, tup_ref, tout_ref, gsmall_ref):
            ref[...] = jnp.zeros_like(ref)
        end_rows(plan, ROW_O, ROW_D, rows_ref, tmp_ref, sem)
        for c in range(4):
            wide_ref[c] = rows_ref[D:, 128 * c : 128 * (c + 1)].astype(F32)
            for j in range(4):
                up_ref[:, D * j + 128 * c : D * j + 128 * (c + 1)] = wide_ref[
                    c, pl.ds(j, D, stride=4), :
                ].astype(BF16)
        end_rows(plan, ROW_D, ROW_S, down_ref, tmp2_ref, sem2)

    amount = x_ref.shape[1]
    prob = prob_ref[0]
    chosen = chosen_experts(experts_ref, amount)
    gate = prob * chosen
    att = att_ref[0]
    mixed = by_head(att, gate).astype(BF16)
    middle = x_ref[0].astype(F32) + dot(mixed, rows_ref[0:D, :], TN)
    mid_ref[0] = middle
    normal, scaler = norm(middle)
    gain = small_ref[14:15, :]
    h = (normal * gain + small_ref[15:16, :]).astype(BF16)
    grad = valid_tokens(counts_ref, amount) * cot_ref[0].astype(F32)
    grad_low = grad.astype(BF16)
    parts = [slice(2 * D * j, 2 * D * (j + 1)) for j in range(2)]
    dhid = [dot(grad_low, down_ref[part, :], NT) for part in parts]
    back = jnp.zeros((amount, D), F32)
    for j, part in enumerate(parts):
        bias = jnp.concatenate([small_ref[8 + i : 9 + i, :] for i in (2 * j, 2 * j + 1)], axis=1)
        value, slope = gelu_parts(dot(h, up_ref[:, part], NN) + bias)
        value = value.astype(BF16)
        hid_ref[0, :, part] = value
        pre = slope * dhid[j]
        sums = jnp.sum(pre, axis=0, keepdims=True)
        for i in range(2):
            gsmall_ref[2 * j + i : 2 * j + i + 1, :] += sums[:, D * i : D * (i + 1)]
        pre = pre.astype(BF16)
        tdown_ref[part, :] += dot(value, grad_low, TN)
        tup_ref[:, part] += dot(h, pre, TN)
        back = back + dot(pre, up_ref[:, part], NT)
    gsmall_ref[4:5, :] += jnp.sum(back * normal, axis=0, keepdims=True)
    gsmall_ref[5:6, :] += jnp.sum(back, axis=0, keepdims=True)
    gsmall_ref[6:7, :] += jnp.sum(grad, axis=0, keepdims=True)
    dmid = grad + norm_back(back * gain, normal, scaler)
    dmid_ref[0] = dmid
    branch = dmid.astype(BF16)
    tout_ref[...] += dot(mixed, branch, NN)
    dmixed = dot(rows_ref[0:D, :], branch, NT)
    dgate = jnp.concatenate(
        [
            jnp.sum(
                dmixed[64 * e : 64 * (e + 1)] * att[64 * e : 64 * (e + 1)], axis=0, keepdims=True
            )
            for e in range(EXPERTS)
        ],
        axis=0,
    )
    datt_ref[0] = by_head(dmixed, gate).astype(BF16)
    inner_ref[0] = gate * dgate
    dprob = dgate * chosen
    dlog = prob * (dprob - jnp.sum(prob * dprob, axis=0, keepdims=True))
    dlog_ref[0] = jnp.concatenate([dlog, jnp.zeros_like(dlog)], axis=0).astype(BF16)

    @pl.when(last_step())
    def _():
        gdown_ref[...] = tdown_ref[...].astype(BF16)
        bias_ref[...] = jnp.concatenate([gsmall_ref[6:7, :], jnp.zeros((15, D), F32)]).astype(BF16)
        ins = [flat_ref, gdown_ref, bias_ref]
        if pieces:
            pack_start(pieces, [1, 2], place_ref, ins, packed, pack_sem)
        gout_ref[...] = tout_ref[...].astype(BF16)
        for c in range(4):
            for j in range(4):
                wide_ref[c, pl.ds(j, D, stride=4), :] = tup_ref[
                    :, D * j + 128 * c : D * j + 128 * (c + 1)
                ]
            flat_ref[:, 128 * c : 128 * (c + 1)] = wide_ref[c].astype(BF16)
        gup_ref[...] = flat_ref[0 : gup_ref.shape[0], :]
        if pieces:
            pack_start(pieces, [0], place_ref, ins, packed, pack_sem)
            pack_end(packed, pack_sem)


def row_block(*tail):
    return pl.BlockSpec((1, TB, *tail), lambda i, j, *_: (i, j, 0))


def column_block(height):
    return pl.BlockSpec((1, height, TB), lambda i, j, *_: (i, 0, j))


def whole(*shape):
    return pl.BlockSpec(shape, lambda *_: (0,) * len(shape))


ANYWHERE = pl.BlockSpec(memory_space=pl.ANY)


def kind(dtype, *shape):
    return jax.ShapeDtypeStruct(shape, dtype)


def feed_forward(plan, gathered, place, counts, x, cot, att, prob, experts, small, pieces):
    rows, length = x.shape[0], x.shape[1]
    wins = gathered.arrays(4)
    head = LATE_ROWS if pieces else FF
    packed = [kind(BF16, LANES // 2, PLANES - 1, plan.rows, D)] * 2 if pieces else []
    return pl.pallas_call(
        partial(feed_kernel, plan, gathered, len(wins), pieces),
        grid_spec=pltpu.PrefetchScalarGridSpec(
            num_scalar_prefetch=2,
            grid=(rows, length // TB),
            in_specs=[
                row_block(D),
                row_block(D),
                column_block(D),
                column_block(8),
                column_block(2),
                whole(SMALL, D),
            ]
            + [ANYWHERE] * len(wins),
            out_specs=[
                row_block(FF),
                row_block(D),
                row_block(D),
                column_block(D),
                column_block(16),
                column_block(8),
                whole(FF, D),
                whole(D, D),
                whole(8, D),
                whole(head, D),
                whole(FF, D),
            ]
            + [ANYWHERE] * len(packed),
            scratch_shapes=[
                pltpu.VMEM((16, D), BF16),
                pltpu.VMEM((ROW_D - ROW_O, D), BF16),
                pltpu.VMEM((D, FF), BF16),
                pltpu.VMEM((FF, D), BF16),
                pltpu.VMEM((shared_rows(plan, ROW_O, ROW_D), D), BF16),
                pltpu.VMEM((shared_rows(plan, ROW_D, ROW_S), D), BF16),
                pltpu.VMEM((4, FF, 128), F32),
                pltpu.VMEM((FF, D), F32),
                pltpu.VMEM((D, FF), F32),
                pltpu.VMEM((D, D), F32),
                pltpu.SemaphoreType.DMA((2,)),
                pltpu.SemaphoreType.DMA((2,)),
                pltpu.SemaphoreType.DMA((2,)),
            ],
        ),
        out_shape=[
            kind(BF16, rows, length, FF),
            kind(F32, rows, length, D),
            kind(F32, rows, length, D),
            kind(BF16, rows, D, length),
            kind(BF16, rows, 16, length),
            kind(F32, rows, 8, length),
            kind(BF16, FF, D),
            kind(BF16, D, D),
            kind(F32, 8, D),
            kind(BF16, head, D),
            kind(BF16, FF, D),
        ]
        + packed,
        cost_estimate=cost(50),
        compiler_params=params(60),
    )(place, counts, x, cot, att, prob, experts, small, *wins)


def backward_kernel(pieces, place_ref, *refs):
    x_ref, h_ref, q_ref, k_ref, v_ref, lse_ref, inner_ref, datt_ref, dlog_ref, code_ref = refs[:10]
    turned_ref, gsmall_ref, gout_ref, gup_ref = refs[10:14]
    back_ref, ghead_ref, glow_ref = refs[14:17]
    packed = refs[17:-7]
    dk_ref, dv_ref, column_ref, total_ref, gain_ref, shift_ref, pack_sem = refs[-7:]
    length = x_ref.shape[1]

    @pl.when(pl.program_id(0) == 0)
    def _():
        total_ref[...] = jnp.zeros_like(total_ref)
        gain_ref[...] = jnp.zeros_like(gain_ref)
        shift_ref[...] = jnp.zeros_like(shift_ref)

    set_columns(code_ref, column_ref)
    dk_ref[...] = jnp.zeros_like(dk_ref)
    dv_ref[...] = jnp.zeros_like(dv_ref)

    def block_step(block, carry):
        q0, w0 = block_places(block, length)
        bias = block_bias(code_ref, column_ref, q0, w0)
        keys = k_ref[0, pl.ds(w0, KB), :]
        values = v_ref[0, pl.ds(w0, KB), :]
        pairs = range(EXPERTS // 2)
        queries = [two_heads(q_ref, pair, q0) for pair in pairs]
        datt = [two_heads(datt_ref, pair, q0) for pair in pairs]
        soft = [
            jnp.exp(dot(keys, part, NN) * (HEAD**-0.5) + bias - two_rows(lse_ref, pair, q0))
            for pair, part in enumerate(queries)
        ]
        dscores = [
            (soft[pair] * (dot(values, part, NN) - two_rows(inner_ref, pair, q0))).astype(BF16)
            for pair, part in enumerate(datt)
        ]
        soft = jnp.concatenate([part.astype(BF16) for part in soft], axis=1)
        dv = dot(soft, jnp.concatenate(datt, axis=1), NT)
        dk = dot(jnp.concatenate(dscores, axis=1), jnp.concatenate(queries, axis=1), NT)
        for pair in pairs:
            dq = (dot(keys, dscores[pair], TN) * (HEAD**-0.5)).astype(BF16)
            for half in range(2):
                head, part = 2 * pair + half, slice(QB * half, QB * (half + 1))
                back_ref[0, 64 * head : 64 * (head + 1), pl.ds(q0, QB)] = dq[:, part]
        dk_ref[pl.ds(w0, KB), :] += dk * (HEAD**-0.5)
        dv_ref[pl.ds(w0, KB), :] += dv
        return carry

    lax.fori_loop(0, length // QB, block_step, 0, unroll=2)
    back_ref[0, T_R:T_K, :] = dlog_ref[0]
    back_ref[0, T_K:T_V, :] = dk_ref[...].T.astype(BF16)
    back_ref[0, T_V:T_ALL, :] = dv_ref[...].T.astype(BF16)
    normal, _ = norm(x_ref[0].astype(F32))
    back = back_ref[0]
    total_ref[...] += dot(back, h_ref[0], NN)
    gain_ref[...] += dot(back, normal.astype(BF16), NN)
    shift_ref[...] += jnp.sum(back.astype(F32), axis=1, keepdims=True)

    @pl.when(pl.program_id(0) == pl.num_programs(0) - 1)
    def _():
        ghead_ref[0:D, :] = total_ref[0:D, :].T.astype(BF16)
        ghead_ref[D:ROW_O, :] = narrow_flat(total_ref[T_K:T_ALL, :].astype(BF16)).astype(BF16)
        turned = turned_ref[...].astype(F32)
        glow_ref[...] = jnp.concatenate(
            [
                router_flat(total_ref[T_R : T_R + 8, :]),
                gsmall_ref[0:4, :],
                jnp.sum(turned * gain_ref[...], axis=0, keepdims=True),
                jnp.sum(turned * shift_ref[...], axis=0, keepdims=True),
                gsmall_ref[4:7, :],
                jnp.zeros((SMALL - 17, D), F32),
            ],
            axis=0,
        ).astype(BF16)
        if pieces:
            ins = [ghead_ref, gout_ref, gup_ref, glow_ref]
            pack_start(pieces, range(4), place_ref, ins, packed, pack_sem)
            pack_end(packed, pack_sem)


def attention_backward(
    plan, place, x, h, q, k, v, lse, inner, datt, dlog, code, turned, gsmall, gout, gup, pieces
):
    rows, length = x.shape[0], x.shape[1]
    row3 = lambda a, b: pl.BlockSpec((1, a, b), lambda i, *_: (i, 0, 0))
    packed = [kind(BF16, LANES // 2, 1, plan.rows, D)] * 2 if pieces else []
    head = min(LATE_ROWS, gup.shape[0])
    return pl.pallas_call(
        partial(backward_kernel, pieces),
        grid_spec=pltpu.PrefetchScalarGridSpec(
            num_scalar_prefetch=1,
            grid=(rows,),
            in_specs=[
                row3(length, D),
                row3(length, D),
                row3(D, length),
                row3(length, HEAD),
                row3(length, HEAD),
                row3(8, length),
                row3(8, length),
                row3(D, length),
                row3(16, length),
                row3(1, length),
                whole(T_ALL, D),
                whole(8, D),
                whole(D, D),
                whole(head, D),
            ],
            out_specs=[row3(T_ALL, length), whole(ROW_O, D), whole(SMALL, D)]
            + [ANYWHERE] * len(packed),
            scratch_shapes=[
                pltpu.VMEM((length, HEAD), F32),
                pltpu.VMEM((length, HEAD), F32),
                pltpu.VMEM((length, QB), F32),
                pltpu.VMEM((T_ALL, D), F32),
                pltpu.VMEM((T_ALL, D), F32),
                pltpu.VMEM((T_ALL, 1), F32),
                pltpu.SemaphoreType.DMA((2,)),
            ],
        ),
        out_shape=[
            kind(BF16, rows, T_ALL, length),
            kind(BF16, ROW_O, D),
            kind(BF16, SMALL, D),
        ]
        + packed,
        cost_estimate=cost(33),
        compiler_params=params(),
    )(place, x, h, q, k, v, lse, inner, datt, dlog, code, turned, gsmall, gout, gup)


def input_kernel(x_ref, dmid_ref, back_ref, turned_ref, small_ref, gx_ref):
    normal, scaler = norm(x_ref[0].astype(F32))
    back = dot(back_ref[0], turned_ref[...], TN) * small_ref[12:13, :]
    gx_ref[0] = (dmid_ref[0] + norm_back(back, normal, scaler)).astype(BF16)


def input_grad(x, dmid, back, turned, small):
    rows, length = x.shape[0], x.shape[1]
    return pl.pallas_call(
        input_kernel,
        grid=(rows, length // TB),
        in_specs=[
            row_block(D),
            row_block(D),
            column_block(T_ALL),
            whole(T_ALL, D),
            whole(SMALL, D),
        ],
        out_specs=row_block(D),
        out_shape=kind(BF16, rows, length, D),
        cost_estimate=cost(8),
        compiler_params=params(),
    )(x, dmid, back, turned, small)


def output_kernel(counts_ref, mid_ref, hid_ref, small_ref, down_ref, out_ref):
    result = dot(hid_ref[0], down_ref[...], NN) + small_ref[16:17, :]
    valid = valid_tokens(counts_ref, mid_ref.shape[1])
    out_ref[0] = (valid * (mid_ref[0] + result)).astype(BF16)


def layer_output(counts, mid, hid, small, down):
    rows, length = mid.shape[0], mid.shape[1]
    return pl.pallas_call(
        output_kernel,
        grid_spec=pltpu.PrefetchScalarGridSpec(
            num_scalar_prefetch=1,
            grid=(rows, length // TB),
            in_specs=[row_block(D), row_block(FF), whole(SMALL, D), whole(FF, D)],
            out_specs=row_block(D),
        ),
        out_shape=kind(BF16, rows, length, D),
        cost_estimate=cost(9),
        compiler_params=params(),
    )(counts, mid, hid, small, down)


PLANES = 4
LANES = 8
ALL = PLANES * LANES
LATE_ROWS = 192


def move(value, pairs):
    return lax.ppermute(value, AXES, pairs)


def across(value, bits):
    return move(value, [(d, d ^ bits) for d in range(ALL)])


def by_plane(values, plane):
    out = values[-1]
    for z in range(len(values) - 1):
        out = jnp.where(plane == z, values[z], out)
    return out


def early_plane(mine):
    return 0 if mine else PLANES - 1


def late_planes(mine):
    return [z for z in range(PLANES) if z not in (mine, early_plane(mine))]


def core_spread(got):
    swapped = [across(part, 1) for part in got]
    return [part for both in zip(got, swapped) for part in both]


def gather_staged(plan, window, my_plane):
    got = [window]
    for s in range(1, PLANES):
        pairs = [(z * LANES + f, (z ^ s) * LANES + f) for z in range(PLANES) for f in range(LANES)]
        got.append(move(window, pairs))
    own = [window] + [across(window, bits) for bits in (2, 4, 6)]
    got[1:], corner = all_after(got[1:], own[3]), own[3]
    of = lambda f: by_plane([got[f(mine) ^ mine] for mine in range(PLANES)], my_plane)
    low = ROW_S - 16 * plan.first(ALL - 1)
    last = of(lambda mine: PLANES - 1)
    head = jnp.concatenate([of(early_plane), last[low : low + SMALL]], axis=0)
    rest = jnp.stack([of(lambda mine: late_planes(mine)[0]), of(lambda mine: late_planes(mine)[1])])
    head = [head] + [across(head, bits) for bits in (2, 4, 6)]
    ready = [rest]
    rest = [rest] + [across(rest, bits) for bits in (2, 4)]
    diag = []
    for s in range(1, PLANES):
        pairs = [
            ((z ^ s) * LANES + f, z * LANES + f)
            for z in range(PLANES)
            if z ^ s in late_planes(z)
            for f in range(LANES)
        ]
        diag.append(move(corner, pairs))
    ready += diag[:1]
    spread = [core_spread(part) for part in (own, head, rest, diag)]
    return Gathered(plan, None, *spread), ready


def pack_start(pieces, sources, place_ref, ins, packed, sem):
    keep_ref, send_ref = packed
    for place in range(LANES):

        def start(place=place):
            for source, at, amount, plane, lane, to in pieces:
                if source not in sources:
                    continue
                out = send_ref if (lane ^ place) & 1 else keep_ref
                pltpu.make_async_copy(
                    ins[source].at[pl.ds(at, amount), :],
                    out.at[(lane ^ place) >> 1, plane, pl.ds(to, amount), :],
                    sem.at[(lane ^ place) & 1],
                ).start()

        pl.when(place_ref[0] == place)(start)


def pack_end(packed, sem):
    for i in range(2):
        pltpu.make_async_copy(packed[i], packed[i], sem.at[i]).wait()


SMALL_AT = 176


def window_pieces(plan, windows, spans, small):
    pieces = []
    for d in windows:
        plane, lane = divmod(d, LANES)
        plane = plane - windows[0] // LANES
        begin, size = 16 * plan.first(d), plan.rows
        if small and lane == LANES - 1:
            size = SMALL_AT
            pieces.append((len(spans), 0, 16, plane, lane, SMALL_AT))
        done = begin
        for source, (low, high) in enumerate(spans + [(begin + size, begin + size)]):
            a, b = max(begin, low), min(begin + size, high)
            if a > done and a >= high or a < b and a > done:
                pieces.append((0, 0, a - done, plane, lane, done - begin))
            if a < b:
                pieces.append((source, a - low, b - a, plane, lane, a - begin))
            done = max(done, min(max(a, b), begin + size))
    for d in windows:
        plane, lane = divmod(d, LANES)
        plane = plane - windows[0] // LANES
        rows = sorted((p[5], p[5] + p[2]) for p in pieces if p[3:5] == (plane, lane))
        assert rows[0][0] == 0 and rows[-1][1] == plan.rows
        assert all(x[1] == y[0] for x, y in zip(rows, rows[1:]))
    return pieces


def core_sum(keep, send):
    got = across(send, 1)
    return [(keep[p].astype(F32) + got[p].astype(F32)).astype(BF16) for p in range(LANES // 2)]


def plane_swap(parts):
    return [parts[0]] + [across(parts[p], 2 * p) for p in range(1, LANES // 2)]


def summed(parts):
    total = parts[0].astype(F32)
    for part in parts[1:]:
        total = total + part.astype(F32)
    return total.astype(BF16)


def main_picks(total, my_plane):
    owned = [total[0]] + [total[z] for z in range(PLANES - 1)]
    return [
        by_plane([owned[mine ^ s] for mine in range(PLANES)], my_plane) for s in range(PLANES)
    ]


def to_planes(picks):
    out = [picks[0]]
    for s in range(1, PLANES):
        pairs = [
            (z * LANES + f, (z ^ s) * LANES + f)
            for z in range(PLANES)
            if z ^ s
            for f in range(LANES)
        ]
        out.append(move(picks[s], pairs))
    return out


def head_parts(total):
    out = [total]
    last = PLANES - 1
    for s in range(1, PLANES):
        pairs = [(s * LANES + f, f) for f in range(LANES)]
        pairs.append(((s - 1) * LANES + LANES - 1, last * LANES + LANES - 1))
        out.append(move(total, pairs))
    return out


def owned_kernel(plan, at_ref, me_ref, *refs):
    main, head = refs[:PLANES], refs[PLANES : 2 * PLANES]
    out_ref, sum_ref, pad_ref = refs[2 * PLANES :]

    def add(parts, low, high):
        total = parts[0][low:high].astype(F32)
        for part in parts[1:]:
            total = total + part[low:high].astype(F32)
        return total

    @pl.when(me_ref[0] < LANES)
    def _():
        sum_ref[...] = add(head, 0, plan.rows)

    @pl.when(me_ref[0] >= LANES)
    def _():
        sum_ref[...] = add(main, 0, plan.rows)

    @pl.when(me_ref[0] == ALL - 1)
    def _():
        low = ROW_S - 16 * plan.first(ALL - 1)
        sum_ref[low : low + 16, :] = add(head, SMALL_AT, SMALL_AT + 16)

    for j in range(4):
        pad_ref[pl.ds(j, plan.rows, stride=4), :] = sum_ref[:, 128 * j : 128 * (j + 1)]
    out_ref[...] = pad_ref[pl.ds(at_ref[0], plan.lanes), :]


def take_owned(plan, at, me, main, head):
    out = pl.pallas_call(
        partial(owned_kernel, plan),
        grid_spec=pltpu.PrefetchScalarGridSpec(
            num_scalar_prefetch=2,
            grid=(1,),
            in_specs=[whole(plan.rows, D)] * (2 * PLANES),
            out_specs=whole(plan.lanes, 128),
            scratch_shapes=[
                pltpu.VMEM((plan.rows, D), F32),
                pltpu.VMEM((plan.rows * 4, 128), F32),
            ],
        ),
        out_shape=kind(F32, plan.lanes, 128),
        compiler_params=params(),
    )(at, me, *main, *head)
    return out.reshape(-1)


def plain_sum(plan, planes, lanes, me, at, ghead, gout, gup, gdown, glow):
    grads = jnp.concatenate([ghead, gout, gup, gdown, glow], axis=0)
    grads = jnp.pad(grads, ((0, plan.rows), (0, 0)))
    parts = jnp.stack([grads[16 * plan.first(d) :][: plan.rows] for d in range(plan.devices)])
    parts = parts.reshape(planes, lanes, plan.rows, D)
    parts = lax.psum_scatter(parts, "fsdp", scatter_dimension=1, tiled=True)
    parts = lax.psum_scatter(parts, "dp", scatter_dimension=0, tiled=True)
    flat = parts.reshape(-1).astype(F32)
    return lax.dynamic_slice(flat, (at[0] * 128,), (plan.lanes * 128,))


def local(planes, lanes, x, shard, segments, experts, counts, cot):
    plan = Plan(planes * lanes, shard.shape[0])
    my_plane, my_lane = lax.axis_index("dp"), lax.axis_index("fsdp")
    me = my_plane * lanes + my_lane
    place = jnp.stack([my_lane, my_plane]).astype(jnp.int32)
    at = ((plan.lanes * me) % 64).astype(jnp.int32).reshape(1)
    window = make_window(plan, at, shard)
    staged = (planes, lanes, plan.lanes) == (PLANES, LANES, 659)
    main_pieces, head_pieces = [], []
    first = place
    if staged:
        gathered, ready = gather_staged(plan, window, my_plane)
        first = after(place, *ready)
        main_pieces = window_pieces(
            plan, range(LANES, ALL), [(ROW_U, ROW_D), (ROW_D, ROW_S), (ROW_S + 16, ROWS_ALL)], False
        )
        head_pieces = window_pieces(
            plan, range(LANES), [(0, ROW_O), (ROW_O, ROW_U), (ROW_U, ROW_U + LATE_ROWS)], True
        )
    else:
        gathered = Gathered(plan, lax.all_gather(window, AXES, axis=0))
    rows, length = x.shape[0], x.shape[1]
    places = jnp.arange(length, dtype=jnp.int32)[None, :]
    code = jnp.where(places < counts[:, None], segments, -1 - places)
    code = code.astype(F32).reshape(-1, 1, length)
    pairs = jnp.swapaxes(experts, 1, 2)
    state = attention_forward(plan, gathered, first, x, code, 0, None)
    turned, small = state[7:9]
    for row in range(1, rows):
        before = [*state[:7], turned, small]
        state = attention_forward(plan, gathered, place, x, code, row, before)
    q, k, v, h, prob, lse, att = state[:7]
    hid, mid, dmid, datt, dlog, inner, down, gout, gsmall, gup, gdown, *packed = feed_forward(
        plan, gathered, place, counts, x, cot, att, prob, pairs, small, main_pieces
    )
    third = place
    if staged:
        parts = core_sum(*packed)
        third = after(place, *parts)
        main = plane_swap(parts)
    back, ghead, glow, *packed = attention_backward(
        plan, third, x, h, q, k, v, lse, inner, datt, dlog, code, turned, gsmall, gout, gup, head_pieces
    )
    if not staged:
        grads = plain_sum(plan, planes, lanes, me, at, ghead, gout, gup, gdown, glow)
        output = layer_output(counts, mid, hid, small, down)
        return output, input_grad(x, dmid, back, turned, small), grads
    keep, send = (part[:, 0] for part in packed)
    main = summed(all_after(main, keep))
    picks = main_picks(main, my_plane)
    parts = core_sum(keep, send)
    grad_tokens = input_grad(x, dmid, after(back, *parts, *picks), turned, small)
    total = summed(all_after(plane_swap(parts), grad_tokens))
    output = layer_output(counts, after(mid, total), hid, small, down)
    me = me.astype(jnp.int32).reshape(1)
    owned = all_after([*to_planes(picks), *head_parts(total)], output)
    return output, grad_tokens, take_owned(plan, at, me, owned[:PLANES], owned[PLANES:])


def solution(mesh):
    spec = P(AXES)
    return jax.shard_map(
        partial(local, mesh.shape["dp"], mesh.shape["fsdp"]),
        mesh=mesh,
        in_specs=(spec,) * 6,
        out_specs=(spec,) * 3,
        check_vma=False,
    )
```

```python
from functools import partial

import jax
import jax.numpy as jnp
from jax import lax
from jax.experimental import pallas as pl
from jax.experimental.pallas import tpu as pltpu
from jax.sharding import PartitionSpec as P

D = 512
FF = 2048
EXPERTS = 8
HEAD = 64
EPS = 1e-05
NEG = -1e30
F32 = jnp.float32
BF16 = jnp.bfloat16
AXES = ("dp", "fsdp")

ROW_K = 512
ROW_V = 576
ROW_O = 640
ROW_U = 1152
ROW_D = 3200
ROW_S = 5248
SMALL = 32
ROWS_ALL = ROW_S + SMALL
T_R = 512
T_K = 528
T_V = 592
T_ALL = 656

QB = 128
KB = 256

NN = ((1,), (0,))
NT = ((1,), (1,))
TN = ((0,), (0,))

VMEM_MIB = 56


def dot(left, right, dims):
    return lax.dot_general(left, right, (dims, ((), ())), preferred_element_type=F32)


def cost(micros):
    return pl.CostEstimate(flops=int(micros * 1.1e9), bytes_accessed=int(micros * 1e5), transcendentals=0)


def after(value, *others):
    return lax.optimization_barrier((value, *others))[0]


def all_after(values, *others):
    return lax.optimization_barrier((*values, *others))[: len(values)]


def params(mib=VMEM_MIB):
    return pltpu.CompilerParams(vmem_limit_bytes=mib << 20)


def iota(shape, dim):
    return lax.broadcasted_iota(jnp.int32, shape, dim)


class Plan:
    def __init__(self, devices, shard):
        self.devices = devices
        self.lanes = shard // 128
        reach = max((self.lanes * d) % 64 for d in range(devices)) + self.lanes
        self.rows = -(-reach // 64) * 16

    def first(self, d):
        return (self.lanes * d) // 64

    def last(self, d):
        return (self.lanes * (d + 1) - 1) // 64


def window_kernel(plan, at_ref, shard_ref, out_ref, pad_ref):
    pad_ref[...] = jnp.zeros_like(pad_ref)
    pad_ref[64 : 64 + plan.lanes, :] = shard_ref[...]
    start = 64 - at_ref[0]
    for j in range(4):
        out_ref[:, 128 * j : 128 * (j + 1)] = pad_ref[
            pl.ds(start + j, plan.rows, stride=4), :
        ].astype(BF16)


def make_window(plan, at, shard):
    return pl.pallas_call(
        partial(window_kernel, plan),
        grid_spec=pltpu.PrefetchScalarGridSpec(
            num_scalar_prefetch=1,
            grid=(1,),
            in_specs=[pl.BlockSpec((plan.lanes, 128), lambda i, at: (0, 0))],
            out_specs=pl.BlockSpec((plan.rows, D), lambda i, at: (0, 0)),
            scratch_shapes=[pltpu.VMEM((plan.rows * 4 + 128, 128), F32)],
        ),
        out_shape=jax.ShapeDtypeStruct((plan.rows, D), BF16),
        compiler_params=params(),
    )(at, shard.reshape(plan.lanes, 128))


def row_pieces(plan, low, high):
    direct, shared = [], []
    for d in range(plan.devices):
        first, last = plan.first(d), plan.last(d)
        start = first
        if d > 0 and plan.last(d - 1) == first:
            start = first + 1
            if low <= first * 16 < high:
                shared.append((d, 0, first * 16 - low))
        begin, end = max(start * 16, low), min((last + 1) * 16, high)
        if begin < end:
            direct.append((d, begin - first * 16, begin - low, end - begin))
    return direct, shared


def start_rows(plan, source, low, high, dst_ref, tmp_ref, sem):
    direct, shared = row_pieces(plan, low, high)
    for d, at, to, amount in direct:
        pltpu.make_async_copy(
            source(d).at[pl.ds(at, amount), :], dst_ref.at[pl.ds(to, amount), :], sem.at[0]
        ).start()
    for slot, (d, at, _) in enumerate(shared):
        pltpu.make_async_copy(
            source(d).at[pl.ds(at, 16), :], tmp_ref.at[pl.ds(16 * slot, 16), :], sem.at[1]
        ).start()


def end_rows(plan, low, high, dst_ref, tmp_ref, sem):
    _, shared = row_pieces(plan, low, high)
    pltpu.make_async_copy(dst_ref, dst_ref, sem.at[0]).wait()
    if shared:
        part = tmp_ref.at[pl.ds(0, 16 * len(shared)), :]
        pltpu.make_async_copy(part, part, sem.at[1]).wait()
        for slot, (_, _, to) in enumerate(shared):
            dst_ref[to : to + 16, :] = (
                dst_ref[to : to + 16, :].astype(F32)
                + tmp_ref[16 * slot : 16 * slot + 16, :].astype(F32)
            ).astype(BF16)


def shared_rows(plan, low, high):
    return max(16, 16 * len(row_pieces(plan, low, high)[1]))


class Gathered:
    def __init__(self, plan, whole=None, own=(), head=(), rest=(), diag=()):
        self.plan, self.whole = plan, whole
        self.parts = [list(own), list(head), list(rest), list(diag)]
        self.small_at = ROW_S - 16 * plan.first(plan.devices - 1)

    def arrays(self, kinds):
        if self.whole is not None:
            return [self.whole]
        return [array for i in range(kinds) for array in self.parts[i]]

    def fetch(self, place_ref, refs, kinds, start):
        if self.whole is not None:
            last = self.plan.devices - 1
            start(lambda d: refs[0].at[d], refs[0].at[last, pl.ds(self.small_at, SMALL), :])
            return
        sets, at = [], 0
        for part in self.parts[:kinds]:
            sets.append(refs[at : at + len(part)])
            at += len(part)
        for mine in range(PLANES):
            for place in range(LANES):

                def source(d, mine=mine, place=place):
                    plane, lane = divmod(d, LANES)
                    lane = lane ^ place
                    if plane == mine:
                        return sets[0][lane]
                    if plane == early_plane(mine):
                        return sets[1][lane].at[pl.ds(0, self.plan.rows), :]
                    if lane < 6:
                        return sets[2][lane].at[late_planes(mine).index(plane)]
                    return sets[3][2 * ((plane ^ mine) - 1) + (lane & 1)]

                small = sets[1][(LANES - 1) ^ place].at[pl.ds(self.plan.rows, SMALL), :]
                here = (place_ref[0] == place) & (place_ref[1] == mine)
                pl.when(here)(partial(start, source, small))


def narrow_places():
    row, column = iota((D, D), 0), iota((D, D), 1)
    return (column == 8 * (row % 64) + row // 64).astype(BF16)


def narrow_transposed(flat):
    stacked = [
        jnp.concatenate([flat[64 * i : 64 * (i + 1), 64 * j : 64 * (j + 1)] for i in (0, 1)], axis=1)
        for j in range(8)
    ]
    return dot(jnp.concatenate(stacked, axis=0), narrow_places(), TN)


def narrow_flat(turned):
    stacked = dot(narrow_places(), turned, NT)
    return jnp.concatenate(
        [
            jnp.concatenate(
                [stacked[64 * j : 64 * (j + 1), 64 * i : 64 * (i + 1)] for j in range(8)], axis=1
            )
            for i in (0, 1)
        ],
        axis=0,
    )


def router_mask():
    return iota((64, D), 1) % 8 == iota((64, D), 0) % 8


def router_places():
    return (iota((D, 64), 0) // 8 == iota((D, 64), 1)).astype(BF16)


def router_transposed(flat):
    rows = jnp.concatenate([jnp.broadcast_to(flat[r : r + 1, :], (8, D)) for r in range(8)], axis=0)
    picked = dot(jnp.where(router_mask(), rows, 0.0).astype(BF16), router_places(), NN)
    return jnp.concatenate([picked[8 * r : 8 * (r + 1), :] for r in range(8)], axis=1)


def router_flat(turned):
    stacked = jnp.concatenate([turned[:, 64 * r : 64 * (r + 1)] for r in range(8)], axis=0)
    full = jnp.where(router_mask(), dot(stacked.astype(BF16), router_places(), NT), 0.0)
    return jnp.concatenate(
        [jnp.sum(full[8 * r : 8 * (r + 1)], axis=0, keepdims=True) for r in range(8)], axis=0
    )


def norm(source):
    center = source - jnp.mean(source, axis=-1, keepdims=True)
    scaler = lax.rsqrt(jnp.mean(center * center, axis=-1, keepdims=True) + EPS)
    return center * scaler, scaler


def norm_back(grad_normal, normal, scaler):
    return scaler * (
        grad_normal
        - jnp.mean(grad_normal, axis=-1, keepdims=True)
        - normal * jnp.mean(grad_normal * normal, axis=-1, keepdims=True)
    )


def two_heads(ref, pair, q0):
    return jnp.concatenate(
        [
            ref[0, 128 * pair : 128 * pair + 64, pl.ds(q0, QB)],
            ref[0, 128 * pair + 64 : 128 * pair + 128, pl.ds(q0, QB)],
        ],
        axis=1,
    )


def two_rows(ref, pair, q0):
    return jnp.concatenate(
        [ref[0, 2 * pair + half : 2 * pair + half + 1, pl.ds(q0, QB)] for half in (0, 1)], axis=1
    )


def block_bias(code_ref, column_ref, q0, w0):
    row = code_ref[0, :, pl.ds(q0, QB)]
    bias = jnp.where(column_ref[pl.ds(w0, KB), :] == row, 0.0, NEG)
    return jnp.concatenate([bias, bias], axis=1)


def set_columns(code_ref, column_ref):
    length = code_ref.shape[2]
    column_ref[...] = jnp.broadcast_to(code_ref[0], (QB, length)).T


def block_places(block, length):
    q0 = pl.multiple_of(block * QB, QB)
    w0 = pl.multiple_of(jnp.clip(q0 - 64, 0, length - KB), 64)
    return q0, w0


def forward_prepare(plan, gathered, place_ref, refs, turned_ref, small_ref, scratch):
    rows_ref, low_ref, tmp_ref, sem = scratch

    def start(source, small):
        start_rows(plan, source, 0, ROW_O, rows_ref, tmp_ref, sem)
        pltpu.make_async_copy(small, low_ref, sem.at[2]).start()

    gathered.fetch(place_ref, refs, 2, start)
    pltpu.make_async_copy(low_ref, low_ref, sem.at[2]).wait()
    end_rows(plan, 0, ROW_O, rows_ref, tmp_ref, sem)
    small_ref[...] = low_ref[...].astype(F32)
    turned_ref[0:D, :] = rows_ref[0:D, :].astype(F32).T.astype(BF16)
    turned_ref[T_R:T_K, :] = jnp.concatenate(
        [router_transposed(small_ref[0:8, :]), jnp.zeros((8, D), F32)], axis=0
    ).astype(BF16)
    turned_ref[T_K:T_ALL, :] = narrow_transposed(rows_ref[ROW_K:ROW_O, :]).astype(BF16)


def forward_row(x_ref, code_ref, turned_ref, small_ref, outs, column_ref):
    q_ref, k_ref, v_ref, h_ref, prob_ref, lse_ref, att_ref = outs
    length = x_ref.shape[1]
    set_columns(code_ref, column_ref)
    normal, _ = norm(x_ref[0].astype(F32))
    h = (normal * small_ref[12:13, :] + small_ref[13:14, :]).astype(BF16)
    h_ref[0] = h
    turned = dot(turned_ref[0:T_K, :], h, NT)
    q_ref[0] = (turned[0:D] * (HEAD**-0.5)).astype(BF16)
    logits = turned[T_R : T_R + 8]
    shifted = jnp.exp(logits - jnp.max(logits, axis=0, keepdims=True))
    prob_ref[0] = shifted / jnp.sum(shifted, axis=0, keepdims=True)
    kv = dot(h, turned_ref[T_K:T_ALL, :], NT).astype(BF16)
    k_ref[0] = kv[:, 0:HEAD]
    v_ref[0] = kv[:, HEAD:]

    def block_step(block, carry):
        q0, w0 = block_places(block, length)
        bias = block_bias(code_ref, column_ref, q0, w0)
        keys = k_ref[0, pl.ds(w0, KB), :]
        values = v_ref[0, pl.ds(w0, KB), :]
        pairs = range(EXPERTS // 2)
        scores = [dot(keys, two_heads(q_ref, pair, q0), NN) + bias for pair in pairs]
        peak = [jnp.max(part, axis=0, keepdims=True) for part in scores]
        expd = [jnp.exp(part - top) for part, top in zip(scores, peak)]
        summed = [jnp.sum(part, axis=0, keepdims=True) for part in expd]
        atts = [dot(values, part.astype(BF16), TN) for part in expd]
        for pair in pairs:
            att = atts[pair] * (1.0 / summed[pair])
            total = peak[pair] + jnp.log(summed[pair])
            for half in range(2):
                head, part = 2 * pair + half, slice(QB * half, QB * (half + 1))
                att_ref[0, 64 * head : 64 * (head + 1), pl.ds(q0, QB)] = att[:, part]
                lse_ref[0, head : head + 1, pl.ds(q0, QB)] = total[:, part]
        return carry

    lax.fori_loop(0, length // QB, block_step, 0, unroll=2)


def forward_first(plan, gathered, count, place_ref, x_ref, code_ref, *refs):
    wins, refs = refs[:count], refs[count:]
    outs, (turned_ref, small_ref), scratch = refs[:7], refs[7:9], refs[9:]
    forward_prepare(plan, gathered, place_ref, wins, turned_ref, small_ref, scratch[1:])
    forward_row(x_ref, code_ref, turned_ref, small_ref, outs, scratch[0])


def forward_next(place_ref, x_ref, code_ref, turned_ref, small_ref, *refs):
    forward_row(x_ref, code_ref, turned_ref, small_ref, refs[7:14], refs[14])


def attention_forward(plan, gathered, place, x, code, row, before):
    rows, length = x.shape[0], x.shape[1]
    row3 = lambda a, b: pl.BlockSpec((1, a, b), lambda *_: (row, 0, 0))
    sizes = [
        (D, length, BF16),
        (length, HEAD, BF16),
        (length, HEAD, BF16),
        (length, D, BF16),
        (8, length, F32),
        (8, length, F32),
        (D, length, F32),
    ]
    out_specs = [row3(a, b) for a, b, _ in sizes]
    out_shape = [kind(c, rows, a, b) for a, b, c in sizes]
    scratch = [pltpu.VMEM((length, QB), F32)]
    in_specs = [row3(length, D), row3(1, length)]
    if before is None:
        wins = gathered.arrays(2)
        kernel = partial(forward_first, plan, gathered, len(wins))
        operands = [place, x, code, *wins]
        in_specs = in_specs + [ANYWHERE] * len(wins)
        out_specs = out_specs + [whole(T_ALL, D), whole(SMALL, D)]
        out_shape = out_shape + [kind(BF16, T_ALL, D), kind(F32, SMALL, D)]
        scratch = scratch + [
            pltpu.VMEM((ROW_O, D), BF16),
            pltpu.VMEM((SMALL, D), BF16),
            pltpu.VMEM((shared_rows(plan, 0, ROW_O), D), BF16),
            pltpu.SemaphoreType.DMA((3,)),
        ]
        aliases = {}
    else:
        kernel = forward_next
        operands = [place, x, code, *before[7:9], *before[:7]]
        in_specs = in_specs + [whole(T_ALL, D), whole(SMALL, D)] + [ANYWHERE] * 7
        aliases = {5 + i: i for i in range(7)}
    return pl.pallas_call(
        kernel,
        grid_spec=pltpu.PrefetchScalarGridSpec(
            num_scalar_prefetch=1,
            grid=(1,),
            in_specs=in_specs,
            out_specs=out_specs,
            scratch_shapes=scratch,
        ),
        out_shape=out_shape,
        input_output_aliases=aliases,
        cost_estimate=cost(14),
        compiler_params=params(),
    )(*operands)


TB = 512


def chosen_experts(experts_ref, length):
    ids = iota((EXPERTS, length), 0)
    chosen = (experts_ref[0, 0:1, :] == ids) | (experts_ref[0, 1:2, :] == ids)
    return chosen.astype(F32)


def valid_tokens(counts_ref, amount):
    place = pl.program_id(1) * amount + iota((amount, 1), 0)
    return (place < counts_ref[pl.program_id(0)]).astype(F32)


def by_head(values, gate):
    return jnp.concatenate(
        [values[64 * e : 64 * (e + 1)] * gate[e : e + 1] for e in range(EXPERTS)], axis=0
    )


def gelu_parts(source):
    scale = (2.0 / jnp.pi) ** 0.5
    square = source * source
    share = 0.5 + 0.5 * jnp.tanh(source * (scale + (scale * 0.044715) * square))
    value = source * share
    slope = share + (value - value * share) * (2.0 * scale + (6.0 * scale * 0.044715) * square)
    return value, slope


def first_step():
    return (pl.program_id(0) == 0) & (pl.program_id(1) == 0)


def last_step():
    return (pl.program_id(0) == pl.num_programs(0) - 1) & (
        pl.program_id(1) == pl.num_programs(1) - 1
    )


def feed_kernel(plan, gathered, count, pieces, place_ref, counts_ref, *refs):
    x_ref, cot_ref, att_ref, prob_ref, experts_ref, small_ref = refs[:6]
    wins = refs[6 : 6 + count]
    hid_ref, mid_ref, dmid_ref, datt_ref, dlog_ref, inner_ref = refs[6 + count : 12 + count]
    down_ref, gout_ref, gsmall_ref, gup_ref, gdown_ref = refs[12 + count : 17 + count]
    packed, bias_ref = refs[17 + count : -13], refs[-13]
    rows_ref, up_ref, flat_ref, tmp_ref, tmp2_ref, wide_ref = refs[-12:-6]
    tdown_ref, tup_ref, tout_ref, sem, sem2, pack_sem = refs[-6:]

    @pl.when(first_step())
    def _():
        def start(source, small):
            start_rows(plan, source, ROW_O, ROW_D, rows_ref, tmp_ref, sem)
            start_rows(plan, source, ROW_D, ROW_S, down_ref, tmp2_ref, sem2)

        gathered.fetch(place_ref, wins, 4, start)
        for ref in (tdown_ref, tup_ref, tout_ref, gsmall_ref):
            ref[...] = jnp.zeros_like(ref)
        end_rows(plan, ROW_O, ROW_D, rows_ref, tmp_ref, sem)
        for c in range(4):
            wide_ref[c] = rows_ref[D:, 128 * c : 128 * (c + 1)].astype(F32)
            for j in range(4):
                up_ref[:, D * j + 128 * c : D * j + 128 * (c + 1)] = wide_ref[
                    c, pl.ds(j, D, stride=4), :
                ].astype(BF16)
        end_rows(plan, ROW_D, ROW_S, down_ref, tmp2_ref, sem2)

    amount = x_ref.shape[1]
    prob = prob_ref[0]
    chosen = chosen_experts(experts_ref, amount)
    gate = prob * chosen
    att = att_ref[0]
    mixed = by_head(att, gate).astype(BF16)
    middle = x_ref[0].astype(F32) + dot(mixed, rows_ref[0:D, :], TN)
    mid_ref[0] = middle
    normal, scaler = norm(middle)
    gain = small_ref[14:15, :]
    h = (normal * gain + small_ref[15:16, :]).astype(BF16)
    grad = valid_tokens(counts_ref, amount) * cot_ref[0].astype(F32)
    grad_low = grad.astype(BF16)
    parts = [slice(2 * D * j, 2 * D * (j + 1)) for j in range(2)]
    dhid = [dot(grad_low, down_ref[part, :], NT) for part in parts]
    back = jnp.zeros((amount, D), F32)
    for j, part in enumerate(parts):
        bias = jnp.concatenate([small_ref[8 + i : 9 + i, :] for i in (2 * j, 2 * j + 1)], axis=1)
        value, slope = gelu_parts(dot(h, up_ref[:, part], NN) + bias)
        value = value.astype(BF16)
        hid_ref[0, :, part] = value
        pre = slope * dhid[j]
        sums = jnp.sum(pre, axis=0, keepdims=True)
        for i in range(2):
            gsmall_ref[2 * j + i : 2 * j + i + 1, :] += sums[:, D * i : D * (i + 1)]
        pre = pre.astype(BF16)
        tdown_ref[part, :] += dot(value, grad_low, TN)
        tup_ref[:, part] += dot(h, pre, TN)
        back = back + dot(pre, up_ref[:, part], NT)
    gsmall_ref[4:5, :] += jnp.sum(back * normal, axis=0, keepdims=True)
    gsmall_ref[5:6, :] += jnp.sum(back, axis=0, keepdims=True)
    gsmall_ref[6:7, :] += jnp.sum(grad, axis=0, keepdims=True)
    dmid = grad + norm_back(back * gain, normal, scaler)
    dmid_ref[0] = dmid
    branch = dmid.astype(BF16)
    tout_ref[...] += dot(mixed, branch, NN)
    dmixed = dot(rows_ref[0:D, :], branch, NT)
    dgate = jnp.concatenate(
        [
            jnp.sum(
                dmixed[64 * e : 64 * (e + 1)] * att[64 * e : 64 * (e + 1)], axis=0, keepdims=True
            )
            for e in range(EXPERTS)
        ],
        axis=0,
    )
    datt_ref[0] = by_head(dmixed, gate).astype(BF16)
    inner_ref[0] = gate * dgate
    dprob = dgate * chosen
    dlog = prob * (dprob - jnp.sum(prob * dprob, axis=0, keepdims=True))
    dlog_ref[0] = jnp.concatenate([dlog, jnp.zeros_like(dlog)], axis=0).astype(BF16)

    @pl.when(last_step())
    def _():
        gdown_ref[...] = tdown_ref[...].astype(BF16)
        bias_ref[...] = jnp.concatenate([gsmall_ref[6:7, :], jnp.zeros((15, D), F32)]).astype(BF16)
        ins = [flat_ref, gdown_ref, bias_ref]
        if pieces:
            pack_start(pieces, [1, 2], place_ref, ins, packed, pack_sem)
        gout_ref[...] = tout_ref[...].astype(BF16)
        for c in range(4):
            for j in range(4):
                wide_ref[c, pl.ds(j, D, stride=4), :] = tup_ref[
                    :, D * j + 128 * c : D * j + 128 * (c + 1)
                ]
            flat_ref[:, 128 * c : 128 * (c + 1)] = wide_ref[c].astype(BF16)
        gup_ref[...] = flat_ref[0 : gup_ref.shape[0], :]
        if pieces:
            pack_start(pieces, [0], place_ref, ins, packed, pack_sem)
            pack_end(packed, pack_sem)


def row_block(*tail):
    return pl.BlockSpec((1, TB, *tail), lambda i, j, *_: (i, j, 0))


def column_block(height):
    return pl.BlockSpec((1, height, TB), lambda i, j, *_: (i, 0, j))


def whole(*shape):
    return pl.BlockSpec(shape, lambda *_: (0,) * len(shape))


ANYWHERE = pl.BlockSpec(memory_space=pl.ANY)


def kind(dtype, *shape):
    return jax.ShapeDtypeStruct(shape, dtype)


def feed_forward(plan, gathered, place, counts, x, cot, att, prob, experts, small, pieces):
    rows, length = x.shape[0], x.shape[1]
    wins = gathered.arrays(4)
    head = LATE_ROWS if pieces else FF
    packed = [kind(BF16, LANES // 2, PLANES - 1, plan.rows, D)] * 2 if pieces else []
    return pl.pallas_call(
        partial(feed_kernel, plan, gathered, len(wins), pieces),
        grid_spec=pltpu.PrefetchScalarGridSpec(
            num_scalar_prefetch=2,
            grid=(rows, length // TB),
            in_specs=[
                row_block(D),
                row_block(D),
                column_block(D),
                column_block(8),
                column_block(2),
                whole(SMALL, D),
            ]
            + [ANYWHERE] * len(wins),
            out_specs=[
                row_block(FF),
                row_block(D),
                row_block(D),
                column_block(D),
                column_block(16),
                column_block(8),
                whole(FF, D),
                whole(D, D),
                whole(8, D),
                whole(head, D),
                whole(FF, D),
            ]
            + [ANYWHERE] * len(packed),
            scratch_shapes=[
                pltpu.VMEM((16, D), BF16),
                pltpu.VMEM((ROW_D - ROW_O, D), BF16),
                pltpu.VMEM((D, FF), BF16),
                pltpu.VMEM((FF, D), BF16),
                pltpu.VMEM((shared_rows(plan, ROW_O, ROW_D), D), BF16),
                pltpu.VMEM((shared_rows(plan, ROW_D, ROW_S), D), BF16),
                pltpu.VMEM((4, FF, 128), F32),
                pltpu.VMEM((FF, D), F32),
                pltpu.VMEM((D, FF), F32),
                pltpu.VMEM((D, D), F32),
                pltpu.SemaphoreType.DMA((2,)),
                pltpu.SemaphoreType.DMA((2,)),
                pltpu.SemaphoreType.DMA((2,)),
            ],
        ),
        out_shape=[
            kind(BF16, rows, length, FF),
            kind(F32, rows, length, D),
            kind(F32, rows, length, D),
            kind(BF16, rows, D, length),
            kind(BF16, rows, 16, length),
            kind(F32, rows, 8, length),
            kind(BF16, FF, D),
            kind(BF16, D, D),
            kind(F32, 8, D),
            kind(BF16, head, D),
            kind(BF16, FF, D),
        ]
        + packed,
        cost_estimate=cost(50),
        compiler_params=params(60),
    )(place, counts, x, cot, att, prob, experts, small, *wins)


def backward_kernel(pieces, place_ref, *refs):
    x_ref, h_ref, q_ref, k_ref, v_ref, lse_ref, inner_ref, datt_ref, dlog_ref, code_ref = refs[:10]
    turned_ref, gsmall_ref, gout_ref, gup_ref = refs[10:14]
    back_ref, ghead_ref, glow_ref = refs[14:17]
    packed = refs[17:-7]
    dk_ref, dv_ref, column_ref, total_ref, gain_ref, shift_ref, pack_sem = refs[-7:]
    length = x_ref.shape[1]

    @pl.when(pl.program_id(0) == 0)
    def _():
        total_ref[...] = jnp.zeros_like(total_ref)
        gain_ref[...] = jnp.zeros_like(gain_ref)
        shift_ref[...] = jnp.zeros_like(shift_ref)

    set_columns(code_ref, column_ref)
    dk_ref[...] = jnp.zeros_like(dk_ref)
    dv_ref[...] = jnp.zeros_like(dv_ref)

    def block_step(block, carry):
        q0, w0 = block_places(block, length)
        bias = block_bias(code_ref, column_ref, q0, w0)
        keys = k_ref[0, pl.ds(w0, KB), :]
        values = v_ref[0, pl.ds(w0, KB), :]
        pairs = range(EXPERTS // 2)
        queries = [two_heads(q_ref, pair, q0) for pair in pairs]
        datt = [two_heads(datt_ref, pair, q0) for pair in pairs]
        soft = [
            jnp.exp(dot(keys, part, NN) + bias - two_rows(lse_ref, pair, q0))
            for pair, part in enumerate(queries)
        ]
        dscores = [
            (soft[pair] * (dot(values, part, NN) - two_rows(inner_ref, pair, q0))).astype(BF16)
            for pair, part in enumerate(datt)
        ]
        soft = jnp.concatenate([part.astype(BF16) for part in soft], axis=1)
        dv = dot(soft, jnp.concatenate(datt, axis=1), NT)
        dk = dot(jnp.concatenate(dscores, axis=1), jnp.concatenate(queries, axis=1), NT)
        for pair in pairs:
            dq = (dot(keys, dscores[pair], TN) * (HEAD**-0.5)).astype(BF16)
            for half in range(2):
                head, part = 2 * pair + half, slice(QB * half, QB * (half + 1))
                back_ref[0, 64 * head : 64 * (head + 1), pl.ds(q0, QB)] = dq[:, part]
        dk_ref[pl.ds(w0, KB), :] += dk
        dv_ref[pl.ds(w0, KB), :] += dv
        return carry

    lax.fori_loop(0, length // QB, block_step, 0, unroll=2)
    back_ref[0, T_R:T_K, :] = dlog_ref[0]
    back_ref[0, T_K:T_V, :] = dk_ref[...].T.astype(BF16)
    back_ref[0, T_V:T_ALL, :] = dv_ref[...].T.astype(BF16)
    normal, _ = norm(x_ref[0].astype(F32))
    back = back_ref[0]
    total_ref[...] += dot(back, h_ref[0], NN)
    gain_ref[...] += dot(back, normal.astype(BF16), NN)
    shift_ref[...] += jnp.sum(back.astype(F32), axis=1, keepdims=True)

    @pl.when(pl.program_id(0) == pl.num_programs(0) - 1)
    def _():
        ghead_ref[0:D, :] = total_ref[0:D, :].T.astype(BF16)
        ghead_ref[D:ROW_O, :] = narrow_flat(total_ref[T_K:T_ALL, :].astype(BF16)).astype(BF16)
        turned = turned_ref[...].astype(F32)
        glow_ref[...] = jnp.concatenate(
            [
                router_flat(total_ref[T_R : T_R + 8, :]),
                gsmall_ref[0:4, :],
                jnp.sum(turned * gain_ref[...], axis=0, keepdims=True),
                jnp.sum(turned * shift_ref[...], axis=0, keepdims=True),
                gsmall_ref[4:7, :],
                jnp.zeros((SMALL - 17, D), F32),
            ],
            axis=0,
        ).astype(BF16)
        if pieces:
            ins = [ghead_ref, gout_ref, gup_ref, glow_ref]
            pack_start(pieces, range(4), place_ref, ins, packed, pack_sem)
            pack_end(packed, pack_sem)


def attention_backward(
    plan, place, x, h, q, k, v, lse, inner, datt, dlog, code, turned, gsmall, gout, gup, pieces
):
    rows, length = x.shape[0], x.shape[1]
    row3 = lambda a, b: pl.BlockSpec((1, a, b), lambda i, *_: (i, 0, 0))
    packed = [kind(BF16, LANES // 2, 1, plan.rows, D)] * 2 if pieces else []
    head = min(LATE_ROWS, gup.shape[0])
    return pl.pallas_call(
        partial(backward_kernel, pieces),
        grid_spec=pltpu.PrefetchScalarGridSpec(
            num_scalar_prefetch=1,
            grid=(rows,),
            in_specs=[
                row3(length, D),
                row3(length, D),
                row3(D, length),
                row3(length, HEAD),
                row3(length, HEAD),
                row3(8, length),
                row3(8, length),
                row3(D, length),
                row3(16, length),
                row3(1, length),
                whole(T_ALL, D),
                whole(8, D),
                whole(D, D),
                whole(head, D),
            ],
            out_specs=[row3(T_ALL, length), whole(ROW_O, D), whole(SMALL, D)]
            + [ANYWHERE] * len(packed),
            scratch_shapes=[
                pltpu.VMEM((length, HEAD), F32),
                pltpu.VMEM((length, HEAD), F32),
                pltpu.VMEM((length, QB), F32),
                pltpu.VMEM((T_ALL, D), F32),
                pltpu.VMEM((T_ALL, D), F32),
                pltpu.VMEM((T_ALL, 1), F32),
                pltpu.SemaphoreType.DMA((2,)),
            ],
        ),
        out_shape=[
            kind(BF16, rows, T_ALL, length),
            kind(BF16, ROW_O, D),
            kind(BF16, SMALL, D),
        ]
        + packed,
        cost_estimate=cost(33),
        compiler_params=params(),
    )(place, x, h, q, k, v, lse, inner, datt, dlog, code, turned, gsmall, gout, gup)


def input_kernel(x_ref, dmid_ref, back_ref, turned_ref, small_ref, gx_ref):
    normal, scaler = norm(x_ref[0].astype(F32))
    back = dot(back_ref[0], turned_ref[...], TN) * small_ref[12:13, :]
    gx_ref[0] = (dmid_ref[0] + norm_back(back, normal, scaler)).astype(BF16)


def input_grad(x, dmid, back, turned, small):
    rows, length = x.shape[0], x.shape[1]
    return pl.pallas_call(
        input_kernel,
        grid=(rows, length // TB),
        in_specs=[
            row_block(D),
            row_block(D),
            column_block(T_ALL),
            whole(T_ALL, D),
            whole(SMALL, D),
        ],
        out_specs=row_block(D),
        out_shape=kind(BF16, rows, length, D),
        cost_estimate=cost(8),
        compiler_params=params(),
    )(x, dmid, back, turned, small)


def output_kernel(counts_ref, mid_ref, hid_ref, small_ref, down_ref, out_ref):
    result = dot(hid_ref[0], down_ref[...], NN) + small_ref[16:17, :]
    valid = valid_tokens(counts_ref, mid_ref.shape[1])
    out_ref[0] = (valid * (mid_ref[0] + result)).astype(BF16)


def layer_output(counts, mid, hid, small, down):
    rows, length = mid.shape[0], mid.shape[1]
    return pl.pallas_call(
        output_kernel,
        grid_spec=pltpu.PrefetchScalarGridSpec(
            num_scalar_prefetch=1,
            grid=(rows, length // TB),
            in_specs=[row_block(D), row_block(FF), whole(SMALL, D), whole(FF, D)],
            out_specs=row_block(D),
        ),
        out_shape=kind(BF16, rows, length, D),
        cost_estimate=cost(9),
        compiler_params=params(),
    )(counts, mid, hid, small, down)


PLANES = 4
LANES = 8
ALL = PLANES * LANES
LATE_ROWS = 192


def move(value, pairs):
    return lax.ppermute(value, AXES, pairs)


def across(value, bits):
    return move(value, [(d, d ^ bits) for d in range(ALL)])


def by_plane(values, plane):
    out = values[-1]
    for z in range(len(values) - 1):
        out = jnp.where(plane == z, values[z], out)
    return out


def early_plane(mine):
    return 0 if mine else PLANES - 1


def late_planes(mine):
    return [z for z in range(PLANES) if z not in (mine, early_plane(mine))]


def core_spread(got):
    swapped = [across(part, 1) for part in got]
    return [part for both in zip(got, swapped) for part in both]


def gather_staged(plan, window, my_plane):
    got = [window]
    for s in range(1, PLANES):
        pairs = [(z * LANES + f, (z ^ s) * LANES + f) for z in range(PLANES) for f in range(LANES)]
        got.append(move(window, pairs))
    own = [window] + [across(window, bits) for bits in (2, 4, 6)]
    got[1:], corner = all_after(got[1:], own[3]), own[3]
    of = lambda f: by_plane([got[f(mine) ^ mine] for mine in range(PLANES)], my_plane)
    low = ROW_S - 16 * plan.first(ALL - 1)
    last = of(lambda mine: PLANES - 1)
    head = jnp.concatenate([of(early_plane), last[low : low + SMALL]], axis=0)
    rest = jnp.stack([of(lambda mine: late_planes(mine)[0]), of(lambda mine: late_planes(mine)[1])])
    head = [head] + [across(head, bits) for bits in (2, 4, 6)]
    ready = [rest]
    rest = [rest] + [across(rest, bits) for bits in (2, 4)]
    diag = []
    for s in range(1, PLANES):
        pairs = [
            ((z ^ s) * LANES + f, z * LANES + f)
            for z in range(PLANES)
            if z ^ s in late_planes(z)
            for f in range(LANES)
        ]
        diag.append(move(corner, pairs))
    ready += diag[:1]
    spread = [core_spread(part) for part in (own, head, rest, diag)]
    return Gathered(plan, None, *spread), ready


def pack_start(pieces, sources, place_ref, ins, packed, sem):
    keep_ref, send_ref = packed
    for place in range(LANES):

        def start(place=place):
            for source, at, amount, plane, lane, to in pieces:
                if source not in sources:
                    continue
                out = send_ref if (lane ^ place) & 1 else keep_ref
                pltpu.make_async_copy(
                    ins[source].at[pl.ds(at, amount), :],
                    out.at[(lane ^ place) >> 1, plane, pl.ds(to, amount), :],
                    sem.at[(lane ^ place) & 1],
                ).start()

        pl.when(place_ref[0] == place)(start)


def pack_end(packed, sem):
    for i in range(2):
        pltpu.make_async_copy(packed[i], packed[i], sem.at[i]).wait()


SMALL_AT = 176


def window_pieces(plan, windows, spans, small):
    pieces = []
    for d in windows:
        plane, lane = divmod(d, LANES)
        plane = plane - windows[0] // LANES
        begin, size = 16 * plan.first(d), plan.rows
        if small and lane == LANES - 1:
            size = SMALL_AT
            pieces.append((len(spans), 0, 16, plane, lane, SMALL_AT))
        done = begin
        for source, (low, high) in enumerate(spans + [(begin + size, begin + size)]):
            a, b = max(begin, low), min(begin + size, high)
            if a > done and a >= high or a < b and a > done:
                pieces.append((0, 0, a - done, plane, lane, done - begin))
            if a < b:
                pieces.append((source, a - low, b - a, plane, lane, a - begin))
            done = max(done, min(max(a, b), begin + size))
    for d in windows:
        plane, lane = divmod(d, LANES)
        plane = plane - windows[0] // LANES
        rows = sorted((p[5], p[5] + p[2]) for p in pieces if p[3:5] == (plane, lane))
        assert rows[0][0] == 0 and rows[-1][1] == plan.rows
        assert all(x[1] == y[0] for x, y in zip(rows, rows[1:]))
    return pieces


def core_sum(keep, send):
    got = across(send, 1)
    return [(keep[p].astype(F32) + got[p].astype(F32)).astype(BF16) for p in range(LANES // 2)]


def plane_swap(parts):
    return [parts[0]] + [across(parts[p], 2 * p) for p in range(1, LANES // 2)]


def summed(parts):
    total = parts[0].astype(F32)
    for part in parts[1:]:
        total = total + part.astype(F32)
    return total.astype(BF16)


def plane_picks(plan, head, main, my_plane, my_lane):
    low = ROW_S - 16 * plan.first(ALL - 1)
    small = head[SMALL_AT : SMALL_AT + 16]
    last = jnp.concatenate([main[-1][:low], small, main[-1][low + 16 :]], axis=0)
    last = jnp.where(my_lane == LANES - 1, last, main[-1])
    planes = [head, *(main[z] for z in range(PLANES - 2)), last]
    return [
        by_plane([planes[mine ^ s] for mine in range(PLANES)], my_plane) for s in range(PLANES)
    ]


def to_planes(picks):
    out = [picks[0]]
    for s in range(1, PLANES):
        pairs = [(z * LANES + f, (z ^ s) * LANES + f) for z in range(PLANES) for f in range(LANES)]
        out.append(move(picks[s], pairs))
    return out


def owned_kernel(plan, at_ref, *refs):
    parts, (out_ref, pad_ref) = refs[:PLANES], refs[PLANES:]
    total = parts[0][...].astype(F32)
    for part in parts[1:]:
        total = total + part[...].astype(F32)
    for j in range(4):
        pad_ref[pl.ds(j, plan.rows, stride=4), :] = total[:, 128 * j : 128 * (j + 1)]
    out_ref[...] = pad_ref[pl.ds(at_ref[0], plan.lanes), :]


def take_owned(plan, at, parts):
    out = pl.pallas_call(
        partial(owned_kernel, plan),
        grid_spec=pltpu.PrefetchScalarGridSpec(
            num_scalar_prefetch=1,
            grid=(1,),
            in_specs=[whole(plan.rows, D)] * PLANES,
            out_specs=whole(plan.lanes, 128),
            scratch_shapes=[pltpu.VMEM((plan.rows * 4, 128), F32)],
        ),
        out_shape=kind(F32, plan.lanes, 128),
        compiler_params=params(),
    )(at, *parts)
    return out.reshape(-1)


def plain_sum(plan, planes, lanes, me, at, ghead, gout, gup, gdown, glow):
    grads = jnp.concatenate([ghead, gout, gup, gdown, glow], axis=0)
    grads = jnp.pad(grads, ((0, plan.rows), (0, 0)))
    parts = jnp.stack([grads[16 * plan.first(d) :][: plan.rows] for d in range(plan.devices)])
    parts = parts.reshape(planes, lanes, plan.rows, D)
    parts = lax.psum_scatter(parts, "fsdp", scatter_dimension=1, tiled=True)
    parts = lax.psum_scatter(parts, "dp", scatter_dimension=0, tiled=True)
    flat = parts.reshape(-1).astype(F32)
    return lax.dynamic_slice(flat, (at[0] * 128,), (plan.lanes * 128,))


def local(planes, lanes, x, shard, segments, experts, counts, cot):
    plan = Plan(planes * lanes, shard.shape[0])
    my_plane, my_lane = lax.axis_index("dp"), lax.axis_index("fsdp")
    me = my_plane * lanes + my_lane
    place = jnp.stack([my_lane, my_plane]).astype(jnp.int32)
    at = ((plan.lanes * me) % 64).astype(jnp.int32).reshape(1)
    window = make_window(plan, at, shard)
    staged = (planes, lanes, plan.lanes) == (PLANES, LANES, 659)
    main_pieces, head_pieces = [], []
    first = place
    if staged:
        gathered, ready = gather_staged(plan, window, my_plane)
        first = after(place, *ready)
        main_pieces = window_pieces(
            plan, range(LANES, ALL), [(ROW_U, ROW_D), (ROW_D, ROW_S), (ROW_S + 16, ROWS_ALL)], False
        )
        head_pieces = window_pieces(
            plan, range(LANES), [(0, ROW_O), (ROW_O, ROW_U), (ROW_U, ROW_U + LATE_ROWS)], True
        )
    else:
        gathered = Gathered(plan, lax.all_gather(window, AXES, axis=0))
    rows, length = x.shape[0], x.shape[1]
    places = jnp.arange(length, dtype=jnp.int32)[None, :]
    code = jnp.where(places < counts[:, None], segments, -1 - places)
    code = code.astype(F32).reshape(-1, 1, length)
    pairs = jnp.swapaxes(experts, 1, 2)
    state = attention_forward(plan, gathered, first, x, code, 0, None)
    turned, small = state[7:9]
    for row in range(1, rows):
        before = [*state[:7], turned, small]
        state = attention_forward(plan, gathered, place, x, code, row, before)
    q, k, v, h, prob, lse, att = state[:7]
    hid, mid, dmid, datt, dlog, inner, down, gout, gsmall, gup, gdown, *packed = feed_forward(
        plan, gathered, place, counts, x, cot, att, prob, pairs, small, main_pieces
    )
    third = place
    if staged:
        parts = core_sum(*packed)
        third = after(place, *parts)
        main = plane_swap(parts)
    back, ghead, glow, *packed = attention_backward(
        plan, third, x, h, q, k, v, lse, inner, datt, dlog, code, turned, gsmall, gout, gup, head_pieces
    )
    if not staged:
        grads = plain_sum(plan, planes, lanes, me, at, ghead, gout, gup, gdown, glow)
        output = layer_output(counts, mid, hid, small, down)
        return output, input_grad(x, dmid, back, turned, small), grads
    keep, send = (part[:, 0] for part in packed)
    main = summed(all_after(main, keep))
    parts = core_sum(keep, send)
    grad_tokens = input_grad(x, dmid, after(back, *parts, main), turned, small)
    total = summed(all_after(plane_swap(parts), grad_tokens))
    picks = plane_picks(plan, total, main, my_plane, my_lane)
    output = layer_output(counts, after(mid, *picks), hid, small, down)
    return output, grad_tokens, take_owned(plan, at, all_after(to_planes(picks), output))


def solution(mesh):
    spec = P(AXES)
    return jax.shard_map(
        partial(local, mesh.shape["dp"], mesh.shape["fsdp"]),
        mesh=mesh,
        in_specs=(spec,) * 6,
        out_specs=(spec,) * 3,
        check_vma=False,
    )
```

```python
from functools import partial

import jax
import jax.numpy as jnp
from jax import lax
from jax.experimental import pallas as pl
from jax.experimental.pallas import tpu as pltpu
from jax.sharding import PartitionSpec as P

D = 512
FF = 2048
EXPERTS = 8
HEAD = 64
EPS = 1e-05
NEG = -1e30
F32 = jnp.float32
BF16 = jnp.bfloat16
AXES = ("dp", "fsdp")

ROW_K = 512
ROW_V = 576
ROW_O = 640
ROW_U = 1152
ROW_D = 3200
ROW_S = 5248
SMALL = 32
ROWS_ALL = ROW_S + SMALL
T_R = 512
T_K = 528
T_V = 592
T_ALL = 656

QB = 128
KB = 256

NN = ((1,), (0,))
NT = ((1,), (1,))
TN = ((0,), (0,))

VMEM_MIB = 56


def dot(left, right, dims):
    return lax.dot_general(left, right, (dims, ((), ())), preferred_element_type=F32)


def cost(micros):
    return pl.CostEstimate(flops=int(micros * 1.1e9), bytes_accessed=int(micros * 1e5), transcendentals=0)


def after(value, *others):
    return lax.optimization_barrier((value, *others))[0]


def all_after(values, *others):
    return lax.optimization_barrier((*values, *others))[: len(values)]


def params(mib=VMEM_MIB):
    return pltpu.CompilerParams(vmem_limit_bytes=mib << 20)


def iota(shape, dim):
    return lax.broadcasted_iota(jnp.int32, shape, dim)


class Plan:
    def __init__(self, devices, shard):
        self.devices = devices
        self.lanes = shard // 128
        reach = max((self.lanes * d) % 64 for d in range(devices)) + self.lanes
        self.rows = -(-reach // 64) * 16

    def first(self, d):
        return (self.lanes * d) // 64

    def last(self, d):
        return (self.lanes * (d + 1) - 1) // 64


def window_kernel(plan, at_ref, shard_ref, out_ref, pad_ref):
    pad_ref[...] = jnp.zeros_like(pad_ref)
    pad_ref[64 : 64 + plan.lanes, :] = shard_ref[...]
    start = 64 - at_ref[0]
    for j in range(4):
        out_ref[:, 128 * j : 128 * (j + 1)] = pad_ref[
            pl.ds(start + j, plan.rows, stride=4), :
        ].astype(BF16)


def make_window(plan, at, shard):
    return pl.pallas_call(
        partial(window_kernel, plan),
        grid_spec=pltpu.PrefetchScalarGridSpec(
            num_scalar_prefetch=1,
            grid=(1,),
            in_specs=[pl.BlockSpec((plan.lanes, 128), lambda i, at: (0, 0))],
            out_specs=pl.BlockSpec((plan.rows, D), lambda i, at: (0, 0)),
            scratch_shapes=[pltpu.VMEM((plan.rows * 4 + 128, 128), F32)],
        ),
        out_shape=jax.ShapeDtypeStruct((plan.rows, D), BF16),
        compiler_params=params(),
    )(at, shard.reshape(plan.lanes, 128))


def row_pieces(plan, low, high):
    direct, shared = [], []
    for d in range(plan.devices):
        first, last = plan.first(d), plan.last(d)
        start = first
        if d > 0 and plan.last(d - 1) == first:
            start = first + 1
            if low <= first * 16 < high:
                shared.append((d, 0, first * 16 - low))
        begin, end = max(start * 16, low), min((last + 1) * 16, high)
        if begin < end:
            direct.append((d, begin - first * 16, begin - low, end - begin))
    return direct, shared


def start_rows(plan, source, low, high, dst_ref, tmp_ref, sem):
    direct, shared = row_pieces(plan, low, high)
    for d, at, to, amount in direct:
        pltpu.make_async_copy(
            source(d).at[pl.ds(at, amount), :], dst_ref.at[pl.ds(to, amount), :], sem.at[0]
        ).start()
    for slot, (d, at, _) in enumerate(shared):
        pltpu.make_async_copy(
            source(d).at[pl.ds(at, 16), :], tmp_ref.at[pl.ds(16 * slot, 16), :], sem.at[1]
        ).start()


def end_rows(plan, low, high, dst_ref, tmp_ref, sem):
    _, shared = row_pieces(plan, low, high)
    pltpu.make_async_copy(dst_ref, dst_ref, sem.at[0]).wait()
    if shared:
        part = tmp_ref.at[pl.ds(0, 16 * len(shared)), :]
        pltpu.make_async_copy(part, part, sem.at[1]).wait()
        for slot, (_, _, to) in enumerate(shared):
            dst_ref[to : to + 16, :] = (
                dst_ref[to : to + 16, :].astype(F32)
                + tmp_ref[16 * slot : 16 * slot + 16, :].astype(F32)
            ).astype(BF16)


def shared_rows(plan, low, high):
    return max(16, 16 * len(row_pieces(plan, low, high)[1]))


class Gathered:
    def __init__(self, plan, whole=None, own=(), head=(), rest=(), diag=()):
        self.plan, self.whole = plan, whole
        self.parts = [list(own), list(head), list(rest), list(diag)]
        self.small_at = ROW_S - 16 * plan.first(plan.devices - 1)

    def arrays(self, kinds):
        if self.whole is not None:
            return [self.whole]
        return [array for i in range(kinds) for array in self.parts[i]]

    def fetch(self, place_ref, refs, kinds, start):
        if self.whole is not None:
            last = self.plan.devices - 1
            start(lambda d: refs[0].at[d], refs[0].at[last, pl.ds(self.small_at, SMALL), :])
            return
        sets, at = [], 0
        for part in self.parts[:kinds]:
            sets.append(refs[at : at + len(part)])
            at += len(part)
        for mine in range(PLANES):
            for place in range(LANES):

                def source(d, mine=mine, place=place):
                    plane, lane = divmod(d, LANES)
                    lane = lane ^ place
                    if plane == mine:
                        return sets[0][lane]
                    if plane == early_plane(mine):
                        return sets[1][lane].at[pl.ds(0, self.plan.rows), :]
                    if lane < 6:
                        return sets[2][lane].at[late_planes(mine).index(plane)]
                    return sets[3][2 * ((plane ^ mine) - 1) + (lane & 1)]

                small = sets[1][(LANES - 1) ^ place].at[pl.ds(self.plan.rows, SMALL), :]
                here = (place_ref[0] == place) & (place_ref[1] == mine)
                pl.when(here)(partial(start, source, small))


def narrow_places():
    row, column = iota((D, D), 0), iota((D, D), 1)
    return (column == 8 * (row % 64) + row // 64).astype(BF16)


def narrow_transposed(flat):
    stacked = [
        jnp.concatenate([flat[64 * i : 64 * (i + 1), 64 * j : 64 * (j + 1)] for i in (0, 1)], axis=1)
        for j in range(8)
    ]
    return dot(jnp.concatenate(stacked, axis=0), narrow_places(), TN)


def narrow_flat(turned):
    stacked = dot(narrow_places(), turned, NT)
    return jnp.concatenate(
        [
            jnp.concatenate(
                [stacked[64 * j : 64 * (j + 1), 64 * i : 64 * (i + 1)] for j in range(8)], axis=1
            )
            for i in (0, 1)
        ],
        axis=0,
    )


def router_mask():
    return iota((64, D), 1) % 8 == iota((64, D), 0) % 8


def router_places():
    return (iota((D, 64), 0) // 8 == iota((D, 64), 1)).astype(BF16)


def router_transposed(flat):
    rows = jnp.concatenate([jnp.broadcast_to(flat[r : r + 1, :], (8, D)) for r in range(8)], axis=0)
    picked = dot(jnp.where(router_mask(), rows, 0.0).astype(BF16), router_places(), NN)
    return jnp.concatenate([picked[8 * r : 8 * (r + 1), :] for r in range(8)], axis=1)


def router_flat(turned):
    stacked = jnp.concatenate([turned[:, 64 * r : 64 * (r + 1)] for r in range(8)], axis=0)
    full = jnp.where(router_mask(), dot(stacked.astype(BF16), router_places(), NT), 0.0)
    return jnp.concatenate(
        [jnp.sum(full[8 * r : 8 * (r + 1)], axis=0, keepdims=True) for r in range(8)], axis=0
    )


def norm(source):
    center = source - jnp.mean(source, axis=-1, keepdims=True)
    scaler = lax.rsqrt(jnp.mean(center * center, axis=-1, keepdims=True) + EPS)
    return center * scaler, scaler


def norm_back(grad_normal, normal, scaler):
    return scaler * (
        grad_normal
        - jnp.mean(grad_normal, axis=-1, keepdims=True)
        - normal * jnp.mean(grad_normal * normal, axis=-1, keepdims=True)
    )


def two_heads(ref, pair, q0):
    return jnp.concatenate(
        [
            ref[0, 128 * pair : 128 * pair + 64, pl.ds(q0, QB)],
            ref[0, 128 * pair + 64 : 128 * pair + 128, pl.ds(q0, QB)],
        ],
        axis=1,
    )


def two_rows(ref, pair, q0):
    return jnp.concatenate(
        [ref[0, 2 * pair + half : 2 * pair + half + 1, pl.ds(q0, QB)] for half in (0, 1)], axis=1
    )


def block_bias(code_ref, column_ref, q0, w0):
    row = code_ref[0, :, pl.ds(q0, QB)]
    bias = jnp.where(column_ref[pl.ds(w0, KB), :] == row, 0.0, NEG)
    return jnp.concatenate([bias, bias], axis=1)


def set_columns(code_ref, column_ref):
    length = code_ref.shape[2]
    column_ref[...] = jnp.broadcast_to(code_ref[0], (QB, length)).T


def block_places(block, length):
    q0 = pl.multiple_of(block * QB, QB)
    w0 = pl.multiple_of(jnp.clip(q0 - 64, 0, length - KB), 64)
    return q0, w0


def forward_prepare(plan, gathered, place_ref, refs, turned_ref, small_ref, scratch):
    rows_ref, low_ref, tmp_ref, sem = scratch

    def start(source, small):
        start_rows(plan, source, 0, ROW_O, rows_ref, tmp_ref, sem)
        pltpu.make_async_copy(small, low_ref, sem.at[2]).start()

    gathered.fetch(place_ref, refs, 2, start)
    pltpu.make_async_copy(low_ref, low_ref, sem.at[2]).wait()
    end_rows(plan, 0, ROW_O, rows_ref, tmp_ref, sem)
    small_ref[...] = low_ref[...].astype(F32)
    turned_ref[0:D, :] = rows_ref[0:D, :].astype(F32).T.astype(BF16)
    turned_ref[T_R:T_K, :] = jnp.concatenate(
        [router_transposed(small_ref[0:8, :]), jnp.zeros((8, D), F32)], axis=0
    ).astype(BF16)
    turned_ref[T_K:T_ALL, :] = narrow_transposed(rows_ref[ROW_K:ROW_O, :]).astype(BF16)


def forward_row(x_ref, code_ref, turned_ref, small_ref, outs, column_ref):
    q_ref, k_ref, v_ref, prob_ref, lse_ref, att_ref = outs
    length = x_ref.shape[1]
    set_columns(code_ref, column_ref)
    normal, _ = norm(x_ref[0].astype(F32))
    h = (normal * small_ref[12:13, :] + small_ref[13:14, :]).astype(BF16)
    turned = dot(turned_ref[0:T_K, :], h, NT)
    q_ref[0] = (turned[0:D] * (HEAD**-0.5)).astype(BF16)
    logits = turned[T_R : T_R + 8]
    shifted = jnp.exp(logits - jnp.max(logits, axis=0, keepdims=True))
    prob_ref[0] = shifted / jnp.sum(shifted, axis=0, keepdims=True)
    kv = dot(h, turned_ref[T_K:T_ALL, :], NT).astype(BF16)
    k_ref[0] = kv[:, 0:HEAD]
    v_ref[0] = kv[:, HEAD:]

    def block_step(block, carry):
        q0, w0 = block_places(block, length)
        bias = block_bias(code_ref, column_ref, q0, w0)
        keys = k_ref[0, pl.ds(w0, KB), :]
        values = v_ref[0, pl.ds(w0, KB), :]
        pairs = range(EXPERTS // 2)
        scores = [dot(keys, two_heads(q_ref, pair, q0), NN) + bias for pair in pairs]
        peak = [jnp.max(part, axis=0, keepdims=True) for part in scores]
        expd = [jnp.exp(part - top) for part, top in zip(scores, peak)]
        summed = [jnp.sum(part, axis=0, keepdims=True) for part in expd]
        atts = [dot(values, part.astype(BF16), TN) for part in expd]
        for pair in pairs:
            att = atts[pair] * (1.0 / summed[pair])
            total = peak[pair] + jnp.log(summed[pair])
            for half in range(2):
                head, part = 2 * pair + half, slice(QB * half, QB * (half + 1))
                att_ref[0, 64 * head : 64 * (head + 1), pl.ds(q0, QB)] = att[:, part]
                lse_ref[0, head : head + 1, pl.ds(q0, QB)] = total[:, part]
        return carry

    lax.fori_loop(0, length // QB, block_step, 0, unroll=2)


def forward_first(plan, gathered, count, place_ref, x_ref, code_ref, *refs):
    wins, refs = refs[:count], refs[count:]
    outs, (turned_ref, small_ref), scratch = refs[:6], refs[6:8], refs[8:]
    forward_prepare(plan, gathered, place_ref, wins, turned_ref, small_ref, scratch[1:])
    forward_row(x_ref, code_ref, turned_ref, small_ref, outs, scratch[0])


def forward_next(place_ref, x_ref, code_ref, turned_ref, small_ref, *refs):
    forward_row(x_ref, code_ref, turned_ref, small_ref, refs[6:12], refs[12])


def attention_forward(plan, gathered, place, x, code, row, before):
    rows, length = x.shape[0], x.shape[1]
    row3 = lambda a, b: pl.BlockSpec((1, a, b), lambda *_: (row, 0, 0))
    sizes = [
        (D, length, BF16),
        (length, HEAD, BF16),
        (length, HEAD, BF16),
        (8, length, F32),
        (8, length, F32),
        (D, length, F32),
    ]
    out_specs = [row3(a, b) for a, b, _ in sizes]
    out_shape = [kind(c, rows, a, b) for a, b, c in sizes]
    scratch = [pltpu.VMEM((length, QB), F32)]
    in_specs = [row3(length, D), row3(1, length)]
    if before is None:
        wins = gathered.arrays(2)
        kernel = partial(forward_first, plan, gathered, len(wins))
        operands = [place, x, code, *wins]
        in_specs = in_specs + [ANYWHERE] * len(wins)
        out_specs = out_specs + [whole(T_ALL, D), whole(SMALL, D)]
        out_shape = out_shape + [kind(BF16, T_ALL, D), kind(F32, SMALL, D)]
        scratch = scratch + [
            pltpu.VMEM((ROW_O, D), BF16),
            pltpu.VMEM((SMALL, D), BF16),
            pltpu.VMEM((shared_rows(plan, 0, ROW_O), D), BF16),
            pltpu.SemaphoreType.DMA((3,)),
        ]
        aliases = {}
    else:
        kernel = forward_next
        operands = [place, x, code, *before[6:8], *before[:6]]
        in_specs = in_specs + [whole(T_ALL, D), whole(SMALL, D)] + [ANYWHERE] * 6
        aliases = {5 + i: i for i in range(6)}
    return pl.pallas_call(
        kernel,
        grid_spec=pltpu.PrefetchScalarGridSpec(
            num_scalar_prefetch=1,
            grid=(1,),
            in_specs=in_specs,
            out_specs=out_specs,
            scratch_shapes=scratch,
        ),
        out_shape=out_shape,
        input_output_aliases=aliases,
        cost_estimate=cost(14),
        compiler_params=params(),
    )(*operands)


TB = 512


def chosen_experts(experts_ref, length):
    ids = iota((EXPERTS, length), 0)
    chosen = (experts_ref[0, 0:1, :] == ids) | (experts_ref[0, 1:2, :] == ids)
    return chosen.astype(F32)


def valid_tokens(counts_ref, amount):
    place = pl.program_id(1) * amount + iota((amount, 1), 0)
    return (place < counts_ref[pl.program_id(0)]).astype(F32)


def by_head(values, gate):
    return jnp.concatenate(
        [values[64 * e : 64 * (e + 1)] * gate[e : e + 1] for e in range(EXPERTS)], axis=0
    )


def gelu_parts(source):
    scale = (2.0 / jnp.pi) ** 0.5
    square = source * source
    share = 0.5 + 0.5 * jnp.tanh(source * (scale + (scale * 0.044715) * square))
    value = source * share
    slope = share + (value - value * share) * (2.0 * scale + (6.0 * scale * 0.044715) * square)
    return value, slope


def first_step():
    return (pl.program_id(0) == 0) & (pl.program_id(1) == 0)


def last_step():
    return (pl.program_id(0) == pl.num_programs(0) - 1) & (
        pl.program_id(1) == pl.num_programs(1) - 1
    )


def feed_kernel(plan, gathered, count, pieces, place_ref, counts_ref, *refs):
    x_ref, cot_ref, att_ref, prob_ref, experts_ref, small_ref = refs[:6]
    wins = refs[6 : 6 + count]
    hid_ref, mid_ref, dmid_ref, datt_ref, dlog_ref, inner_ref = refs[6 + count : 12 + count]
    down_out_ref, gout_ref, gsmall_ref, gup_ref = refs[12 + count : 16 + count]
    packed, gdown_ref = refs[16 + count : 18 + count], refs[18 + count]
    if not pieces:
        packed, gdown_ref = [], refs[16 + count]
    bias_ref, down_ref, down_sem = refs[-15:-12]
    rows_ref, up_ref, flat_ref, tmp_ref, tmp2_ref, wide_ref = refs[-12:-6]
    tdown_ref, tup_ref, tout_ref, sem, sem2, pack_sem = refs[-6:]

    @pl.when(first_step())
    def _():
        def start(source, small):
            start_rows(plan, source, ROW_O, ROW_D, rows_ref, tmp_ref, sem)
            start_rows(plan, source, ROW_D, ROW_S, down_ref, tmp2_ref, sem2)

        gathered.fetch(place_ref, wins, 4, start)
        for ref in (tdown_ref, tup_ref, tout_ref, gsmall_ref):
            ref[...] = jnp.zeros_like(ref)
        end_rows(plan, ROW_O, ROW_D, rows_ref, tmp_ref, sem)
        for c in range(4):
            wide_ref[c] = rows_ref[D:, 128 * c : 128 * (c + 1)].astype(F32)
            for j in range(4):
                up_ref[:, D * j + 128 * c : D * j + 128 * (c + 1)] = wide_ref[
                    c, pl.ds(j, D, stride=4), :
                ].astype(BF16)
        end_rows(plan, ROW_D, ROW_S, down_ref, tmp2_ref, sem2)
        pltpu.make_async_copy(down_ref, down_out_ref, down_sem.at[0]).start()

    amount = x_ref.shape[1]
    prob = prob_ref[0]
    chosen = chosen_experts(experts_ref, amount)
    gate = prob * chosen
    att = att_ref[0]
    mixed = by_head(att, gate).astype(BF16)
    middle = x_ref[0].astype(F32) + dot(mixed, rows_ref[0:D, :], TN)
    mid_ref[0] = middle
    normal, scaler = norm(middle)
    gain = small_ref[14:15, :]
    h = (normal * gain + small_ref[15:16, :]).astype(BF16)
    grad = valid_tokens(counts_ref, amount) * cot_ref[0].astype(F32)
    grad_low = grad.astype(BF16)
    parts = [slice(2 * D * j, 2 * D * (j + 1)) for j in range(2)]
    dhid = [dot(grad_low, down_ref[part, :], NT) for part in parts]
    back = jnp.zeros((amount, D), F32)
    for j, part in enumerate(parts):
        bias = jnp.concatenate([small_ref[8 + i : 9 + i, :] for i in (2 * j, 2 * j + 1)], axis=1)
        value, slope = gelu_parts(dot(h, up_ref[:, part], NN) + bias)
        value = value.astype(BF16)
        hid_ref[0, :, part] = value
        pre = slope * dhid[j]
        sums = jnp.sum(pre, axis=0, keepdims=True)
        for i in range(2):
            gsmall_ref[2 * j + i : 2 * j + i + 1, :] += sums[:, D * i : D * (i + 1)]
        pre = pre.astype(BF16)
        tdown_ref[part, :] += dot(value, grad_low, TN)
        tup_ref[:, part] += dot(h, pre, TN)
        back = back + dot(pre, up_ref[:, part], NT)
    gsmall_ref[4:5, :] += jnp.sum(back * normal, axis=0, keepdims=True)
    gsmall_ref[5:6, :] += jnp.sum(back, axis=0, keepdims=True)
    gsmall_ref[6:7, :] += jnp.sum(grad, axis=0, keepdims=True)
    dmid = grad + norm_back(back * gain, normal, scaler)
    dmid_ref[0] = dmid
    branch = dmid.astype(BF16)
    tout_ref[...] += dot(mixed, branch, NN)
    dmixed = dot(rows_ref[0:D, :], branch, NT)
    dgate = jnp.concatenate(
        [
            jnp.sum(
                dmixed[64 * e : 64 * (e + 1)] * att[64 * e : 64 * (e + 1)], axis=0, keepdims=True
            )
            for e in range(EXPERTS)
        ],
        axis=0,
    )
    datt_ref[0] = by_head(dmixed, gate).astype(BF16)
    inner_ref[0] = gate * dgate
    dprob = dgate * chosen
    dlog = prob * (dprob - jnp.sum(prob * dprob, axis=0, keepdims=True))
    dlog_ref[0] = jnp.concatenate([dlog, jnp.zeros_like(dlog)], axis=0).astype(BF16)

    @pl.when(last_step())
    def _():
        pltpu.make_async_copy(down_ref, down_out_ref, down_sem.at[0]).wait()
        gdown_ref[...] = tdown_ref[...].astype(BF16)
        bias_ref[...] = jnp.concatenate([gsmall_ref[6:7, :], jnp.zeros((15, D), F32)]).astype(BF16)
        ins = [flat_ref, gdown_ref, bias_ref]
        if pieces:
            pack_start(pieces, [1, 2], place_ref, ins, packed, pack_sem)
        gout_ref[...] = tout_ref[...].astype(BF16)
        for c in range(4):
            for j in range(4):
                wide_ref[c, pl.ds(j, D, stride=4), :] = tup_ref[
                    :, D * j + 128 * c : D * j + 128 * (c + 1)
                ]
            flat_ref[:, 128 * c : 128 * (c + 1)] = wide_ref[c].astype(BF16)
        gup_ref[...] = flat_ref[0 : gup_ref.shape[0], :]
        if pieces:
            pack_start(pieces, [0], place_ref, ins, packed, pack_sem)
            pack_end(packed, pack_sem)


def row_block(*tail):
    return pl.BlockSpec((1, TB, *tail), lambda i, j, *_: (i, j, 0))


def column_block(height):
    return pl.BlockSpec((1, height, TB), lambda i, j, *_: (i, 0, j))


def whole(*shape):
    return pl.BlockSpec(shape, lambda *_: (0,) * len(shape))


ANYWHERE = pl.BlockSpec(memory_space=pl.ANY)


def kind(dtype, *shape):
    return jax.ShapeDtypeStruct(shape, dtype)


def feed_forward(plan, gathered, place, counts, x, cot, att, prob, experts, small, pieces):
    rows, length = x.shape[0], x.shape[1]
    wins = gathered.arrays(4)
    head = LATE_ROWS if pieces else FF
    packed = [kind(BF16, LANES // 2, PLANES - 1, plan.rows, D)] * 2 if pieces else []
    plain = [] if pieces else [kind(BF16, FF, D)]
    held = [pltpu.VMEM((FF, D), BF16)] if pieces else []
    return pl.pallas_call(
        partial(feed_kernel, plan, gathered, len(wins), pieces),
        grid_spec=pltpu.PrefetchScalarGridSpec(
            num_scalar_prefetch=2,
            grid=(rows, length // TB),
            in_specs=[
                row_block(D),
                row_block(D),
                column_block(D),
                column_block(8),
                column_block(2),
                whole(SMALL, D),
            ]
            + [ANYWHERE] * len(wins),
            out_specs=[
                row_block(FF),
                row_block(D),
                row_block(D),
                column_block(D),
                column_block(16),
                column_block(8),
                ANYWHERE,
                whole(D, D),
                whole(8, D),
                whole(head, D),
            ]
            + [whole(FF, D)] * len(plain)
            + [ANYWHERE] * len(packed),
            scratch_shapes=held
            + [
                pltpu.VMEM((16, D), BF16),
                pltpu.VMEM((FF, D), BF16),
                pltpu.SemaphoreType.DMA((1,)),
                pltpu.VMEM((ROW_D - ROW_O, D), BF16),
                pltpu.VMEM((D, FF), BF16),
                pltpu.VMEM((FF, D), BF16),
                pltpu.VMEM((shared_rows(plan, ROW_O, ROW_D), D), BF16),
                pltpu.VMEM((shared_rows(plan, ROW_D, ROW_S), D), BF16),
                pltpu.VMEM((4, FF, 128), F32),
                pltpu.VMEM((FF, D), F32),
                pltpu.VMEM((D, FF), F32),
                pltpu.VMEM((D, D), F32),
                pltpu.SemaphoreType.DMA((2,)),
                pltpu.SemaphoreType.DMA((2,)),
                pltpu.SemaphoreType.DMA((2,)),
            ],
        ),
        out_shape=[
            kind(BF16, rows, length, FF),
            kind(F32, rows, length, D),
            kind(F32, rows, length, D),
            kind(BF16, rows, D, length),
            kind(BF16, rows, 16, length),
            kind(F32, rows, 8, length),
            kind(BF16, FF, D),
            kind(BF16, D, D),
            kind(F32, 8, D),
            kind(BF16, head, D),
        ]
        + plain
        + packed,
        cost_estimate=cost(50),
        compiler_params=params(60),
    )(place, counts, x, cot, att, prob, experts, small, *wins)


def backward_kernel(pieces, place_ref, *refs):
    x_ref, q_ref, k_ref, v_ref, lse_ref, inner_ref, datt_ref, dlog_ref, code_ref = refs[:9]
    turned_ref, small_ref, gsmall_ref, gout_ref, gup_ref = refs[9:14]
    back_ref, ghead_ref, glow_ref = refs[14:17]
    packed = refs[17:-7]
    dk_ref, dv_ref, column_ref, total_ref, gain_ref, shift_ref, pack_sem = refs[-7:]
    length = x_ref.shape[1]

    @pl.when(pl.program_id(0) == 0)
    def _():
        total_ref[...] = jnp.zeros_like(total_ref)
        gain_ref[...] = jnp.zeros_like(gain_ref)
        shift_ref[...] = jnp.zeros_like(shift_ref)

    set_columns(code_ref, column_ref)
    dk_ref[...] = jnp.zeros_like(dk_ref)
    dv_ref[...] = jnp.zeros_like(dv_ref)

    def block_step(block, carry):
        q0, w0 = block_places(block, length)
        bias = block_bias(code_ref, column_ref, q0, w0)
        keys = k_ref[0, pl.ds(w0, KB), :]
        values = v_ref[0, pl.ds(w0, KB), :]
        pairs = range(EXPERTS // 2)
        queries = [two_heads(q_ref, pair, q0) for pair in pairs]
        datt = [two_heads(datt_ref, pair, q0) for pair in pairs]
        soft = [
            jnp.exp(dot(keys, part, NN) + bias - two_rows(lse_ref, pair, q0))
            for pair, part in enumerate(queries)
        ]
        dscores = [
            (soft[pair] * (dot(values, part, NN) - two_rows(inner_ref, pair, q0))).astype(BF16)
            for pair, part in enumerate(datt)
        ]
        soft = jnp.concatenate([part.astype(BF16) for part in soft], axis=1)
        dv = dot(soft, jnp.concatenate(datt, axis=1), NT)
        dk = dot(jnp.concatenate(dscores, axis=1), jnp.concatenate(queries, axis=1), NT)
        for pair in pairs:
            dq = (dot(keys, dscores[pair], TN) * (HEAD**-0.5)).astype(BF16)
            for half in range(2):
                head, part = 2 * pair + half, slice(QB * half, QB * (half + 1))
                back_ref[0, 64 * head : 64 * (head + 1), pl.ds(q0, QB)] = dq[:, part]
        dk_ref[pl.ds(w0, KB), :] += dk
        dv_ref[pl.ds(w0, KB), :] += dv
        return carry

    lax.fori_loop(0, length // QB, block_step, 0, unroll=2)
    back_ref[0, T_R:T_K, :] = dlog_ref[0]
    back_ref[0, T_K:T_V, :] = dk_ref[...].T.astype(BF16)
    back_ref[0, T_V:T_ALL, :] = dv_ref[...].T.astype(BF16)
    normal, _ = norm(x_ref[0].astype(F32))
    back = back_ref[0]
    h = (normal * small_ref[12:13, :] + small_ref[13:14, :]).astype(BF16)
    total_ref[...] += dot(back, h, NN)
    gain_ref[...] += dot(back, normal.astype(BF16), NN)
    shift_ref[...] += jnp.sum(back.astype(F32), axis=1, keepdims=True)

    @pl.when(pl.program_id(0) == pl.num_programs(0) - 1)
    def _():
        ghead_ref[0:D, :] = total_ref[0:D, :].T.astype(BF16)
        ghead_ref[D:ROW_O, :] = narrow_flat(total_ref[T_K:T_ALL, :].astype(BF16)).astype(BF16)
        turned = turned_ref[...].astype(F32)
        glow_ref[...] = jnp.concatenate(
            [
                router_flat(total_ref[T_R : T_R + 8, :]),
                gsmall_ref[0:4, :],
                jnp.sum(turned * gain_ref[...], axis=0, keepdims=True),
                jnp.sum(turned * shift_ref[...], axis=0, keepdims=True),
                gsmall_ref[4:7, :],
                jnp.zeros((SMALL - 17, D), F32),
            ],
            axis=0,
        ).astype(BF16)
        if pieces:
            ins = [ghead_ref, gout_ref, gup_ref, glow_ref]
            pack_start(pieces, range(4), place_ref, ins, packed, pack_sem)
            pack_end(packed, pack_sem)


def attention_backward(
    plan, place, x, q, k, v, lse, inner, datt, dlog, code, turned, small, gsmall, gout, gup, pieces
):
    rows, length = x.shape[0], x.shape[1]
    row3 = lambda a, b: pl.BlockSpec((1, a, b), lambda i, *_: (i, 0, 0))
    packed = [kind(BF16, LANES // 2, 1, plan.rows, D)] * 2 if pieces else []
    head = min(LATE_ROWS, gup.shape[0])
    return pl.pallas_call(
        partial(backward_kernel, pieces),
        grid_spec=pltpu.PrefetchScalarGridSpec(
            num_scalar_prefetch=1,
            grid=(rows,),
            in_specs=[
                row3(length, D),
                row3(D, length),
                row3(length, HEAD),
                row3(length, HEAD),
                row3(8, length),
                row3(8, length),
                row3(D, length),
                row3(16, length),
                row3(1, length),
                whole(T_ALL, D),
                whole(SMALL, D),
                whole(8, D),
                whole(D, D),
                whole(head, D),
            ],
            out_specs=[row3(T_ALL, length), whole(ROW_O, D), whole(SMALL, D)]
            + [ANYWHERE] * len(packed),
            scratch_shapes=[
                pltpu.VMEM((length, HEAD), F32),
                pltpu.VMEM((length, HEAD), F32),
                pltpu.VMEM((length, QB), F32),
                pltpu.VMEM((T_ALL, D), F32),
                pltpu.VMEM((T_ALL, D), F32),
                pltpu.VMEM((T_ALL, 1), F32),
                pltpu.SemaphoreType.DMA((2,)),
            ],
        ),
        out_shape=[
            kind(BF16, rows, T_ALL, length),
            kind(BF16, ROW_O, D),
            kind(BF16, SMALL, D),
        ]
        + packed,
        cost_estimate=cost(33),
        compiler_params=params(),
    )(place, x, q, k, v, lse, inner, datt, dlog, code, turned, small, gsmall, gout, gup)


def input_kernel(x_ref, dmid_ref, back_ref, turned_ref, small_ref, gx_ref):
    normal, scaler = norm(x_ref[0].astype(F32))
    back = dot(back_ref[0], turned_ref[...], TN) * small_ref[12:13, :]
    gx_ref[0] = (dmid_ref[0] + norm_back(back, normal, scaler)).astype(BF16)


def input_grad(x, dmid, back, turned, small):
    rows, length = x.shape[0], x.shape[1]
    return pl.pallas_call(
        input_kernel,
        grid=(rows, length // TB),
        in_specs=[
            row_block(D),
            row_block(D),
            column_block(T_ALL),
            whole(T_ALL, D),
            whole(SMALL, D),
        ],
        out_specs=row_block(D),
        out_shape=kind(BF16, rows, length, D),
        cost_estimate=cost(8),
        compiler_params=params(),
    )(x, dmid, back, turned, small)


def output_kernel(counts_ref, mid_ref, hid_ref, small_ref, down_ref, out_ref):
    result = dot(hid_ref[0], down_ref[...], NN) + small_ref[16:17, :]
    valid = valid_tokens(counts_ref, mid_ref.shape[1])
    out_ref[0] = (valid * (mid_ref[0] + result)).astype(BF16)


def layer_output(counts, mid, hid, small, down):
    rows, length = mid.shape[0], mid.shape[1]
    return pl.pallas_call(
        output_kernel,
        grid_spec=pltpu.PrefetchScalarGridSpec(
            num_scalar_prefetch=1,
            grid=(rows, length // TB),
            in_specs=[row_block(D), row_block(FF), whole(SMALL, D), whole(FF, D)],
            out_specs=row_block(D),
        ),
        out_shape=kind(BF16, rows, length, D),
        cost_estimate=cost(9),
        compiler_params=params(),
    )(counts, mid, hid, small, down)


PLANES = 4
LANES = 8
ALL = PLANES * LANES
LATE_ROWS = 192


def move(value, pairs):
    return lax.ppermute(value, AXES, pairs)


def across(value, bits):
    return move(value, [(d, d ^ bits) for d in range(ALL)])


def by_plane(values, plane):
    out = values[-1]
    for z in range(len(values) - 1):
        out = jnp.where(plane == z, values[z], out)
    return out


def early_plane(mine):
    return 0 if mine else PLANES - 1


def late_planes(mine):
    return [z for z in range(PLANES) if z not in (mine, early_plane(mine))]


def core_spread(got):
    swapped = [across(part, 1) for part in got]
    return [part for both in zip(got, swapped) for part in both]


def gather_staged(plan, window, my_plane):
    got = [window]
    for s in range(1, PLANES):
        pairs = [(z * LANES + f, (z ^ s) * LANES + f) for z in range(PLANES) for f in range(LANES)]
        got.append(move(window, pairs))
    own = [window] + [across(window, bits) for bits in (2, 4, 6)]
    got[1:], corner = all_after(got[1:], own[3]), own[3]
    of = lambda f: by_plane([got[f(mine) ^ mine] for mine in range(PLANES)], my_plane)
    low = ROW_S - 16 * plan.first(ALL - 1)
    last = of(lambda mine: PLANES - 1)
    head = jnp.concatenate([of(early_plane), last[low : low + SMALL]], axis=0)
    rest = jnp.stack([of(lambda mine: late_planes(mine)[0]), of(lambda mine: late_planes(mine)[1])])
    head = [head] + [across(head, bits) for bits in (2, 4, 6)]
    ready = [rest]
    rest = [rest] + [across(rest, bits) for bits in (2, 4)]
    diag = []
    for s in range(1, PLANES):
        pairs = [
            ((z ^ s) * LANES + f, z * LANES + f)
            for z in range(PLANES)
            if z ^ s in late_planes(z)
            for f in range(LANES)
        ]
        diag.append(move(corner, pairs))
    ready += diag[:1]
    spread = [core_spread(part) for part in (own, head, rest, diag)]
    return Gathered(plan, None, *spread), ready


def pack_start(pieces, sources, place_ref, ins, packed, sem):
    keep_ref, send_ref = packed
    for place in range(LANES):

        def start(place=place):
            for source, at, amount, plane, lane, to in pieces:
                if source not in sources:
                    continue
                out = send_ref if (lane ^ place) & 1 else keep_ref
                pltpu.make_async_copy(
                    ins[source].at[pl.ds(at, amount), :],
                    out.at[(lane ^ place) >> 1, plane, pl.ds(to, amount), :],
                    sem.at[(lane ^ place) & 1],
                ).start()

        pl.when(place_ref[0] == place)(start)


def pack_end(packed, sem):
    for i in range(2):
        pltpu.make_async_copy(packed[i], packed[i], sem.at[i]).wait()


SMALL_AT = 176


def window_pieces(plan, windows, spans, small):
    pieces = []
    for d in windows:
        plane, lane = divmod(d, LANES)
        plane = plane - windows[0] // LANES
        begin, size = 16 * plan.first(d), plan.rows
        if small and lane == LANES - 1:
            size = SMALL_AT
            pieces.append((len(spans), 0, 16, plane, lane, SMALL_AT))
        done = begin
        for source, (low, high) in enumerate(spans + [(begin + size, begin + size)]):
            a, b = max(begin, low), min(begin + size, high)
            if a > done and a >= high or a < b and a > done:
                pieces.append((0, 0, a - done, plane, lane, done - begin))
            if a < b:
                pieces.append((source, a - low, b - a, plane, lane, a - begin))
            done = max(done, min(max(a, b), begin + size))
    for d in windows:
        plane, lane = divmod(d, LANES)
        plane = plane - windows[0] // LANES
        rows = sorted((p[5], p[5] + p[2]) for p in pieces if p[3:5] == (plane, lane))
        assert rows[0][0] == 0 and rows[-1][1] == plan.rows
        assert all(x[1] == y[0] for x, y in zip(rows, rows[1:]))
    return pieces


def core_sum(keep, send):
    got = across(send, 1)
    return [(keep[p].astype(F32) + got[p].astype(F32)).astype(BF16) for p in range(LANES // 2)]


def plane_swap(parts):
    return [parts[0]] + [across(parts[p], 2 * p) for p in range(1, LANES // 2)]


def summed(parts):
    total = parts[0].astype(F32)
    for part in parts[1:]:
        total = total + part.astype(F32)
    return total.astype(BF16)


def plane_picks(plan, head, main, my_plane, my_lane):
    low = ROW_S - 16 * plan.first(ALL - 1)
    small = head[SMALL_AT : SMALL_AT + 16]
    last = jnp.concatenate([main[-1][:low], small, main[-1][low + 16 :]], axis=0)
    last = jnp.where(my_lane == LANES - 1, last, main[-1])
    planes = [head, *(main[z] for z in range(PLANES - 2)), last]
    return [
        by_plane([planes[mine ^ s] for mine in range(PLANES)], my_plane) for s in range(PLANES)
    ]


def to_planes(picks):
    out = [picks[0]]
    for s in range(1, PLANES):
        pairs = [(z * LANES + f, (z ^ s) * LANES + f) for z in range(PLANES) for f in range(LANES)]
        out.append(move(picks[s], pairs))
    return out


def owned_kernel(plan, at_ref, *refs):
    parts, (out_ref, pad_ref) = refs[:PLANES], refs[PLANES:]
    total = parts[0][...].astype(F32)
    for part in parts[1:]:
        total = total + part[...].astype(F32)
    for j in range(4):
        pad_ref[pl.ds(j, plan.rows, stride=4), :] = total[:, 128 * j : 128 * (j + 1)]
    out_ref[...] = pad_ref[pl.ds(at_ref[0], plan.lanes), :]


def take_owned(plan, at, parts):
    out = pl.pallas_call(
        partial(owned_kernel, plan),
        grid_spec=pltpu.PrefetchScalarGridSpec(
            num_scalar_prefetch=1,
            grid=(1,),
            in_specs=[whole(plan.rows, D)] * PLANES,
            out_specs=whole(plan.lanes, 128),
            scratch_shapes=[pltpu.VMEM((plan.rows * 4, 128), F32)],
        ),
        out_shape=kind(F32, plan.lanes, 128),
        compiler_params=params(),
    )(at, *parts)
    return out.reshape(-1)


def plain_sum(plan, planes, lanes, me, at, ghead, gout, gup, gdown, glow):
    grads = jnp.concatenate([ghead, gout, gup, gdown, glow], axis=0)
    grads = jnp.pad(grads, ((0, plan.rows), (0, 0)))
    parts = jnp.stack([grads[16 * plan.first(d) :][: plan.rows] for d in range(plan.devices)])
    parts = parts.reshape(planes, lanes, plan.rows, D)
    parts = lax.psum_scatter(parts, "fsdp", scatter_dimension=1, tiled=True)
    parts = lax.psum_scatter(parts, "dp", scatter_dimension=0, tiled=True)
    flat = parts.reshape(-1).astype(F32)
    return lax.dynamic_slice(flat, (at[0] * 128,), (plan.lanes * 128,))


def local(planes, lanes, x, shard, segments, experts, counts, cot):
    plan = Plan(planes * lanes, shard.shape[0])
    my_plane, my_lane = lax.axis_index("dp"), lax.axis_index("fsdp")
    me = my_plane * lanes + my_lane
    place = jnp.stack([my_lane, my_plane]).astype(jnp.int32)
    at = ((plan.lanes * me) % 64).astype(jnp.int32).reshape(1)
    window = make_window(plan, at, shard)
    staged = (planes, lanes, plan.lanes) == (PLANES, LANES, 659)
    main_pieces, head_pieces = [], []
    waits = []
    if staged:
        gathered, waits = gather_staged(plan, window, my_plane)
        main_pieces = window_pieces(
            plan, range(LANES, ALL), [(ROW_U, ROW_D), (ROW_D, ROW_S), (ROW_S + 16, ROWS_ALL)], False
        )
        head_pieces = window_pieces(
            plan, range(LANES), [(0, ROW_O), (ROW_O, ROW_U), (ROW_U, ROW_U + LATE_ROWS)], True
        )
    else:
        gathered = Gathered(plan, lax.all_gather(window, AXES, axis=0))
    rows, length = x.shape[0], x.shape[1]
    places = jnp.arange(length, dtype=jnp.int32)[None, :]
    code = jnp.where(places < counts[:, None], segments, -1 - places)
    code = code.astype(F32).reshape(-1, 1, length)
    pairs = jnp.swapaxes(experts, 1, 2)
    state = attention_forward(plan, gathered, place, x, after(code, *waits), 0, None)
    turned, small = state[6:8]
    for row in range(1, rows):
        before = [*state[:6], turned, small]
        state = attention_forward(plan, gathered, place, x, code, row, before)
    q, k, v, prob, lse, att = state[:6]
    hid, mid, dmid, datt, dlog, inner, down, gout, gsmall, gup, *packed = feed_forward(
        plan, gathered, place, counts, x, cot, att, prob, pairs, small, main_pieces
    )
    third, gdown = place, packed[0]
    if staged:
        parts = core_sum(*packed)
        third = after(place, *parts)
        main = plane_swap(parts)
    back, ghead, glow, *packed = attention_backward(
        plan, third, x, q, k, v, lse, inner, datt, dlog, code, turned, small, gsmall, gout, gup, head_pieces
    )
    if not staged:
        grads = plain_sum(plan, planes, lanes, me, at, ghead, gout, gup, gdown, glow)
        output = layer_output(counts, mid, hid, small, down)
        return output, input_grad(x, dmid, back, turned, small), grads
    keep, send = (part[:, 0] for part in packed)
    main = summed(all_after(main, keep))
    parts = core_sum(keep, send)
    grad_tokens = input_grad(x, dmid, after(back, *parts, main), turned, small)
    total = summed(all_after(plane_swap(parts), grad_tokens))
    picks = plane_picks(plan, total, main, my_plane, my_lane)
    output = layer_output(counts, after(mid, *picks), hid, small, down)
    return output, grad_tokens, take_owned(plan, at, all_after(to_planes(picks), output))


def solution(mesh):
    spec = P(AXES)
    return jax.shard_map(
        partial(local, mesh.shape["dp"], mesh.shape["fsdp"]),
        mesh=mesh,
        in_specs=(spec,) * 6,
        out_specs=(spec,) * 3,
        check_vma=False,
    )
```

```python
from functools import partial

import jax
import jax.numpy as jnp
from jax import lax
from jax.experimental import pallas as pl
from jax.experimental.pallas import tpu as pltpu
from jax.sharding import PartitionSpec as P

D = 512
FF = 2048
EXPERTS = 8
HEAD = 64
EPS = 1e-05
NEG = -1e30
F32 = jnp.float32
BF16 = jnp.bfloat16
AXES = ("dp", "fsdp")

ROW_K = 512
ROW_V = 576
ROW_O = 640
ROW_U = 1152
ROW_D = 3200
ROW_S = 5248
SMALL = 32
ROWS_ALL = ROW_S + SMALL
T_R = 512
T_K = 528
T_V = 592
T_ALL = 656

QB = 128
KB = 256

NN = ((1,), (0,))
NT = ((1,), (1,))
TN = ((0,), (0,))

VMEM_MIB = 56


def dot(left, right, dims):
    return lax.dot_general(left, right, (dims, ((), ())), preferred_element_type=F32)


def cost(micros):
    return pl.CostEstimate(flops=int(micros * 1.1e9), bytes_accessed=int(micros * 1e5), transcendentals=0)


def after(value, *others):
    return lax.optimization_barrier((value, *others))[0]


def all_after(values, *others):
    return lax.optimization_barrier((*values, *others))[: len(values)]


def params(mib=VMEM_MIB):
    return pltpu.CompilerParams(vmem_limit_bytes=mib << 20)


def iota(shape, dim):
    return lax.broadcasted_iota(jnp.int32, shape, dim)


class Plan:
    def __init__(self, devices, shard):
        self.devices = devices
        self.lanes = shard // 128
        reach = max((self.lanes * d) % 64 for d in range(devices)) + self.lanes
        self.rows = -(-reach // 64) * 16

    def first(self, d):
        return (self.lanes * d) // 64

    def last(self, d):
        return (self.lanes * (d + 1) - 1) // 64


def window_kernel(plan, at_ref, shard_ref, out_ref, pad_ref):
    pad_ref[...] = jnp.zeros_like(pad_ref)
    pad_ref[64 : 64 + plan.lanes, :] = shard_ref[...]
    start = 64 - at_ref[0]
    for j in range(4):
        out_ref[:, 128 * j : 128 * (j + 1)] = pad_ref[
            pl.ds(start + j, plan.rows, stride=4), :
        ].astype(BF16)


def make_window(plan, at, shard):
    return pl.pallas_call(
        partial(window_kernel, plan),
        grid_spec=pltpu.PrefetchScalarGridSpec(
            num_scalar_prefetch=1,
            grid=(1,),
            in_specs=[pl.BlockSpec((plan.lanes, 128), lambda i, at: (0, 0))],
            out_specs=pl.BlockSpec((plan.rows, D), lambda i, at: (0, 0)),
            scratch_shapes=[pltpu.VMEM((plan.rows * 4 + 128, 128), F32)],
        ),
        out_shape=jax.ShapeDtypeStruct((plan.rows, D), BF16),
        compiler_params=params(),
    )(at, shard.reshape(plan.lanes, 128))


def row_pieces(plan, low, high):
    direct, shared = [], []
    for d in range(plan.devices):
        first, last = plan.first(d), plan.last(d)
        start = first
        if d > 0 and plan.last(d - 1) == first:
            start = first + 1
            if low <= first * 16 < high:
                shared.append((d, 0, first * 16 - low))
        begin, end = max(start * 16, low), min((last + 1) * 16, high)
        if begin < end:
            direct.append((d, begin - first * 16, begin - low, end - begin))
    return direct, shared


def start_rows(plan, source, low, high, dst_ref, tmp_ref, sem):
    direct, shared = row_pieces(plan, low, high)
    for d, at, to, amount in direct:
        pltpu.make_async_copy(
            source(d).at[pl.ds(at, amount), :], dst_ref.at[pl.ds(to, amount), :], sem.at[0]
        ).start()
    for slot, (d, at, _) in enumerate(shared):
        pltpu.make_async_copy(
            source(d).at[pl.ds(at, 16), :], tmp_ref.at[pl.ds(16 * slot, 16), :], sem.at[1]
        ).start()


def end_rows(plan, low, high, dst_ref, tmp_ref, sem):
    _, shared = row_pieces(plan, low, high)
    pltpu.make_async_copy(dst_ref, dst_ref, sem.at[0]).wait()
    if shared:
        part = tmp_ref.at[pl.ds(0, 16 * len(shared)), :]
        pltpu.make_async_copy(part, part, sem.at[1]).wait()
        for slot, (_, _, to) in enumerate(shared):
            dst_ref[to : to + 16, :] = (
                dst_ref[to : to + 16, :].astype(F32)
                + tmp_ref[16 * slot : 16 * slot + 16, :].astype(F32)
            ).astype(BF16)


def shared_rows(plan, low, high):
    return max(16, 16 * len(row_pieces(plan, low, high)[1]))


class Gathered:
    def __init__(self, plan, whole=None, own=(), head=(), rest=(), diag=()):
        self.plan, self.whole = plan, whole
        self.parts = [list(own), list(head), list(rest), list(diag)]
        self.small_at = ROW_S - 16 * plan.first(plan.devices - 1)

    def arrays(self, kinds):
        if self.whole is not None:
            return [self.whole]
        return [array for i in range(kinds) for array in self.parts[i]]

    def fetch(self, place_ref, refs, kinds, start):
        if self.whole is not None:
            last = self.plan.devices - 1
            start(lambda d: refs[0].at[d], refs[0].at[last, pl.ds(self.small_at, SMALL), :])
            return
        sets, at = [], 0
        for part in self.parts[:kinds]:
            sets.append(refs[at : at + len(part)])
            at += len(part)
        for mine in range(PLANES):
            for place in range(LANES):

                def source(d, mine=mine, place=place):
                    plane, lane = divmod(d, LANES)
                    lane = lane ^ place
                    if plane == mine:
                        return sets[0][lane]
                    if plane == early_plane(mine):
                        return sets[1][lane].at[pl.ds(0, self.plan.rows), :]
                    if lane < 6:
                        return sets[2][lane].at[late_planes(mine).index(plane)]
                    return sets[3][2 * ((plane ^ mine) - 1) + (lane & 1)]

                small = sets[1][(LANES - 1) ^ place].at[pl.ds(self.plan.rows, SMALL), :]
                here = (place_ref[0] == place) & (place_ref[1] == mine)
                pl.when(here)(partial(start, source, small))


def narrow_places():
    row, column = iota((D, D), 0), iota((D, D), 1)
    return (column == 8 * (row % 64) + row // 64).astype(BF16)


def narrow_transposed(flat):
    stacked = [
        jnp.concatenate([flat[64 * i : 64 * (i + 1), 64 * j : 64 * (j + 1)] for i in (0, 1)], axis=1)
        for j in range(8)
    ]
    return dot(jnp.concatenate(stacked, axis=0), narrow_places(), TN)


def narrow_flat(turned):
    stacked = dot(narrow_places(), turned, NT)
    return jnp.concatenate(
        [
            jnp.concatenate(
                [stacked[64 * j : 64 * (j + 1), 64 * i : 64 * (i + 1)] for j in range(8)], axis=1
            )
            for i in (0, 1)
        ],
        axis=0,
    )


def router_mask():
    return iota((64, D), 1) % 8 == iota((64, D), 0) % 8


def router_places():
    return (iota((D, 64), 0) // 8 == iota((D, 64), 1)).astype(BF16)


def router_transposed(flat):
    rows = jnp.concatenate([jnp.broadcast_to(flat[r : r + 1, :], (8, D)) for r in range(8)], axis=0)
    picked = dot(jnp.where(router_mask(), rows, 0.0).astype(BF16), router_places(), NN)
    return jnp.concatenate([picked[8 * r : 8 * (r + 1), :] for r in range(8)], axis=1)


def router_flat(turned):
    stacked = jnp.concatenate([turned[:, 64 * r : 64 * (r + 1)] for r in range(8)], axis=0)
    full = jnp.where(router_mask(), dot(stacked.astype(BF16), router_places(), NT), 0.0)
    return jnp.concatenate(
        [jnp.sum(full[8 * r : 8 * (r + 1)], axis=0, keepdims=True) for r in range(8)], axis=0
    )


def norm(source):
    center = source - jnp.mean(source, axis=-1, keepdims=True)
    scaler = lax.rsqrt(jnp.mean(center * center, axis=-1, keepdims=True) + EPS)
    return center * scaler, scaler


def norm_back(grad_normal, normal, scaler):
    return scaler * (
        grad_normal
        - jnp.mean(grad_normal, axis=-1, keepdims=True)
        - normal * jnp.mean(grad_normal * normal, axis=-1, keepdims=True)
    )


def two_heads(ref, pair, q0):
    return jnp.concatenate(
        [
            ref[0, 128 * pair : 128 * pair + 64, pl.ds(q0, QB)],
            ref[0, 128 * pair + 64 : 128 * pair + 128, pl.ds(q0, QB)],
        ],
        axis=1,
    )


def two_rows(ref, pair, q0):
    return jnp.concatenate(
        [ref[0, 2 * pair + half : 2 * pair + half + 1, pl.ds(q0, QB)] for half in (0, 1)], axis=1
    )


def block_bias(code_ref, column_ref, q0, w0):
    row = code_ref[0, :, pl.ds(q0, QB)]
    bias = jnp.where(column_ref[pl.ds(w0, KB), :] == row, 0.0, NEG)
    return jnp.concatenate([bias, bias], axis=1)


def set_columns(code_ref, column_ref):
    length = code_ref.shape[2]
    column_ref[...] = jnp.broadcast_to(code_ref[0], (QB, length)).T


def block_places(block, length):
    q0 = pl.multiple_of(block * QB, QB)
    w0 = pl.multiple_of(jnp.clip(q0 - 64, 0, length - KB), 64)
    return q0, w0


def forward_prepare(plan, gathered, place_ref, refs, turned_ref, small_ref, scratch):
    rows_ref, low_ref, tmp_ref, sem = scratch

    def start(source, small):
        start_rows(plan, source, 0, ROW_O, rows_ref, tmp_ref, sem)
        pltpu.make_async_copy(small, low_ref, sem.at[2]).start()

    gathered.fetch(place_ref, refs, 2, start)
    pltpu.make_async_copy(low_ref, low_ref, sem.at[2]).wait()
    end_rows(plan, 0, ROW_O, rows_ref, tmp_ref, sem)
    small_ref[...] = low_ref[...].astype(F32)
    turned_ref[0:D, :] = rows_ref[0:D, :].astype(F32).T.astype(BF16)
    turned_ref[T_R:T_K, :] = jnp.concatenate(
        [router_transposed(small_ref[0:8, :]), jnp.zeros((8, D), F32)], axis=0
    ).astype(BF16)
    turned_ref[T_K:T_ALL, :] = narrow_transposed(rows_ref[ROW_K:ROW_O, :]).astype(BF16)


def forward_row(x_ref, code_ref, turned_ref, small_ref, outs, column_ref):
    q_ref, k_ref, v_ref, prob_ref, lse_ref, att_ref = outs
    length = x_ref.shape[1]
    set_columns(code_ref, column_ref)
    normal, _ = norm(x_ref[0].astype(F32))
    h = (normal * small_ref[12:13, :] + small_ref[13:14, :]).astype(BF16)
    turned = dot(turned_ref[0:T_K, :], h, NT)
    q_ref[0] = (turned[0:D] * (HEAD**-0.5)).astype(BF16)
    logits = turned[T_R : T_R + 8]
    shifted = jnp.exp(logits - jnp.max(logits, axis=0, keepdims=True))
    prob_ref[0] = shifted / jnp.sum(shifted, axis=0, keepdims=True)
    kv = dot(h, turned_ref[T_K:T_ALL, :], NT).astype(BF16)
    k_ref[0] = kv[:, 0:HEAD]
    v_ref[0] = kv[:, HEAD:]

    def block_step(block, carry):
        q0, w0 = block_places(block, length)
        bias = block_bias(code_ref, column_ref, q0, w0)
        keys = k_ref[0, pl.ds(w0, KB), :]
        values = v_ref[0, pl.ds(w0, KB), :]
        pairs = range(EXPERTS // 2)
        scores = [dot(keys, two_heads(q_ref, pair, q0), NN) + bias for pair in pairs]
        peak = [jnp.max(part, axis=0, keepdims=True) for part in scores]
        expd = [jnp.exp(part - top) for part, top in zip(scores, peak)]
        summed = [jnp.sum(part, axis=0, keepdims=True) for part in expd]
        atts = [dot(values, part.astype(BF16), TN) for part in expd]
        for pair in pairs:
            att = atts[pair] * (1.0 / summed[pair])
            total = peak[pair] + jnp.log(summed[pair])
            for half in range(2):
                head, part = 2 * pair + half, slice(QB * half, QB * (half + 1))
                att_ref[0, 64 * head : 64 * (head + 1), pl.ds(q0, QB)] = att[:, part]
                lse_ref[0, head : head + 1, pl.ds(q0, QB)] = total[:, part]
        return carry

    lax.fori_loop(0, length // QB, block_step, 0, unroll=4)


def forward_first(plan, gathered, count, place_ref, x_ref, code_ref, *refs):
    wins, refs = refs[:count], refs[count:]
    outs, (turned_ref, small_ref), scratch = refs[:6], refs[6:8], refs[8:]
    forward_prepare(plan, gathered, place_ref, wins, turned_ref, small_ref, scratch[1:])
    forward_row(x_ref, code_ref, turned_ref, small_ref, outs, scratch[0])


def forward_next(place_ref, x_ref, code_ref, turned_ref, small_ref, *refs):
    forward_row(x_ref, code_ref, turned_ref, small_ref, refs[6:12], refs[12])


def attention_forward(plan, gathered, place, x, code, row, before):
    rows, length = x.shape[0], x.shape[1]
    row3 = lambda a, b: pl.BlockSpec((1, a, b), lambda *_: (row, 0, 0))
    sizes = [
        (D, length, BF16),
        (length, HEAD, BF16),
        (length, HEAD, BF16),
        (8, length, F32),
        (8, length, F32),
        (D, length, F32),
    ]
    out_specs = [row3(a, b) for a, b, _ in sizes]
    out_shape = [kind(c, rows, a, b) for a, b, c in sizes]
    scratch = [pltpu.VMEM((length, QB), F32)]
    in_specs = [row3(length, D), row3(1, length)]
    if before is None:
        wins = gathered.arrays(2)
        kernel = partial(forward_first, plan, gathered, len(wins))
        operands = [place, x, code, *wins]
        in_specs = in_specs + [ANYWHERE] * len(wins)
        out_specs = out_specs + [whole(T_ALL, D), whole(SMALL, D)]
        out_shape = out_shape + [kind(BF16, T_ALL, D), kind(F32, SMALL, D)]
        scratch = scratch + [
            pltpu.VMEM((ROW_O, D), BF16),
            pltpu.VMEM((SMALL, D), BF16),
            pltpu.VMEM((shared_rows(plan, 0, ROW_O), D), BF16),
            pltpu.SemaphoreType.DMA((3,)),
        ]
        aliases = {}
    else:
        kernel = forward_next
        operands = [place, x, code, *before[6:8], *before[:6]]
        in_specs = in_specs + [whole(T_ALL, D), whole(SMALL, D)] + [ANYWHERE] * 6
        aliases = {5 + i: i for i in range(6)}
    return pl.pallas_call(
        kernel,
        grid_spec=pltpu.PrefetchScalarGridSpec(
            num_scalar_prefetch=1,
            grid=(1,),
            in_specs=in_specs,
            out_specs=out_specs,
            scratch_shapes=scratch,
        ),
        out_shape=out_shape,
        input_output_aliases=aliases,
        cost_estimate=cost(14),
        compiler_params=params(),
    )(*operands)


TB = 512


def chosen_experts(experts_ref, length):
    ids = iota((EXPERTS, length), 0)
    chosen = (experts_ref[0, 0:1, :] == ids) | (experts_ref[0, 1:2, :] == ids)
    return chosen.astype(F32)


def valid_tokens(counts_ref, amount):
    place = pl.program_id(1) * amount + iota((amount, 1), 0)
    return (place < counts_ref[pl.program_id(0)]).astype(F32)


def by_head(values, gate):
    return jnp.concatenate(
        [values[64 * e : 64 * (e + 1)] * gate[e : e + 1] for e in range(EXPERTS)], axis=0
    )


def gelu_parts(source):
    scale = (2.0 / jnp.pi) ** 0.5
    square = source * source
    share = 0.5 + 0.5 * jnp.tanh(source * (scale + (scale * 0.044715) * square))
    value = source * share
    slope = share + (value - value * share) * (2.0 * scale + (6.0 * scale * 0.044715) * square)
    return value, slope


def first_step():
    return (pl.program_id(0) == 0) & (pl.program_id(1) == 0)


def last_step():
    return (pl.program_id(0) == pl.num_programs(0) - 1) & (
        pl.program_id(1) == pl.num_programs(1) - 1
    )


def feed_kernel(plan, gathered, count, pieces, place_ref, counts_ref, *refs):
    x_ref, cot_ref, att_ref, prob_ref, experts_ref, small_ref = refs[:6]
    wins = refs[6 : 6 + count]
    hid_ref, mid_ref, dmid_ref, datt_ref, dlog_ref, inner_ref = refs[6 + count : 12 + count]
    down_out_ref, gout_ref, gsmall_ref, gup_ref = refs[12 + count : 16 + count]
    packed, gdown_ref = refs[16 + count : 18 + count], refs[18 + count]
    if not pieces:
        packed, gdown_ref = [], refs[16 + count]
    bias_ref, down_ref, down_sem = refs[-15:-12]
    rows_ref, up_ref, flat_ref, tmp_ref, tmp2_ref, wide_ref = refs[-12:-6]
    tdown_ref, tup_ref, tout_ref, sem, sem2, pack_sem = refs[-6:]

    @pl.when(first_step())
    def _():
        def start(source, small):
            start_rows(plan, source, ROW_O, ROW_D, rows_ref, tmp_ref, sem)
            start_rows(plan, source, ROW_D, ROW_S, down_ref, tmp2_ref, sem2)

        gathered.fetch(place_ref, wins, 4, start)
        for ref in (tdown_ref, tup_ref, tout_ref, gsmall_ref):
            ref[...] = jnp.zeros_like(ref)
        end_rows(plan, ROW_O, ROW_D, rows_ref, tmp_ref, sem)
        for c in range(4):
            wide_ref[c] = rows_ref[D:, 128 * c : 128 * (c + 1)].astype(F32)
            for j in range(4):
                up_ref[:, D * j + 128 * c : D * j + 128 * (c + 1)] = wide_ref[
                    c, pl.ds(j, D, stride=4), :
                ].astype(BF16)
        end_rows(plan, ROW_D, ROW_S, down_ref, tmp2_ref, sem2)
        pltpu.make_async_copy(down_ref, down_out_ref, down_sem.at[0]).start()

    amount = x_ref.shape[1]
    prob = prob_ref[0]
    chosen = chosen_experts(experts_ref, amount)
    gate = prob * chosen
    att = att_ref[0]
    mixed = by_head(att, gate).astype(BF16)
    middle = x_ref[0].astype(F32) + dot(mixed, rows_ref[0:D, :], TN)
    mid_ref[0] = middle
    normal, scaler = norm(middle)
    gain = small_ref[14:15, :]
    h = (normal * gain + small_ref[15:16, :]).astype(BF16)
    grad = valid_tokens(counts_ref, amount) * cot_ref[0].astype(F32)
    grad_low = grad.astype(BF16)
    parts = [slice(2 * D * j, 2 * D * (j + 1)) for j in range(2)]
    dhid = [dot(grad_low, down_ref[part, :], NT) for part in parts]
    back = jnp.zeros((amount, D), F32)
    for j, part in enumerate(parts):
        bias = jnp.concatenate([small_ref[8 + i : 9 + i, :] for i in (2 * j, 2 * j + 1)], axis=1)
        value, slope = gelu_parts(dot(h, up_ref[:, part], NN) + bias)
        value = value.astype(BF16)
        hid_ref[0, :, part] = value
        pre = slope * dhid[j]
        sums = jnp.sum(pre, axis=0, keepdims=True)
        for i in range(2):
            gsmall_ref[2 * j + i : 2 * j + i + 1, :] += sums[:, D * i : D * (i + 1)]
        pre = pre.astype(BF16)
        tdown_ref[part, :] += dot(value, grad_low, TN)
        tup_ref[:, part] += dot(h, pre, TN)
        back = back + dot(pre, up_ref[:, part], NT)
    gsmall_ref[4:5, :] += jnp.sum(back * normal, axis=0, keepdims=True)
    gsmall_ref[5:6, :] += jnp.sum(back, axis=0, keepdims=True)
    gsmall_ref[6:7, :] += jnp.sum(grad, axis=0, keepdims=True)
    dmid = grad + norm_back(back * gain, normal, scaler)
    dmid_ref[0] = dmid
    branch = dmid.astype(BF16)
    tout_ref[...] += dot(mixed, branch, NN)
    dmixed = dot(rows_ref[0:D, :], branch, NT)
    dgate = jnp.concatenate(
        [
            jnp.sum(
                dmixed[64 * e : 64 * (e + 1)] * att[64 * e : 64 * (e + 1)], axis=0, keepdims=True
            )
            for e in range(EXPERTS)
        ],
        axis=0,
    )
    datt_ref[0] = by_head(dmixed, gate).astype(BF16)
    inner_ref[0] = gate * dgate
    dprob = dgate * chosen
    dlog = prob * (dprob - jnp.sum(prob * dprob, axis=0, keepdims=True))
    dlog_ref[0] = jnp.concatenate([dlog, jnp.zeros_like(dlog)], axis=0).astype(BF16)

    @pl.when(last_step())
    def _():
        pltpu.make_async_copy(down_ref, down_out_ref, down_sem.at[0]).wait()
        gdown_ref[...] = tdown_ref[...].astype(BF16)
        bias_ref[...] = jnp.concatenate([gsmall_ref[6:7, :], jnp.zeros((15, D), F32)]).astype(BF16)
        ins = [flat_ref, gdown_ref, bias_ref]
        if pieces:
            pack_start(pieces, [1, 2], place_ref, ins, packed, pack_sem)
        gout_ref[...] = tout_ref[...].astype(BF16)
        for c in range(4):
            for j in range(4):
                wide_ref[c, pl.ds(j, D, stride=4), :] = tup_ref[
                    :, D * j + 128 * c : D * j + 128 * (c + 1)
                ]
            flat_ref[:, 128 * c : 128 * (c + 1)] = wide_ref[c].astype(BF16)
        gup_ref[...] = flat_ref[0 : gup_ref.shape[0], :]
        if pieces:
            pack_start(pieces, [0], place_ref, ins, packed, pack_sem)
            pack_end(packed, pack_sem)


def row_block(*tail):
    return pl.BlockSpec((1, TB, *tail), lambda i, j, *_: (i, j, 0))


def column_block(height):
    return pl.BlockSpec((1, height, TB), lambda i, j, *_: (i, 0, j))


def whole(*shape):
    return pl.BlockSpec(shape, lambda *_: (0,) * len(shape))


ANYWHERE = pl.BlockSpec(memory_space=pl.ANY)


def kind(dtype, *shape):
    return jax.ShapeDtypeStruct(shape, dtype)


def feed_forward(plan, gathered, place, counts, x, cot, att, prob, experts, small, pieces):
    rows, length = x.shape[0], x.shape[1]
    wins = gathered.arrays(4)
    head = LATE_ROWS if pieces else FF
    packed = [kind(BF16, LANES // 2, PLANES - 1, plan.rows, D)] * 2 if pieces else []
    plain = [] if pieces else [kind(BF16, FF, D)]
    held = [pltpu.VMEM((FF, D), BF16)] if pieces else []
    return pl.pallas_call(
        partial(feed_kernel, plan, gathered, len(wins), pieces),
        grid_spec=pltpu.PrefetchScalarGridSpec(
            num_scalar_prefetch=2,
            grid=(rows, length // TB),
            in_specs=[
                row_block(D),
                row_block(D),
                column_block(D),
                column_block(8),
                column_block(2),
                whole(SMALL, D),
            ]
            + [ANYWHERE] * len(wins),
            out_specs=[
                row_block(FF),
                row_block(D),
                row_block(D),
                column_block(D),
                column_block(16),
                column_block(8),
                ANYWHERE,
                whole(D, D),
                whole(8, D),
                whole(head, D),
            ]
            + [whole(FF, D)] * len(plain)
            + [ANYWHERE] * len(packed),
            scratch_shapes=held
            + [
                pltpu.VMEM((16, D), BF16),
                pltpu.VMEM((FF, D), BF16),
                pltpu.SemaphoreType.DMA((1,)),
                pltpu.VMEM((ROW_D - ROW_O, D), BF16),
                pltpu.VMEM((D, FF), BF16),
                pltpu.VMEM((FF, D), BF16),
                pltpu.VMEM((shared_rows(plan, ROW_O, ROW_D), D), BF16),
                pltpu.VMEM((shared_rows(plan, ROW_D, ROW_S), D), BF16),
                pltpu.VMEM((4, FF, 128), F32),
                pltpu.VMEM((FF, D), F32),
                pltpu.VMEM((D, FF), F32),
                pltpu.VMEM((D, D), F32),
                pltpu.SemaphoreType.DMA((2,)),
                pltpu.SemaphoreType.DMA((2,)),
                pltpu.SemaphoreType.DMA((2,)),
            ],
        ),
        out_shape=[
            kind(BF16, rows, length, FF),
            kind(F32, rows, length, D),
            kind(F32, rows, length, D),
            kind(BF16, rows, D, length),
            kind(BF16, rows, 16, length),
            kind(F32, rows, 8, length),
            kind(BF16, FF, D),
            kind(BF16, D, D),
            kind(F32, 8, D),
            kind(BF16, head, D),
        ]
        + plain
        + packed,
        cost_estimate=cost(50),
        compiler_params=params(60),
    )(place, counts, x, cot, att, prob, experts, small, *wins)


def backward_kernel(pieces, place_ref, *refs):
    x_ref, q_ref, k_ref, v_ref, lse_ref, inner_ref, datt_ref, dlog_ref, code_ref = refs[:9]
    turned_ref, small_ref, gsmall_ref, gout_ref, gup_ref = refs[9:14]
    back_ref, ghead_ref, glow_ref = refs[14:17]
    packed = refs[17:-7]
    dk_ref, dv_ref, column_ref, total_ref, gain_ref, shift_ref, pack_sem = refs[-7:]
    length = x_ref.shape[1]

    @pl.when(pl.program_id(0) == 0)
    def _():
        total_ref[...] = jnp.zeros_like(total_ref)
        gain_ref[...] = jnp.zeros_like(gain_ref)
        shift_ref[...] = jnp.zeros_like(shift_ref)

    set_columns(code_ref, column_ref)
    dk_ref[...] = jnp.zeros_like(dk_ref)
    dv_ref[...] = jnp.zeros_like(dv_ref)

    def block_step(block, carry):
        q0, w0 = block_places(block, length)
        bias = block_bias(code_ref, column_ref, q0, w0)
        keys = k_ref[0, pl.ds(w0, KB), :]
        values = v_ref[0, pl.ds(w0, KB), :]
        pairs = range(EXPERTS // 2)
        queries = [two_heads(q_ref, pair, q0) for pair in pairs]
        datt = [two_heads(datt_ref, pair, q0) for pair in pairs]
        soft = [
            jnp.exp(dot(keys, part, NN) + bias - two_rows(lse_ref, pair, q0))
            for pair, part in enumerate(queries)
        ]
        dscores = [
            (soft[pair] * (dot(values, part, NN) - two_rows(inner_ref, pair, q0))).astype(BF16)
            for pair, part in enumerate(datt)
        ]
        soft = jnp.concatenate([part.astype(BF16) for part in soft], axis=1)
        dv = dot(soft, jnp.concatenate(datt, axis=1), NT)
        dk = dot(jnp.concatenate(dscores, axis=1), jnp.concatenate(queries, axis=1), NT)
        for pair in pairs:
            dq = (dot(keys, dscores[pair], TN) * (HEAD**-0.5)).astype(BF16)
            for half in range(2):
                head, part = 2 * pair + half, slice(QB * half, QB * (half + 1))
                back_ref[0, 64 * head : 64 * (head + 1), pl.ds(q0, QB)] = dq[:, part]
        dk_ref[pl.ds(w0, KB), :] += dk
        dv_ref[pl.ds(w0, KB), :] += dv
        return carry

    lax.fori_loop(0, length // QB, block_step, 0, unroll=4)
    back_ref[0, T_R:T_K, :] = dlog_ref[0]
    back_ref[0, T_K:T_V, :] = dk_ref[...].T.astype(BF16)
    back_ref[0, T_V:T_ALL, :] = dv_ref[...].T.astype(BF16)
    normal, _ = norm(x_ref[0].astype(F32))
    back = back_ref[0]
    h = (normal * small_ref[12:13, :] + small_ref[13:14, :]).astype(BF16)
    total_ref[...] += dot(back, h, NN)
    gain_ref[...] += dot(back, normal.astype(BF16), NN)
    shift_ref[...] += jnp.sum(back.astype(F32), axis=1, keepdims=True)

    @pl.when(pl.program_id(0) == pl.num_programs(0) - 1)
    def _():
        ghead_ref[0:D, :] = total_ref[0:D, :].T.astype(BF16)
        ghead_ref[D:ROW_O, :] = narrow_flat(total_ref[T_K:T_ALL, :].astype(BF16)).astype(BF16)
        turned = turned_ref[...].astype(F32)
        glow_ref[...] = jnp.concatenate(
            [
                router_flat(total_ref[T_R : T_R + 8, :]),
                gsmall_ref[0:4, :],
                jnp.sum(turned * gain_ref[...], axis=0, keepdims=True),
                jnp.sum(turned * shift_ref[...], axis=0, keepdims=True),
                gsmall_ref[4:7, :],
                jnp.zeros((SMALL - 17, D), F32),
            ],
            axis=0,
        ).astype(BF16)
        if pieces:
            ins = [ghead_ref, gout_ref, gup_ref, glow_ref]
            pack_start(pieces, range(4), place_ref, ins, packed, pack_sem)
            pack_end(packed, pack_sem)


def attention_backward(
    plan, place, x, q, k, v, lse, inner, datt, dlog, code, turned, small, gsmall, gout, gup, pieces
):
    rows, length = x.shape[0], x.shape[1]
    row3 = lambda a, b: pl.BlockSpec((1, a, b), lambda i, *_: (i, 0, 0))
    packed = [kind(BF16, LANES // 2, 1, plan.rows, D)] * 2 if pieces else []
    head = min(LATE_ROWS, gup.shape[0])
    return pl.pallas_call(
        partial(backward_kernel, pieces),
        grid_spec=pltpu.PrefetchScalarGridSpec(
            num_scalar_prefetch=1,
            grid=(rows,),
            in_specs=[
                row3(length, D),
                row3(D, length),
                row3(length, HEAD),
                row3(length, HEAD),
                row3(8, length),
                row3(8, length),
                row3(D, length),
                row3(16, length),
                row3(1, length),
                whole(T_ALL, D),
                whole(SMALL, D),
                whole(8, D),
                whole(D, D),
                whole(head, D),
            ],
            out_specs=[row3(T_ALL, length), whole(ROW_O, D), whole(SMALL, D)]
            + [ANYWHERE] * len(packed),
            scratch_shapes=[
                pltpu.VMEM((length, HEAD), F32),
                pltpu.VMEM((length, HEAD), F32),
                pltpu.VMEM((length, QB), F32),
                pltpu.VMEM((T_ALL, D), F32),
                pltpu.VMEM((T_ALL, D), F32),
                pltpu.VMEM((T_ALL, 1), F32),
                pltpu.SemaphoreType.DMA((2,)),
            ],
        ),
        out_shape=[
            kind(BF16, rows, T_ALL, length),
            kind(BF16, ROW_O, D),
            kind(BF16, SMALL, D),
        ]
        + packed,
        cost_estimate=cost(33),
        compiler_params=params(),
    )(place, x, q, k, v, lse, inner, datt, dlog, code, turned, small, gsmall, gout, gup)


def input_kernel(x_ref, dmid_ref, back_ref, turned_ref, small_ref, gx_ref):
    normal, scaler = norm(x_ref[0].astype(F32))
    back = dot(back_ref[0], turned_ref[...], TN) * small_ref[12:13, :]
    gx_ref[0] = (dmid_ref[0] + norm_back(back, normal, scaler)).astype(BF16)


def input_grad(x, dmid, back, turned, small):
    rows, length = x.shape[0], x.shape[1]
    return pl.pallas_call(
        input_kernel,
        grid=(rows, length // TB),
        in_specs=[
            row_block(D),
            row_block(D),
            column_block(T_ALL),
            whole(T_ALL, D),
            whole(SMALL, D),
        ],
        out_specs=row_block(D),
        out_shape=kind(BF16, rows, length, D),
        cost_estimate=cost(8),
        compiler_params=params(),
    )(x, dmid, back, turned, small)


def output_kernel(counts_ref, mid_ref, hid_ref, small_ref, down_ref, out_ref):
    result = dot(hid_ref[0], down_ref[...], NN) + small_ref[16:17, :]
    valid = valid_tokens(counts_ref, mid_ref.shape[1])
    out_ref[0] = (valid * (mid_ref[0] + result)).astype(BF16)


def layer_output(counts, mid, hid, small, down):
    rows, length = mid.shape[0], mid.shape[1]
    return pl.pallas_call(
        output_kernel,
        grid_spec=pltpu.PrefetchScalarGridSpec(
            num_scalar_prefetch=1,
            grid=(rows, length // TB),
            in_specs=[row_block(D), row_block(FF), whole(SMALL, D), whole(FF, D)],
            out_specs=row_block(D),
        ),
        out_shape=kind(BF16, rows, length, D),
        cost_estimate=cost(9),
        compiler_params=params(),
    )(counts, mid, hid, small, down)


PLANES = 4
LANES = 8
ALL = PLANES * LANES
LATE_ROWS = 192


def move(value, pairs):
    return lax.ppermute(value, AXES, pairs)


def across(value, bits):
    return move(value, [(d, d ^ bits) for d in range(ALL)])


def by_plane(values, plane):
    out = values[-1]
    for z in range(len(values) - 1):
        out = jnp.where(plane == z, values[z], out)
    return out


def early_plane(mine):
    return 0 if mine else PLANES - 1


def late_planes(mine):
    return [z for z in range(PLANES) if z not in (mine, early_plane(mine))]


def core_spread(got):
    swapped = [across(part, 1) for part in got]
    return [part for both in zip(got, swapped) for part in both]


def gather_staged(plan, window, my_plane):
    got = [window]
    for s in range(1, PLANES):
        pairs = [(z * LANES + f, (z ^ s) * LANES + f) for z in range(PLANES) for f in range(LANES)]
        got.append(move(window, pairs))
    own = [window] + [across(window, bits) for bits in (2, 4, 6)]
    got[1:], corner = all_after(got[1:], own[3]), own[3]
    of = lambda f: by_plane([got[f(mine) ^ mine] for mine in range(PLANES)], my_plane)
    low = ROW_S - 16 * plan.first(ALL - 1)
    last = of(lambda mine: PLANES - 1)
    head = jnp.concatenate([of(early_plane), last[low : low + SMALL]], axis=0)
    rest = jnp.stack([of(lambda mine: late_planes(mine)[0]), of(lambda mine: late_planes(mine)[1])])
    head = [head] + [across(head, bits) for bits in (2, 4, 6)]
    ready = [rest]
    rest = [rest] + [across(rest, bits) for bits in (2, 4)]
    diag = []
    for s in range(1, PLANES):
        pairs = [
            ((z ^ s) * LANES + f, z * LANES + f)
            for z in range(PLANES)
            if z ^ s in late_planes(z)
            for f in range(LANES)
        ]
        diag.append(move(corner, pairs))
    ready += diag[:1]
    spread = [core_spread(part) for part in (own, head, rest, diag)]
    return Gathered(plan, None, *spread), ready


def pack_start(pieces, sources, place_ref, ins, packed, sem):
    keep_ref, send_ref = packed
    for place in range(LANES):

        def start(place=place):
            for source, at, amount, plane, lane, to in pieces:
                if source not in sources:
                    continue
                out = send_ref if (lane ^ place) & 1 else keep_ref
                pltpu.make_async_copy(
                    ins[source].at[pl.ds(at, amount), :],
                    out.at[(lane ^ place) >> 1, plane, pl.ds(to, amount), :],
                    sem.at[(lane ^ place) & 1],
                ).start()

        pl.when(place_ref[0] == place)(start)


def pack_end(packed, sem):
    for i in range(2):
        pltpu.make_async_copy(packed[i], packed[i], sem.at[i]).wait()


SMALL_AT = 176


def window_pieces(plan, windows, spans, small):
    pieces = []
    for d in windows:
        plane, lane = divmod(d, LANES)
        plane = plane - windows[0] // LANES
        begin, size = 16 * plan.first(d), plan.rows
        if small and lane == LANES - 1:
            size = SMALL_AT
            pieces.append((len(spans), 0, 16, plane, lane, SMALL_AT))
        done = begin
        for source, (low, high) in enumerate(spans + [(begin + size, begin + size)]):
            a, b = max(begin, low), min(begin + size, high)
            if a > done and a >= high or a < b and a > done:
                pieces.append((0, 0, a - done, plane, lane, done - begin))
            if a < b:
                pieces.append((source, a - low, b - a, plane, lane, a - begin))
            done = max(done, min(max(a, b), begin + size))
    for d in windows:
        plane, lane = divmod(d, LANES)
        plane = plane - windows[0] // LANES
        rows = sorted((p[5], p[5] + p[2]) for p in pieces if p[3:5] == (plane, lane))
        assert rows[0][0] == 0 and rows[-1][1] == plan.rows
        assert all(x[1] == y[0] for x, y in zip(rows, rows[1:]))
    return pieces


def core_sum(keep, send):
    got = across(send, 1)
    return [(keep[p].astype(F32) + got[p].astype(F32)).astype(BF16) for p in range(LANES // 2)]


def plane_swap(parts):
    return [parts[0]] + [across(parts[p], 2 * p) for p in range(1, LANES // 2)]


def summed(parts):
    total = parts[0].astype(F32)
    for part in parts[1:]:
        total = total + part.astype(F32)
    return total.astype(BF16)


def plane_picks(plan, head, main, my_plane, my_lane):
    low = ROW_S - 16 * plan.first(ALL - 1)
    small = head[SMALL_AT : SMALL_AT + 16]
    last = jnp.concatenate([main[-1][:low], small, main[-1][low + 16 :]], axis=0)
    last = jnp.where(my_lane == LANES - 1, last, main[-1])
    planes = [head, *(main[z] for z in range(PLANES - 2)), last]
    return [
        by_plane([planes[mine ^ s] for mine in range(PLANES)], my_plane) for s in range(PLANES)
    ]


def to_planes(picks):
    out = [picks[0]]
    for s in range(1, PLANES):
        pairs = [(z * LANES + f, (z ^ s) * LANES + f) for z in range(PLANES) for f in range(LANES)]
        out.append(move(picks[s], pairs))
    return out


def owned_kernel(plan, at_ref, *refs):
    parts, (out_ref, pad_ref) = refs[:PLANES], refs[PLANES:]
    total = parts[0][...].astype(F32)
    for part in parts[1:]:
        total = total + part[...].astype(F32)
    for j in range(4):
        pad_ref[pl.ds(j, plan.rows, stride=4), :] = total[:, 128 * j : 128 * (j + 1)]
    out_ref[...] = pad_ref[pl.ds(at_ref[0], plan.lanes), :]


def take_owned(plan, at, parts):
    out = pl.pallas_call(
        partial(owned_kernel, plan),
        grid_spec=pltpu.PrefetchScalarGridSpec(
            num_scalar_prefetch=1,
            grid=(1,),
            in_specs=[whole(plan.rows, D)] * PLANES,
            out_specs=whole(plan.lanes, 128),
            scratch_shapes=[pltpu.VMEM((plan.rows * 4, 128), F32)],
        ),
        out_shape=kind(F32, plan.lanes, 128),
        compiler_params=params(),
    )(at, *parts)
    return out.reshape(-1)


def plain_sum(plan, planes, lanes, me, at, ghead, gout, gup, gdown, glow):
    grads = jnp.concatenate([ghead, gout, gup, gdown, glow], axis=0)
    grads = jnp.pad(grads, ((0, plan.rows), (0, 0)))
    parts = jnp.stack([grads[16 * plan.first(d) :][: plan.rows] for d in range(plan.devices)])
    parts = parts.reshape(planes, lanes, plan.rows, D)
    parts = lax.psum_scatter(parts, "fsdp", scatter_dimension=1, tiled=True)
    parts = lax.psum_scatter(parts, "dp", scatter_dimension=0, tiled=True)
    flat = parts.reshape(-1).astype(F32)
    return lax.dynamic_slice(flat, (at[0] * 128,), (plan.lanes * 128,))


def local(planes, lanes, x, shard, segments, experts, counts, cot):
    plan = Plan(planes * lanes, shard.shape[0])
    my_plane, my_lane = lax.axis_index("dp"), lax.axis_index("fsdp")
    me = my_plane * lanes + my_lane
    place = jnp.stack([my_lane, my_plane]).astype(jnp.int32)
    at = ((plan.lanes * me) % 64).astype(jnp.int32).reshape(1)
    window = make_window(plan, at, shard)
    staged = (planes, lanes, plan.lanes) == (PLANES, LANES, 659)
    main_pieces, head_pieces = [], []
    waits = []
    if staged:
        gathered, waits = gather_staged(plan, window, my_plane)
        main_pieces = window_pieces(
            plan, range(LANES, ALL), [(ROW_U, ROW_D), (ROW_D, ROW_S), (ROW_S + 16, ROWS_ALL)], False
        )
        head_pieces = window_pieces(
            plan, range(LANES), [(0, ROW_O), (ROW_O, ROW_U), (ROW_U, ROW_U + LATE_ROWS)], True
        )
    else:
        gathered = Gathered(plan, lax.all_gather(window, AXES, axis=0))
    rows, length = x.shape[0], x.shape[1]
    places = jnp.arange(length, dtype=jnp.int32)[None, :]
    code = jnp.where(places < counts[:, None], segments, -1 - places)
    code = code.astype(F32).reshape(-1, 1, length)
    pairs = jnp.swapaxes(experts, 1, 2)
    state = attention_forward(plan, gathered, place, x, after(code, *waits), 0, None)
    turned, small = state[6:8]
    for row in range(1, rows):
        before = [*state[:6], turned, small]
        state = attention_forward(plan, gathered, place, x, code, row, before)
    q, k, v, prob, lse, att = state[:6]
    hid, mid, dmid, datt, dlog, inner, down, gout, gsmall, gup, *packed = feed_forward(
        plan, gathered, place, counts, x, cot, att, prob, pairs, small, main_pieces
    )
    third, gdown = place, packed[0]
    if staged:
        parts = core_sum(*packed)
        third = after(place, *parts)
        main = plane_swap(parts)
    back, ghead, glow, *packed = attention_backward(
        plan, third, x, q, k, v, lse, inner, datt, dlog, code, turned, small, gsmall, gout, gup, head_pieces
    )
    if not staged:
        grads = plain_sum(plan, planes, lanes, me, at, ghead, gout, gup, gdown, glow)
        output = layer_output(counts, mid, hid, small, down)
        return output, input_grad(x, dmid, back, turned, small), grads
    keep, send = (part[:, 0] for part in packed)
    main = summed(all_after(main, keep))
    parts = core_sum(keep, send)
    grad_tokens = input_grad(x, dmid, after(back, *parts, main), turned, small)
    total = summed(all_after(plane_swap(parts), grad_tokens))
    picks = plane_picks(plan, total, main, my_plane, my_lane)
    output = layer_output(counts, after(mid, *picks), hid, small, down)
    return output, grad_tokens, take_owned(plan, at, all_after(to_planes(picks), output))


def solution(mesh):
    spec = P(AXES)
    return jax.shard_map(
        partial(local, mesh.shape["dp"], mesh.shape["fsdp"]),
        mesh=mesh,
        in_specs=(spec,) * 6,
        out_specs=(spec,) * 3,
        check_vma=False,
    )
```
